512 devices in a mesh: tm: 32 (over z_lo, x, core), chan: 16 (over z_hi, y).
Axes of the slice: x: 4, y: 8, z: 8 (z_hi: 2, z_lo: 4; z = z_hi * 4 + z_lo), core: 2. Of those that a mesh axis runs over, the one named last changes fastest.
Arguments:
- arrived: bfloat16 [2048, 512, 128], P('tm', 'chan')
- row_target: int32 [2048], P('tm'), may hold values from 0 to 2047, as said below
- clip_lengths: int32 [4], replicated, may hold values from 1 to 32, 64 in all
- conv_weight: bfloat16 [3, 3, 3, 512, 512], P(None, None, None, 'chan'), may hold values from -0.0546875 to 0.0546875
- gn_gain: float32 [512], replicated, may hold values from 0.1 to 1.9
- gn_bias: float32 [512], replicated, may hold values from -3 to 3
Outputs:
- features: bfloat16 [16, 64, 64, 512], P('chan', 'tm')
The draws below stay inside these ranges and needn't reach their ends.
Inputs may be any that keep to these rules, and one draw needn't show every extreme that they name: `row_target`: a permutation of the 2048 packed frame rows; the 64 rows arrived on one device of tm go to 17 owners of time slabs of 64 consecutive packed rows, at most 4 to one owner, and exactly 4 to some.
All inputs are finite; a program needn't handle non-finite values.
Results may differ from the reference program's by a relative error of at most 0.001.
Values may be sent and summed in bfloat16 or wider, within the bound.
No kernel may reach another device: no remote copies, remote signals or barrier semaphores. Data moves between devices by JAX's collectives and lax.ppermute only.
A program may use at most 64 MiB of HBM per device.

```python
import math
import jax
import jax.numpy as jnp
import numpy as np
from jax import lax

CIN = 512
COUT = 512
GROUPS = 32
WIN_H = 32
WIN_W = 128
FR_DEV = 2
CLIPS = 4
FRAMES = 64
N_TM = 32
N_CHAN = 16


def draw_arrived(key, part):
    row_total = FRAMES * WIN_H
    value_key = jax.random.fold_in(key, 11)
    scale_key = jax.random.fold_in(key, 12)
    values = jnp.clip(jax.random.normal(value_key, (row_total, CIN, WIN_W), jnp.float32), -6.0, 6.0)
    scales = jnp.exp(jax.random.uniform(scale_key, (row_total, 1, 1), jnp.float32, 0.0, math.log(8.0)))
    return (values * scales).astype(jnp.bfloat16)


def shuffled_rows(one_key):
    return jax.random.permutation(one_key, FR_DEV * WIN_H).astype(jnp.int32)


def draw_row_target(key, part):
    rows_dev = FR_DEV * WIN_H
    slabs = N_TM
    capacity = 2 * rows_dev // slabs
    halves = slabs // 2
    offsets = jax.random.permutation(jax.random.fold_in(key, 1), slabs)[:halves + 1].astype(jnp.int32)
    ordinal = jnp.arange(rows_dev, dtype=jnp.int32)
    full_part = (halves - 1) * capacity
    blocks = jnp.where(ordinal < full_part, ordinal // capacity, halves - 1 + (ordinal - full_part) // (capacity // 2))
    sources = jnp.arange(slabs, dtype=jnp.int32)
    owners = (sources[:, None] + offsets[blocks][None, :]) % slabs
    owner_order = jax.vmap(shuffled_rows)(jax.random.split(jax.random.fold_in(key, 2), slabs))
    source_order = jax.vmap(shuffled_rows)(jax.random.split(jax.random.fold_in(key, 3), slabs))
    target_value = owners * rows_dev + owner_order[owners, jnp.broadcast_to(ordinal[None, :], owners.shape)]
    result = jnp.zeros((slabs, rows_dev), jnp.int32)
    result = result.at[jnp.broadcast_to(sources[:, None], owners.shape), source_order].set(target_value.astype(jnp.int32))
    return result.reshape(-1)


def level_of(rng, extent, shards, low, largest):
    level, own = 1.0, jax.random.fold_in(rng, 6)
    for position, shards_of in shards:
        steps = jnp.exp(jax.random.uniform(jax.random.fold_in(own, position), (shards_of,), jnp.float32, low / len(shards), largest / len(shards)))
        level = level * jnp.repeat(steps, extent[position] // shards_of).reshape([-1 if axis == position else 1 for axis in range(len(extent))])
    return level


def split_up(amount, total, reach, skew):
    portions = [(1 << 20) // math.isqrt(rank ** skew) + 1 for rank in range(2, amount + 1)]
    rest, given = total - reach - (amount - 1), [1] * (amount - 1)
    while rest > 0:
        candidates = [i for i in range(amount - 1) if given[i] < reach]
        mass, budget = sum([portions[i] for i in candidates]), rest
        for i in candidates:
            more = min(reach - given[i], max(1, budget * portions[i] // mass), rest)
            given[i] = given[i] + more
            rest = rest - more
    return np.array([reach] + given)


def uneven(key, number_of, total, limit, skew):
    if number_of == 2:
        one = jax.random.randint(key, (), max(1, total - limit), min(limit, total - 1) + 1)
        return jnp.stack([one, total - one])
    sizes = jnp.asarray(split_up(number_of, total, limit, skew), jnp.int32)
    twos = (number_of - 1) // 2
    donor, taker = sizes[1:1 + 2 * twos:2], sizes[2:2 + 2 * twos:2]
    margin = jnp.minimum(donor - 1, limit - taker)
    passed = jax.random.randint(jax.random.fold_in(key, 1), (twos,), 0, 1 << 20) % (margin + 1)
    sizes = sizes.at[1:1 + 2 * twos:2].set(donor - passed).at[2:2 + 2 * twos:2].set(taker + passed)
    return sizes[jax.random.permutation(jax.random.fold_in(key, 2), number_of)]


def scatter_about(own_key, shape, deviation, reach, cuts=(), kind=jnp.bfloat16):
    factor_of = level_of(own_key, shape, cuts, -0.22, 0.18) if cuts else 1.0
    values = jax.random.normal(own_key, shape, jnp.float32) * deviation * factor_of
    return jnp.minimum(jnp.maximum(values, -reach), reach).astype(kind)


def setup_inputs(seed: int = 0) -> dict:
    seeds = jax.random.split(jax.random.key(seed), 7)
    arrived = draw_arrived(jax.random.fold_in(seeds[6], 71), 0)
    row_target = draw_row_target(jax.random.fold_in(seeds[6], 71), 0)
    clip_lengths = uneven(seeds[2], CLIPS, FRAMES, FRAMES // 2, 2).astype(jnp.int32)
    conv_weight = scatter_about(seeds[3], (3, 3, 3, CIN, COUT), (27 * CIN) ** -0.5, 0.0546875, ((3, 16),))
    gn_gain = jnp.clip(1.0 + 0.18 * jax.random.normal(seeds[4], (COUT,), jnp.float32), 0.1, 1.9)
    gn_bias = scatter_about(seeds[5], (COUT,), 0.5, 3.0, (), jnp.float32)
    return {"arrived": arrived, "row_target": row_target, "clip_lengths": clip_lengths, "conv_weight": conv_weight, "gn_gain": gn_gain, "gn_bias": gn_bias}


EPSILON = 1e-05

def spatial_taps(frames):
    frame_total, row_total, chan_total, col_total = frames.shape
    paired_rows = frames.reshape(frame_total, row_total // 2, 2, chan_total, col_total)
    even_rows = paired_rows[:, :, 0]
    odd_rows = paired_rows[:, :, 1]
    upper_rows = jnp.concatenate([jnp.zeros_like(odd_rows[:, :1]), odd_rows[:, :-1]], axis=1)
    tapped = []
    for picked in (upper_rows, even_rows, odd_rows):
        paired_cols = picked.reshape(frame_total, row_total // 2, chan_total, col_total // 2, 2)
        even_cols = paired_cols[..., 0]
        odd_cols = paired_cols[..., 1]
        left_cols = jnp.concatenate([jnp.zeros_like(odd_cols[..., :1]), odd_cols[..., :-1]], axis=3)
        tapped.extend([left_cols, even_cols, odd_cols])
    return tapped

def clip_masks(first_frame, frame_total, clip_lengths, value_type):
    clip_ends = jnp.cumsum(clip_lengths).astype(jnp.int32)
    starts = (clip_ends - clip_lengths).astype(jnp.int32)
    frame_ids = first_frame + jnp.arange(frame_total, dtype=jnp.int32)
    member = (frame_ids[:, None] >= starts[None, :]) & (frame_ids[:, None] < clip_ends[None, :])
    clip_first = lax.optimization_barrier(jnp.sum(jnp.where(member, starts[None, :], 0), axis=1)).astype(jnp.int32)
    allowed = jnp.stack([frame_ids - (2 - offset) >= clip_first for offset in range(3)])
    return (member.astype(jnp.float32), allowed.astype(value_type))

def build_patches(frames, allowed, frame_total):
    spatial = spatial_taps(frames)
    pieces = []
    for offset in range(3):
        frame_mask = allowed[offset][:, None, None, None]
        for tapped in spatial:
            pieces.append(tapped[offset:offset + frame_total] * frame_mask)
    return jnp.stack(pieces)

def reference(arrived, row_target, clip_lengths, conv_weight, gn_gain, gn_bias):
    chan_dev = CIN // N_CHAN
    video = jnp.zeros_like(arrived).at[row_target].set(arrived)
    video = video.reshape(FRAMES, WIN_H, CIN, WIN_W)
    member, allowed = clip_masks(0, FRAMES, clip_lengths, arrived.dtype)
    padded = jnp.concatenate([jnp.zeros_like(video[:2]), video], axis=0)
    kernel = conv_weight.reshape(27, CIN, COUT)

    def add_group(group, running):
        frames = lax.dynamic_slice_in_dim(padded, group * chan_dev, chan_dev, 2)
        weights = lax.dynamic_slice_in_dim(kernel, group * chan_dev, chan_dev, 1)
        patches = build_patches(frames, allowed, FRAMES).astype(jnp.float32)
        partial_sum = jnp.einsum('ktncw,kcd->ntwd', patches, weights.astype(jnp.float32), precision=lax.Precision.HIGHEST)
        return running + partial_sum
    conv = lax.fori_loop(0, N_CHAN, add_group, jnp.zeros((WIN_H // 2, FRAMES, WIN_W // 2, COUT), jnp.float32))
    group_size = COUT // GROUPS
    grouped = conv.reshape(WIN_H // 2, FRAMES, WIN_W // 2, GROUPS, group_size)
    frame_sums = lax.optimization_barrier(jnp.sum(grouped, axis=(0, 2, 4)))
    frame_squares = lax.optimization_barrier(jnp.sum(grouped * grouped, axis=(0, 2, 4)))
    clip_sums = jnp.dot(member.T, frame_sums, precision=lax.Precision.HIGHEST)
    clip_squares = jnp.dot(member.T, frame_squares, precision=lax.Precision.HIGHEST)
    entries = clip_lengths.astype(jnp.float32)[:, None] * float(WIN_H // 2 * (WIN_W // 2) * group_size)
    clip_mean = clip_sums / entries
    clip_var = clip_squares / entries - clip_mean * clip_mean
    clip_scale = lax.rsqrt(clip_var + EPSILON)
    frame_mean = jnp.dot(member, clip_mean, precision=lax.Precision.HIGHEST)
    frame_scale = jnp.dot(member, clip_scale, precision=lax.Precision.HIGHEST)
    centred = (grouped - frame_mean[None, :, None, :, None]) * frame_scale[None, :, None, :, None]
    shaped = centred.reshape(conv.shape) * gn_gain + gn_bias
    return jax.nn.silu(shaped).astype(jnp.bfloat16)
```

```python
import jax
import jax.numpy as jnp
from jax import lax
from jax.experimental import pallas as pl
from jax.experimental.pallas import tpu as pltpu
from jax.sharding import Mesh, PartitionSpec as P

TM = ("zl", "x", "co")
CH = ("zh", "y")
SLABS = 32
ROWS = 64
CAP = 4
CH_DEV = 32
NY = 8
OUT_ROWS = 16
COUT = 512
GROUPS = 32
GROUP_SIZE = 16
EPSILON = 1e-05
BF = jnp.bfloat16
F32 = jnp.float32
HIGHEST = lax.Precision.HIGHEST

VMEM = pl.BlockSpec(memory_space=pltpu.VMEM)
SMEM = pl.BlockSpec(memory_space=pltpu.SMEM)


def params(mib):
    return pltpu.CompilerParams(vmem_limit_bytes=mib * 1024 * 1024)


def pack_kernel(target, arrived, send, counts, places):
    places[...] = jnp.full(places.shape, float(ROWS), F32)

    def clear(i, carry):
        counts[i] = 0
        return carry

    lax.fori_loop(0, SLABS, clear, 0)

    def one(i, carry):
        t = target[i]
        owner = lax.shift_right_logical(t, 6)
        rank = counts[owner]
        counts[owner] = rank + 1
        send[owner, pl.ds(pl.multiple_of(rank * CH_DEV, CH_DEV), CH_DEV), :] = arrived[i]
        place = lax.bitwise_and(t, ROWS - 1).astype(F32)
        places[owner, pl.ds(rank, 1), :] = jnp.full((1, 128), place, F32)
        return carry

    lax.fori_loop(0, ROWS, one, 0)
    send[:, CAP * CH_DEV:, :] = places[...].astype(BF)


def place_kernel(got, out, table, table_s, sem):
    zh = lax.axis_index("zh")
    lane = lax.broadcasted_iota(jnp.int32, (16, 128), 1)
    acc = jnp.zeros((16, 128), F32)
    for s in range(SLABS):
        acc = jnp.where(lane == s, got[s, CAP * CH_DEV:, :].astype(F32), acc)
    table[...] = acc.astype(jnp.int32)
    copy = pltpu.make_async_copy(table, table_s, sem)
    copy.start()
    copy.wait()
    for f in range(2):
        first = f * 6 + (1 - lax.bitwise_xor(0, zh)) * 3
        out[first] = jnp.zeros((CH_DEV, 128), BF)

    def spot(i, f, b):
        half = 1 - lax.bitwise_xor(lax.shift_right_logical(i, 3), zh)
        return lax.bitwise_and(i, NY - 1) * 12 + f * 6 + half * 3 + b

    def one(s, carry):
        for r in range(CAP):
            place = table_s[r, s]

            @pl.when(place < ROWS)
            def _():
                row = got[s, r * CH_DEV:(r + 1) * CH_DEV, :]
                f = lax.shift_right_logical(place, 5)
                h = lax.bitwise_and(place, 31)
                odd = lax.bitwise_and(h, 1)
                i = lax.shift_right_logical(h, 1)
                out[spot(i, f, 1 + odd)] = row

                @pl.when((odd == 1) & (i < OUT_ROWS - 1))
                def _():
                    out[spot(i + 1, f, 0)] = row
        return carry

    lax.fori_loop(0, SLABS, one, 0)


def clip_start_of(lengths, frame):
    first = jnp.int32(0)
    end = jnp.int32(0)
    for k in range(4):
        start = end
        end = end + lengths[k]
        first = jnp.where((frame >= start) & (frame < end), start, first)
    return first


def conv_kernel(lengths, own, before, *rest):
    weights, (out_far, out_near, taps, acc) = rest[:NY], rest[NY:]
    step = pl.program_id(0)
    y = lax.axis_index("y")
    core = lax.axis_index("co")
    slab = (lax.axis_index("zl") * 4 + lax.axis_index("x")) * 2 + core
    sign = 2 * core - 1
    sources = [y]
    for s in range(1, 4):
        sources += [y + sign * s, y - sign * s]
    sources.append(y + 4)
    sources = [lax.bitwise_and(s + NY, NY - 1) for s in sources]

    @pl.when(step == 0)
    def _():
        acc[...] = jnp.zeros(acc.shape, F32)
        j = lax.broadcasted_iota(jnp.int32, (192, 128), 0)
        w = lax.broadcasted_iota(jnp.int32, (192, 128), 1)
        wanted = jnp.where(j < 64, 2 * j - 1, jnp.where(j < 128, 2 * j - 128, 2 * j - 255))
        pick = (w == wanted).astype(F32).astype(BF)
        for f in range(4):
            block = before if f < 2 else own
            for sb in range(6):
                at = (f % 2) * 6 + sb
                x = jnp.concatenate([block[s, at] for s in sources], axis=0)
                t = lax.dot_general(pick, x, (((1,), (1,)), ((), ())),
                                    preferred_element_type=F32).astype(BF)
                for e in range(3):
                    taps[f, sb, :, e * 256:(e + 1) * 256] = t[e * 64:(e + 1) * 64]

    a = step // 3
    b = step % 3
    w = jnp.concatenate([ref[e] for e in range(3) for ref in weights], axis=0)
    blocks = []
    for f in range(2):
        frame = slab * 2 + f
        allowed = frame - 2 + a >= clip_start_of(lengths, frame)
        gate = jnp.full((64, 768), jnp.where(allowed, 1.0, 0.0), F32).astype(BF)
        for half in range(2):
            blocks.append(taps[f + a, half * 3 + b] * gate)
    lhs = jnp.concatenate([blocks[0], blocks[2], blocks[1], blocks[3]], axis=0)
    acc[...] += jnp.dot(lhs, w, preferred_element_type=F32)

    @pl.when(step == 8)
    def _():
        out_far[...] = acc[:128]
        out_near[...] = acc[128:]


def group_matrix(channels_first):
    shape = (COUT, 128) if channels_first else (128, COUT)
    c = lax.broadcasted_iota(jnp.int32, shape, 0 if channels_first else 1)
    g = lax.broadcasted_iota(jnp.int32, shape, 1 if channels_first else 0)
    return (lax.shift_right_logical(c, 4) == g).astype(F32)


def member_of(lengths, frame):
    end = jnp.int32(0)
    flags = []
    for k in range(4):
        start = end
        end = end + lengths[k]
        flags.append(jnp.where((frame >= start) & (frame < end), 1.0, 0.0).astype(F32))
    return flags


def stat_kernel(lengths, near, far, conv_out, stats):
    slab = (lax.axis_index("zl") * 4 + lax.axis_index("x")) * 2 + lax.axis_index("co")
    conv = near[...] + far[...]
    conv_out[...] = conv
    rows = []
    for f in range(2):
        part = conv[f * 64:(f + 1) * 64]
        rows.append(jnp.sum(part, axis=0, keepdims=True))
        rows.append(jnp.sum(part * part, axis=0, keepdims=True))
    rows = jnp.concatenate(rows + rows, axis=0)
    grouped = jnp.dot(rows, group_matrix(True), precision=HIGHEST, preferred_element_type=F32)
    m0 = member_of(lengths, slab * 2)
    m1 = member_of(lengths, slab * 2 + 1)
    sums = [grouped[0:1] * m0[k] + grouped[2:3] * m1[k] for k in range(4)]
    squares = [grouped[1:2] * m0[k] + grouped[3:4] * m1[k] for k in range(4)]
    tile = jnp.concatenate(sums + squares, axis=0)
    stats[...] = jnp.broadcast_to(tile[None], stats.shape)


def middle_kernel(got, out):
    out[...] = jnp.broadcast_to(jnp.sum(got[...], axis=0)[None], out.shape)


def final_kernel(lengths, got, conv, gain, bias, out):
    slab = (lax.axis_index("zl") * 4 + lax.axis_index("x")) * 2 + lax.axis_index("co")
    total = jnp.sum(got[...], axis=0)
    spread = group_matrix(False)
    for f in range(2):
        flags = member_of(lengths, slab * 2 + f)
        sums = jnp.zeros((1, 128), F32)
        squares = jnp.zeros((1, 128), F32)
        frames = jnp.float32(0)
        for k in range(4):
            sums = sums + total[k:k + 1] * flags[k]
            squares = squares + total[4 + k:5 + k] * flags[k]
            frames = frames + flags[k] * lengths[k].astype(F32)
        entries = jnp.full((1, 128), frames * float(OUT_ROWS * 64 * GROUP_SIZE), F32)
        mean = sums / entries
        var = squares / entries - mean * mean
        scale = lax.rsqrt(var + EPSILON)
        both = jnp.concatenate([mean, scale] * 4, axis=0)
        wide = jnp.dot(both, spread, precision=HIGHEST, preferred_element_type=F32)
        part = conv[f * 64:(f + 1) * 64]
        v = ((part - wide[0:1]) * wide[1:2]) * gain[...] + bias[...]
        out[f] = (v / (1.0 + jnp.exp(-v))).astype(BF)


def shuffle(x, axis):
    return lax.all_to_all(x, axis, split_axis=0, concat_axis=0, tiled=True)


def gathered_weights(kernel):
    ring = [(c * NY + y, c * NY + (y + (1 if c == 0 else NY - 1)) % NY)
            for c in range(2) for y in range(NY)]
    swap = [(0, 1), (1, 0)]
    shards = [kernel]
    moving = kernel
    for _ in range(3):
        moving = lax.ppermute(moving, ("co", "y"), ring)
        shards += [moving, lax.ppermute(moving, "co", swap)]
    shards.append(lax.ppermute(moving, ("co", "y"), ring))
    return shards


def body(arrived, row_target, clip_lengths, conv_weight, gn_gain, gn_bias):
    weights = gathered_weights(conv_weight.reshape(27, CH_DEV, COUT))
    send = pl.pallas_call(
        pack_kernel,
        out_shape=jax.ShapeDtypeStruct((SLABS, 144, 128), BF),
        in_specs=[SMEM, VMEM],
        out_specs=VMEM,
        scratch_shapes=[pltpu.SMEM((SLABS,), jnp.int32), pltpu.VMEM((SLABS, 16, 128), F32)],
        compiler_params=params(16),
    )(row_target, arrived)
    got = shuffle(send, TM)
    placed = pl.pallas_call(
        place_kernel,
        out_shape=jax.ShapeDtypeStruct((NY * 12, CH_DEV, 128), BF),
        in_specs=[VMEM],
        out_specs=VMEM,
        scratch_shapes=[
            pltpu.VMEM((16, 128), jnp.int32),
            pltpu.SMEM((16, 128), jnp.int32),
            pltpu.SemaphoreType.DMA,
        ],
        compiler_params=params(16),
    )(got)
    own = shuffle(placed.reshape(NY, 12, CH_DEV, 128), "y")
    before = lax.ppermute(own, TM, [(i, i + 1) for i in range(SLABS - 1)])
    whole = pl.BlockSpec((NY, 12, CH_DEV, 128), lambda t: (0, 0, 0, 0))
    tap = pl.BlockSpec((3, CH_DEV, COUT), lambda t: (t, 0, 0))
    part = pl.BlockSpec((128, COUT), lambda t: (0, 0))
    far, near = pl.pallas_call(
        conv_kernel,
        grid=(9,),
        out_shape=[jax.ShapeDtypeStruct((128, COUT), F32)] * 2,
        in_specs=[SMEM, whole, whole] + [tap] * NY,
        out_specs=[part, part],
        scratch_shapes=[pltpu.VMEM((4, 6, 64, 768), BF), pltpu.VMEM((256, COUT), F32)],
        compiler_params=params(32),
    )(clip_lengths, own, before, *weights)
    far = lax.ppermute(far, "zh", [(0, 1), (1, 0)])
    conv, stats = pl.pallas_call(
        stat_kernel,
        out_shape=[jax.ShapeDtypeStruct((128, COUT), F32), jax.ShapeDtypeStruct((16, 8, 128), F32)],
        in_specs=[SMEM, VMEM, VMEM],
        out_specs=[VMEM, VMEM],
        compiler_params=params(16),
    )(clip_lengths, near, far)
    stats = shuffle(stats, CH)
    stats = pl.pallas_call(
        middle_kernel,
        out_shape=jax.ShapeDtypeStruct((SLABS, 8, 128), F32),
        in_specs=[VMEM],
        out_specs=VMEM,
    )(stats)
    stats = shuffle(stats, TM)
    out = pl.pallas_call(
        final_kernel,
        out_shape=jax.ShapeDtypeStruct((2, 64, COUT), BF),
        in_specs=[SMEM, VMEM, VMEM, VMEM, VMEM],
        out_specs=VMEM,
        compiler_params=params(16),
    )(clip_lengths, stats, conv, gn_gain.reshape(1, COUT), gn_bias.reshape(1, COUT))
    return out.reshape(1, 2, 64, COUT)


def solution(mesh):
    fine = Mesh(mesh.devices.reshape(4, 4, 2, 2, 8), TM + CH)
    in_specs = (P(TM, CH, None), P(TM), P(), P(None, None, None, CH, None), P(), P())
    out_specs = P(CH, TM, None, None)
    return jax.shard_map(body, mesh=fine, in_specs=in_specs, out_specs=out_specs, check_vma=False)
```

```python
import functools

import jax
import jax.numpy as jnp
from jax import lax
from jax.experimental import pallas as pl
from jax.experimental.pallas import tpu as pltpu
from jax.sharding import Mesh, PartitionSpec as P

TM = ("zl", "x", "co")
CH = ("zh", "y")
SLABS = 32
ROWS = 64
CAP = 4
CH_DEV = 32
NY = 8
OUT_ROWS = 16
COUT = 512
GROUPS = 32
GROUP_SIZE = 16
EPSILON = 1e-05
BF = jnp.bfloat16
F32 = jnp.float32
HIGHEST = lax.Precision.HIGHEST

VMEM = pl.BlockSpec(memory_space=pltpu.VMEM)
SMEM = pl.BlockSpec(memory_space=pltpu.SMEM)


def params(mib):
    return pltpu.CompilerParams(vmem_limit_bytes=mib * 1024 * 1024)


def pack_kernel(target, arrived, send, places, counts, sem):
    places[...] = jnp.full(places.shape, float(ROWS), F32)

    def clear(i, carry):
        counts[i] = 0
        return carry

    lax.fori_loop(0, SLABS, clear, 0)

    def one(i, carry):
        t = target[i]
        owner = lax.shift_right_logical(t, 6)
        rank = counts[owner]
        counts[owner] = rank + 1
        pltpu.make_async_copy(arrived.at[i], send.at[owner * CAP + rank], sem).start()
        place = lax.bitwise_and(t, ROWS - 1).astype(F32)
        places[owner, pl.ds(rank, 1), :] = jnp.full((1, 128), place, F32)
        return carry

    lax.fori_loop(0, ROWS, one, 0)
    pltpu.make_async_copy(arrived, send.at[pl.ds(0, ROWS)], sem).wait()


def spot(zh, i, f, b):
    near = 1 - lax.bitwise_xor(lax.shift_right_logical(i, 3), zh)
    return near * 48 + lax.bitwise_and(i, NY - 1) * 6 + f * 3 + b


def table_kernel(got, moves, table, table_s, sem):
    zh = lax.axis_index("zh")
    lane = lax.broadcasted_iota(jnp.int32, (8, 128), 1)
    acc = jnp.zeros((8, 128), F32)
    for s in range(SLABS):
        acc = jnp.where(lane == s, got[s], acc)
    table[...] = acc.astype(jnp.int32)
    copy = pltpu.make_async_copy(table, table_s, sem)
    copy.start()
    copy.wait()

    def one(s, n):
        for r in range(CAP):
            place = table_s[r, s]
            f = lax.shift_right_logical(place, 5)
            h = lax.bitwise_and(place, 31)
            odd = lax.bitwise_and(h, 1)
            i = lax.shift_right_logical(h, 1)
            first = spot(zh, i, f, 1 + odd)
            shared = (odd == 1) & (i < OUT_ROWS - 1)
            moves[0, n] = s * CAP + r
            moves[1, n] = first
            moves[2, n] = jnp.where(shared, spot(zh, i + 1, f, 0), first)
            n = jnp.where(place < ROWS, n + 1, n)
        return n

    lax.fori_loop(0, SLABS, one, jnp.int32(0))


def place_kernel(moves, got, far, near, both):
    zh = lax.axis_index("zh")
    for f in range(2):
        both[spot(zh, jnp.int32(0), f, 0)] = jnp.zeros((CH_DEV, 128), BF)

    def some(n, carry):
        for k in range(8):
            row = got[moves[0, n * 8 + k]]
            both[moves[1, n * 8 + k]] = row
            both[moves[2, n * 8 + k]] = row
        return carry

    lax.fori_loop(0, ROWS // 8, some, 0)
    far[...] = both[:48]
    near[...] = both[48:]


def clip_start_of(lengths, frame):
    first = jnp.int32(0)
    end = jnp.int32(0)
    for k in range(4):
        start = end
        end = end + lengths[k]
        first = jnp.where((frame >= start) & (frame < end), start, first)
    return first


def conv_kernel(late, lengths, frames, *rest):
    weights, rest = rest[:NY], rest[NY:]
    out, taps = rest[-2:]
    y = lax.axis_index("y")
    core = lax.axis_index("co")
    slab = (lax.axis_index("zl") * 4 + lax.axis_index("x")) * 2 + core
    sign = 2 * core - 1
    sources = [y]
    for s in range(1, 4):
        sources += [y + sign * s, y - sign * s]
    sources.append(y + 4)
    sources = [lax.bitwise_and(s + NY, NY - 1) for s in sources]
    j = lax.broadcasted_iota(jnp.int32, (192, 128), 0)
    w = lax.broadcasted_iota(jnp.int32, (192, 128), 1)
    wanted = jnp.where(j < 64, 2 * j - 1, jnp.where(j < 128, 2 * j - 128, 2 * j - 255))
    pick = (w == wanted).astype(F32).astype(BF)
    for t in range(2):
        for b in range(3):
            x = jnp.concatenate([frames[s, t * 3 + b] for s in sources], axis=0)
            picked = lax.dot_general(pick, x, (((1,), (1,)), ((), ())),
                                     preferred_element_type=F32).astype(BF)
            for e in range(3):
                taps[t, b, :, e * 256:(e + 1) * 256] = picked[e * 64:(e + 1) * 64]
    out[...] = jnp.zeros(out.shape, F32) if late else rest[0][...]

    def gate(f, a):
        frame = slab * 2 + f
        allowed = frame - 2 + a >= clip_start_of(lengths, frame)
        return jnp.full((64, 768), jnp.where(allowed, 1.0, 0.0), F32).astype(BF)

    plan = [(2, [(0, 0), (1, 1)]), (1, [(1, 0)])] if late else [(0, [(0, 0), (1, 1)]), (1, [(0, 1)])]

    def row_tap(b, carry):
        for a, pairs in plan:
            tap = (a * 3 + b) * 3
            kernel = jnp.concatenate([ref[tap + e] for e in range(3) for ref in weights], axis=0)
            lhs = jnp.concatenate([taps[t, b] * gate(f, a) for f, t in pairs], axis=0)
            first = pairs[0][0] * 64
            rows = slice(first, first + 64 * len(pairs))
            out[rows] += jnp.dot(lhs, kernel, preferred_element_type=F32)
        return carry

    lax.fori_loop(0, 3, row_tap, 0)


def group_matrix(channels_first):
    shape = (COUT, 128) if channels_first else (128, COUT)
    c = lax.broadcasted_iota(jnp.int32, shape, 0 if channels_first else 1)
    g = lax.broadcasted_iota(jnp.int32, shape, 1 if channels_first else 0)
    return (lax.shift_right_logical(c, 4) == g).astype(F32)


def member_of(lengths, frame):
    end = jnp.int32(0)
    flags = []
    for k in range(4):
        start = end
        end = end + lengths[k]
        flags.append(jnp.where((frame >= start) & (frame < end), 1.0, 0.0).astype(F32))
    return flags


def stat_kernel(lengths, near, far, conv_out, stats):
    slab = (lax.axis_index("zl") * 4 + lax.axis_index("x")) * 2 + lax.axis_index("co")
    conv = near[...] + far[...]
    conv_out[...] = conv
    rows = []
    for f in range(2):
        part = conv[f * 64:(f + 1) * 64]
        rows.append(jnp.sum(part, axis=0, keepdims=True))
        rows.append(jnp.sum(part * part, axis=0, keepdims=True))
    rows = jnp.concatenate(rows + rows, axis=0)
    grouped = jnp.dot(rows, group_matrix(True), precision=HIGHEST, preferred_element_type=F32)
    m0 = member_of(lengths, slab * 2)
    m1 = member_of(lengths, slab * 2 + 1)
    sums = [grouped[0:1] * m0[k] + grouped[2:3] * m1[k] for k in range(4)]
    squares = [grouped[1:2] * m0[k] + grouped[3:4] * m1[k] for k in range(4)]
    tile = jnp.concatenate(sums + squares, axis=0)
    stats[...] = jnp.broadcast_to(tile[None], stats.shape)


def middle_kernel(got, out):
    out[...] = jnp.broadcast_to(jnp.sum(got[...], axis=0)[None], out.shape)


def final_kernel(lengths, got, conv, gain, bias, out):
    slab = (lax.axis_index("zl") * 4 + lax.axis_index("x")) * 2 + lax.axis_index("co")
    total = jnp.sum(got[...], axis=0)
    spread = group_matrix(False)
    for f in range(2):
        flags = member_of(lengths, slab * 2 + f)
        sums = jnp.zeros((1, 128), F32)
        squares = jnp.zeros((1, 128), F32)
        frames = jnp.float32(0)
        for k in range(4):
            sums = sums + total[k:k + 1] * flags[k]
            squares = squares + total[4 + k:5 + k] * flags[k]
            frames = frames + flags[k] * lengths[k].astype(F32)
        entries = jnp.full((1, 128), frames * float(OUT_ROWS * 64 * GROUP_SIZE), F32)
        mean = sums / entries
        var = squares / entries - mean * mean
        scale = lax.rsqrt(var + EPSILON)
        both = jnp.concatenate([mean, scale] * 4, axis=0)
        wide = jnp.dot(both, spread, precision=HIGHEST, preferred_element_type=F32)
        part = conv[f * 64:(f + 1) * 64]
        v = ((part - wide[0:1]) * wide[1:2]) * gain[...] + bias[...]
        out[f] = (v / (1.0 + jnp.exp(-v))).astype(BF)


def shuffle(x, axis):
    return lax.all_to_all(x, axis, split_axis=0, concat_axis=0, tiled=True)


def gathered_weights(kernel):
    ring = [(c * NY + y, c * NY + (y + (1 if c == 0 else NY - 1)) % NY)
            for c in range(2) for y in range(NY)]
    swap = [(0, 1), (1, 0)]
    moved = [kernel]
    swapped = []
    for step in range(4):
        moved.append(lax.ppermute(moved[-1], ("co", "y"), ring))
        if step < 3:
            swapped.append(lax.ppermute(moved[-1], "co", swap))
    return moved, swapped


def convolve(late, lengths, frames, weights, start=()):
    return pl.pallas_call(
        functools.partial(conv_kernel, late),
        out_shape=jax.ShapeDtypeStruct((128, COUT), F32),
        in_specs=[SMEM] + [VMEM] * (1 + NY + len(start)),
        out_specs=VMEM,
        scratch_shapes=[pltpu.VMEM((2, 3, 64, 768), BF)],
        compiler_params=params(24),
    )(lengths, frames, *weights, *start)


def body(arrived, row_target, clip_lengths, conv_weight, gn_gain, gn_bias):
    moved, swapped = gathered_weights(conv_weight.reshape(27, CH_DEV, COUT))
    send, places = pl.pallas_call(
        pack_kernel,
        out_shape=[
            jax.ShapeDtypeStruct((SLABS * CAP, CH_DEV, 128), BF),
            jax.ShapeDtypeStruct((SLABS, 8, 128), F32),
        ],
        in_specs=[SMEM, pl.BlockSpec(memory_space=pl.ANY)],
        out_specs=[pl.BlockSpec(memory_space=pl.ANY), VMEM],
        scratch_shapes=[pltpu.SMEM((SLABS,), jnp.int32), pltpu.SemaphoreType.DMA],
        compiler_params=params(8),
    )(row_target, arrived)
    got = shuffle(send, TM)
    places = shuffle(places, TM)
    moves = pl.pallas_call(
        table_kernel,
        out_shape=jax.ShapeDtypeStruct((3, 128), jnp.int32),
        in_specs=[VMEM],
        out_specs=SMEM,
        scratch_shapes=[
            pltpu.VMEM((8, 128), jnp.int32),
            pltpu.SMEM((8, 128), jnp.int32),
            pltpu.SemaphoreType.DMA,
        ],
    )(places)
    got, moved[3] = lax.optimization_barrier((got, moved[3]))
    far, near = pl.pallas_call(
        place_kernel,
        out_shape=[jax.ShapeDtypeStruct((NY * 6, CH_DEV, 128), BF)] * 2,
        in_specs=[SMEM, VMEM],
        out_specs=[VMEM, VMEM],
        scratch_shapes=[pltpu.VMEM((96, CH_DEV, 128), BF)],
        compiler_params=params(8),
    )(moves, got)
    weights = [moved[0], moved[1], swapped[0], moved[2], swapped[1], moved[3], swapped[2], moved[4]]
    sums = []
    owns = [shuffle(rows.reshape(NY, 6, CH_DEV, 128), "y") for rows in (far, near)]
    befores = [lax.ppermute(own, TM, [(i, i + 1) for i in range(SLABS - 1)]) for own in owns]
    for own, before in zip(owns, befores):
        part = convolve(True, clip_lengths, own, weights)
        sums.append(convolve(False, clip_lengths, before, weights, (part,)))
    far, near = sums
    far = lax.ppermute(far, "zh", [(0, 1), (1, 0)])
    conv, stats = pl.pallas_call(
        stat_kernel,
        out_shape=[jax.ShapeDtypeStruct((128, COUT), F32), jax.ShapeDtypeStruct((16, 8, 128), F32)],
        in_specs=[SMEM, VMEM, VMEM],
        out_specs=[VMEM, VMEM],
        compiler_params=params(16),
    )(clip_lengths, near, far)
    stats = shuffle(stats, ("y", "co"))
    stats = pl.pallas_call(
        middle_kernel,
        out_shape=jax.ShapeDtypeStruct((SLABS, 8, 128), F32),
        in_specs=[VMEM],
        out_specs=VMEM,
    )(stats)
    stats = shuffle(stats, ("zl", "zh", "x"))
    out = pl.pallas_call(
        final_kernel,
        out_shape=jax.ShapeDtypeStruct((2, 64, COUT), BF),
        in_specs=[SMEM, VMEM, VMEM, VMEM, VMEM],
        out_specs=VMEM,
        compiler_params=params(16),
    )(clip_lengths, stats, conv, gn_gain.reshape(1, COUT), gn_bias.reshape(1, COUT))
    return out.reshape(1, 2, 64, COUT)


def solution(mesh):
    fine = Mesh(mesh.devices.reshape(4, 4, 2, 2, 8), TM + CH)
    in_specs = (P(TM, CH, None), P(TM), P(), P(None, None, None, CH, None), P(), P())
    out_specs = P(CH, TM, None, None)
    return jax.shard_map(body, mesh=fine, in_specs=in_specs, out_specs=out_specs, check_vma=False)
```

```python
import functools

import jax
import jax.numpy as jnp
from jax import lax
from jax.experimental import pallas as pl
from jax.experimental.pallas import tpu as pltpu
from jax.sharding import Mesh, PartitionSpec as P

TM = ("zl", "x", "co")
CH = ("zh", "y")
SLABS = 32
ROWS = 64
CAP = 4
CH_DEV = 32
NY = 8
OUT_ROWS = 16
COUT = 512
GROUPS = 32
GROUP_SIZE = 16
EPSILON = 1e-05
BF = jnp.bfloat16
F32 = jnp.float32
HIGHEST = lax.Precision.HIGHEST

VMEM = pl.BlockSpec(memory_space=pltpu.VMEM)
SMEM = pl.BlockSpec(memory_space=pltpu.SMEM)
HBM = pl.BlockSpec(memory_space=pltpu.HBM)


def params(mib):
    return pltpu.CompilerParams(vmem_limit_bytes=mib * 1024 * 1024)


def pack_kernel(target, arrived, send, counts, places, rounded, sems):
    places[...] = jnp.full(places.shape, float(ROWS), F32)

    def clear(i, carry):
        counts[i] = 0
        return carry

    lax.fori_loop(0, SLABS, clear, 0)

    def one(i, carry):
        t = target[i]
        owner = lax.shift_right_logical(t, 6)
        rank = counts[owner]
        counts[owner] = rank + 1
        slot = pl.ds(pl.multiple_of(rank * CH_DEV, CH_DEV), CH_DEV)
        pltpu.make_async_copy(arrived.at[i], send.at[owner, slot], sems.at[0]).start()
        place = lax.bitwise_and(t, ROWS - 1).astype(F32)
        places[owner, pl.ds(rank, 1), :] = jnp.full((1, 128), place, F32)
        return carry

    lax.fori_loop(0, ROWS, one, 0)
    rounded[...] = places[...].astype(BF)
    listed = pltpu.make_async_copy(rounded, send.at[:, pl.ds(CAP * CH_DEV, 16)], sems.at[1])
    listed.start()
    pltpu.make_async_copy(arrived, arrived, sems.at[0]).wait()
    listed.wait()


def my_slab():
    return (lax.axis_index("zl") * 4 + lax.axis_index("x")) * 2 + lax.axis_index("co")


def spot(zh, i, f, b):
    near = 1 - lax.bitwise_xor(lax.shift_right_logical(i, 3), zh)
    return near * 48 + lax.bitwise_and(i, NY - 1) * 6 + f * 3 + b


def place_kernel(got, far, near, both, table, moves, sems):
    zh = lax.axis_index("zh")
    lane = lax.broadcasted_iota(jnp.int32, (16, 128), 1)
    place = jnp.full((16, 128), float(ROWS), F32)
    for s in range(SLABS):
        place = jnp.where(lane == s, got[s, CAP * CH_DEV:, :].astype(F32), place)
    place = place.astype(jnp.int32)
    f = lax.shift_right_logical(place, 5)
    h = lax.bitwise_and(place, 31)
    odd = lax.bitwise_and(h, 1)
    i = lax.shift_right_logical(h, 1)
    first = spot(zh, i, f, 1 + odd)
    second = jnp.where((odd == 1) & (i < OUT_ROWS - 1), spot(zh, i + 1, f, 0), first)
    table[...] = jnp.where(place < ROWS, first * 128 + second, 96 * 128 + 96)
    copy = pltpu.make_async_copy(table, moves, sems.at[0])
    copy.start()
    for f in range(2):
        both[spot(zh, jnp.int32(0), f, 0)] = jnp.zeros((CH_DEV, 128), BF)
    copy.wait()

    def some(s, carry):
        for source in (2 * s, 2 * s + 1):
            for r in range(CAP):
                move = moves[r, source]
                row = got[source, r * CH_DEV:(r + 1) * CH_DEV, :]
                both[lax.shift_right_logical(move, 7)] = row
                both[lax.bitwise_and(move, 127)] = row
        return carry

    lax.fori_loop(0, SLABS // 2, some, 0)
    copies = [
        pltpu.make_async_copy(both.at[pl.ds(48 * k, 48)], out, sems.at[k])
        for k, out in enumerate((far, near))
    ]
    for copy in copies:
        copy.start()
    for copy in copies:
        copy.wait()


def clip_start_of(lengths, frame):
    first = jnp.int32(0)
    end = jnp.int32(0)
    for k in range(4):
        start = end
        end = end + lengths[k]
        first = jnp.where((frame >= start) & (frame < end), start, first)
    return first


def conv_kernel(lengths, frames, *rest):
    weights, (own, after, taps) = rest[:NY], rest[NY:]
    y = lax.axis_index("y")
    core = lax.axis_index("co")
    slab = my_slab()
    sign = 2 * core - 1
    sources = [y]
    for s in range(1, 4):
        sources += [y + sign * s, y - sign * s]
    sources.append(y + 4)
    sources = [lax.bitwise_and(s + NY, NY - 1) for s in sources]
    j = lax.broadcasted_iota(jnp.int32, (192, 128), 0)
    w = lax.broadcasted_iota(jnp.int32, (192, 128), 1)
    wanted = jnp.where(j < 64, 2 * j - 1, jnp.where(j < 128, 2 * j - 128, 2 * j - 255))
    pick = (w == wanted).astype(F32).astype(BF)
    for t in range(2):
        for b in range(3):
            x = jnp.concatenate([frames[s, t * 3 + b] for s in sources], axis=0)
            picked = lax.dot_general(pick, x, (((1,), (1,)), ((), ())),
                                     preferred_element_type=F32).astype(BF)
            for e in range(3):
                taps[b, t * 64:(t + 1) * 64, e * 256:(e + 1) * 256] = picked[e * 64:(e + 1) * 64]
    own[...] = jnp.zeros(own.shape, F32)
    after[...] = jnp.zeros(after.shape, F32)

    def gates(a):
        parts = []
        for t in range(2):
            frame = slab * 2 + t
            allowed = frame >= clip_start_of(lengths, frame + 2 - a)
            parts.append(jnp.full((64, 768), jnp.where(allowed, 1.0, 0.0), F32).astype(BF))
        return jnp.concatenate(parts, axis=0)

    def row_tap(b, carry):
        lhs = taps[b]
        for a in range(3):
            tap = (a * 3 + b) * 3
            kernel = jnp.concatenate([ref[tap + e] for e in range(3) for ref in weights], axis=0)
            part = jnp.dot(lhs * gates(a), kernel, preferred_element_type=F32)
            if a == 0:
                after[...] += part
            elif a == 1:
                own[64:] += part[:64]
                after[:64] += part[64:]
            else:
                own[...] += part
        return carry

    lax.fori_loop(0, 3, row_tap, 0)


def group_matrix(channels_first):
    shape = (COUT, 128) if channels_first else (128, COUT)
    c = lax.broadcasted_iota(jnp.int32, shape, 0 if channels_first else 1)
    g = lax.broadcasted_iota(jnp.int32, shape, 1 if channels_first else 0)
    return (lax.shift_right_logical(c, 4) == g).astype(F32)


def member_of(lengths, frame):
    end = jnp.int32(0)
    flags = []
    for k in range(4):
        start = end
        end = end + lengths[k]
        flags.append(jnp.where((frame >= start) & (frame < end), 1.0, 0.0).astype(F32))
    return flags


def stat_kernel(lengths, near, before, conv_out, stats):
    slab = my_slab()
    conv = near[...] + before[...]
    conv_out[...] = conv
    rows = []
    for f in range(2):
        part = conv[f * 64:(f + 1) * 64]
        rows.append(jnp.sum(part, axis=0, keepdims=True))
        rows.append(jnp.sum(part * part, axis=0, keepdims=True))
    rows = jnp.concatenate(rows + rows, axis=0)
    grouped = jnp.dot(rows, group_matrix(True), precision=HIGHEST, preferred_element_type=F32)
    m0 = member_of(lengths, slab * 2)
    m1 = member_of(lengths, slab * 2 + 1)
    sums = [grouped[0:1] * m0[k] + grouped[2:3] * m1[k] for k in range(4)]
    squares = [grouped[1:2] * m0[k] + grouped[3:4] * m1[k] for k in range(4)]
    tile = jnp.concatenate(sums + squares, axis=0)
    stats[...] = jnp.broadcast_to(tile[None], stats.shape)


def middle_kernel(got, out):
    out[...] = jnp.broadcast_to(jnp.sum(got[...], axis=0)[None], out.shape)


def final_kernel(lengths, got, conv, gain, bias, out):
    slab = my_slab()
    total = jnp.sum(got[...], axis=0)
    spread = group_matrix(False)
    for f in range(2):
        flags = member_of(lengths, slab * 2 + f)
        sums = jnp.zeros((1, 128), F32)
        squares = jnp.zeros((1, 128), F32)
        frames = jnp.float32(0)
        for k in range(4):
            sums = sums + total[k:k + 1] * flags[k]
            squares = squares + total[4 + k:5 + k] * flags[k]
            frames = frames + flags[k] * lengths[k].astype(F32)
        entries = jnp.full((1, 128), frames * float(OUT_ROWS * 64 * GROUP_SIZE), F32)
        mean = sums / entries
        var = squares / entries - mean * mean
        scale = lax.rsqrt(var + EPSILON)
        both = jnp.concatenate([mean, scale] * 4, axis=0)
        wide = jnp.dot(both, spread, precision=HIGHEST, preferred_element_type=F32)
        part = conv[f * 64:(f + 1) * 64]
        v = ((part - wide[0:1]) * wide[1:2]) * gain[...] + bias[...]
        out[f] = (v / (1.0 + jnp.exp(-v))).astype(BF)


def shuffle(x, axis):
    return lax.all_to_all(x, axis, split_axis=0, concat_axis=0, tiled=True)


def gathered_weights(kernel):
    ring = [(c * NY + y, c * NY + (y + (1 if c == 0 else NY - 1)) % NY)
            for c in range(2) for y in range(NY)]
    swap = [(0, 1), (1, 0)]
    moved = [kernel]
    swapped = []
    for step in range(4):
        moved.append(lax.ppermute(moved[-1], ("co", "y"), ring))
        if step < 3:
            swapped.append(lax.ppermute(moved[-1], "co", swap))
    return moved, swapped


def convolve(lengths, frames, weights):
    return pl.pallas_call(
        conv_kernel,
        out_shape=[jax.ShapeDtypeStruct((128, COUT), F32)] * 2,
        in_specs=[SMEM] + [VMEM] * (1 + NY),
        out_specs=[VMEM, VMEM],
        scratch_shapes=[pltpu.VMEM((3, 128, 768), BF)],
        compiler_params=params(24),
    )(lengths, frames, *weights)


def body(arrived, row_target, clip_lengths, conv_weight, gn_gain, gn_bias):
    moved, swapped = gathered_weights(conv_weight.reshape(27, CH_DEV, COUT))
    send = pl.pallas_call(
        pack_kernel,
        out_shape=jax.ShapeDtypeStruct((SLABS, 144, 128), BF),
        in_specs=[SMEM, HBM],
        out_specs=HBM,
        scratch_shapes=[
            pltpu.SMEM((SLABS,), jnp.int32),
            pltpu.VMEM((SLABS, 16, 128), F32),
            pltpu.VMEM((SLABS, 16, 128), BF),
            pltpu.SemaphoreType.DMA((2,)),
        ],
        compiler_params=params(60),
    )(row_target, arrived)
    got = shuffle(send, TM)
    got, moved[3], swapped[0], swapped[1] = lax.optimization_barrier(
        (got, moved[3], swapped[0], swapped[1])
    )
    far, near = pl.pallas_call(
        place_kernel,
        out_shape=[jax.ShapeDtypeStruct((NY * 6, CH_DEV, 128), BF)] * 2,
        in_specs=[VMEM],
        out_specs=[HBM, HBM],
        scratch_shapes=[
            pltpu.VMEM((97, CH_DEV, 128), BF),
            pltpu.VMEM((16, 128), jnp.int32),
            pltpu.SMEM((16, 128), jnp.int32),
            pltpu.SemaphoreType.DMA((2,)),
        ],
        compiler_params=params(8),
    )(got)
    weights = [moved[0], moved[1], swapped[0], moved[2], swapped[1], moved[3], swapped[2], moved[4]]
    onward = [(i, i + 1) for i in range(SLABS - 1)]
    far = shuffle(far.reshape(NY, 6, CH_DEV, 128), "y")
    near = shuffle(near.reshape(NY, 6, CH_DEV, 128), "y")
    far, far_after = convolve(clip_lengths, far, weights)
    far_before = lax.ppermute(far_after, TM, onward)
    near, near_after = convolve(clip_lengths, near, weights)
    near_before = lax.ppermute(near_after, TM, onward)
    far = lax.ppermute(far + far_before, "zh", [(0, 1), (1, 0)])
    near = near + far
    conv, stats = pl.pallas_call(
        stat_kernel,
        out_shape=[jax.ShapeDtypeStruct((128, COUT), F32), jax.ShapeDtypeStruct((16, 8, 128), F32)],
        in_specs=[SMEM, VMEM, VMEM],
        out_specs=[VMEM, VMEM],
        compiler_params=params(16),
    )(clip_lengths, near, near_before)
    stats = shuffle(stats, ("y", "co"))
    stats = pl.pallas_call(
        middle_kernel,
        out_shape=jax.ShapeDtypeStruct((SLABS, 8, 128), F32),
        in_specs=[VMEM],
        out_specs=VMEM,
    )(stats)
    stats = shuffle(stats, ("zl", "zh", "x"))
    out = pl.pallas_call(
        final_kernel,
        out_shape=jax.ShapeDtypeStruct((2, 64, COUT), BF),
        in_specs=[SMEM, VMEM, VMEM, VMEM, VMEM],
        out_specs=VMEM,
        compiler_params=params(16),
    )(clip_lengths, stats, conv, gn_gain.reshape(1, COUT), gn_bias.reshape(1, COUT))
    return out.reshape(1, 2, 64, COUT)


def solution(mesh):
    fine = Mesh(mesh.devices.reshape(4, 4, 2, 2, 8), TM + CH)
    in_specs = (P(TM, CH, None), P(TM), P(), P(None, None, None, CH, None), P(), P())
    out_specs = P(CH, TM, None, None)
    return jax.shard_map(body, mesh=fine, in_specs=in_specs, out_specs=out_specs, check_vma=False)
```

```python
import functools

import jax
import jax.numpy as jnp
from jax import lax
from jax.experimental import pallas as pl
from jax.experimental.pallas import tpu as pltpu
from jax.sharding import Mesh, PartitionSpec as P

TM = ("zl", "x", "co")
CH = ("zh", "y")
SLABS = 32
ROWS = 64
CAP = 4
CH_DEV = 32
NY = 8
OUT_ROWS = 16
COUT = 512
GROUPS = 32
GROUP_SIZE = 16
EPSILON = 1e-05
BF = jnp.bfloat16
F32 = jnp.float32
HIGHEST = lax.Precision.HIGHEST

VMEM = pl.BlockSpec(memory_space=pltpu.VMEM)
SMEM = pl.BlockSpec(memory_space=pltpu.SMEM)
HBM = pl.BlockSpec(memory_space=pltpu.HBM)


def params(mib):
    return pltpu.CompilerParams(vmem_limit_bytes=mib * 1024 * 1024)


def pack_kernel(target, arrived, send, counts, places, rounded, sems):
    places[...] = jnp.full(places.shape, float(ROWS), F32)

    def clear(i, carry):
        counts[i] = 0
        return carry

    lax.fori_loop(0, SLABS, clear, 0)

    def one(i, carry):
        t = target[i]
        owner = lax.shift_right_logical(t, 6)
        rank = counts[owner]
        counts[owner] = rank + 1
        slot = pl.ds(pl.multiple_of(rank * CH_DEV, CH_DEV), CH_DEV)
        pltpu.make_async_copy(arrived.at[i], send.at[owner, slot], sems.at[0]).start()
        place = lax.bitwise_and(t, ROWS - 1).astype(F32)
        places[owner, pl.ds(rank, 1), :] = jnp.full((1, 128), place, F32)
        return carry

    lax.fori_loop(0, ROWS, one, 0)
    rounded[...] = places[...].astype(BF)
    listed = pltpu.make_async_copy(rounded, send.at[:, pl.ds(CAP * CH_DEV, 16)], sems.at[1])
    listed.start()
    pltpu.make_async_copy(arrived, arrived, sems.at[0]).wait()
    listed.wait()


def my_slab():
    return (lax.axis_index("zl") * 4 + lax.axis_index("x")) * 2 + lax.axis_index("co")


def spot(zh, i, f, b):
    near = 1 - lax.bitwise_xor(lax.shift_right_logical(i, 3), zh)
    return near * 48 + lax.bitwise_and(i, NY - 1) * 6 + f * 3 + b


def place_kernel(got, far, near, both, table, moves, sems):
    zh = lax.axis_index("zh")
    lane = lax.broadcasted_iota(jnp.int32, (16, 128), 1)
    place = jnp.full((16, 128), float(ROWS), F32)
    for s in range(SLABS):
        place = jnp.where(lane == s, got[s, CAP * CH_DEV:, :].astype(F32), place)
    place = place.astype(jnp.int32)
    f = lax.shift_right_logical(place, 5)
    h = lax.bitwise_and(place, 31)
    odd = lax.bitwise_and(h, 1)
    i = lax.shift_right_logical(h, 1)
    first = spot(zh, i, f, 1 + odd)
    second = jnp.where((odd == 1) & (i < OUT_ROWS - 1), spot(zh, i + 1, f, 0), first)
    table[...] = jnp.where(place < ROWS, first * 128 + second, 96 * 128 + 96)
    copy = pltpu.make_async_copy(table, moves, sems.at[0])
    copy.start()
    for f in range(2):
        both[spot(zh, jnp.int32(0), f, 0)] = jnp.zeros((CH_DEV, 128), BF)
    copy.wait()

    def some(s, carry):
        for source in (2 * s, 2 * s + 1):
            for r in range(CAP):
                move = moves[r, source]
                row = got[source, r * CH_DEV:(r + 1) * CH_DEV, :]
                both[lax.shift_right_logical(move, 7)] = row
                both[lax.bitwise_and(move, 127)] = row
        return carry

    lax.fori_loop(0, SLABS // 2, some, 0)
    copies = [
        pltpu.make_async_copy(both.at[pl.ds(48 * k, 48)], out, sems.at[k])
        for k, out in enumerate((far, near))
    ]
    for copy in copies:
        copy.start()
    for copy in copies:
        copy.wait()


def clip_start_of(lengths, frame):
    first = jnp.int32(0)
    end = jnp.int32(0)
    for k in range(4):
        start = end
        end = end + lengths[k]
        first = jnp.where((frame >= start) & (frame < end), start, first)
    return first


def conv_kernel(lengths, frames, *rest):
    weights, (own, after, taps) = rest[:NY], rest[NY:]
    y = lax.axis_index("y")
    core = lax.axis_index("co")
    slab = my_slab()
    sign = 2 * core - 1
    sources = [y]
    for s in range(1, 4):
        sources += [y + sign * s, y - sign * s]
    sources.append(y + 4)
    sources = [lax.bitwise_and(s + NY, NY - 1) for s in sources]
    j = lax.broadcasted_iota(jnp.int32, (192, 128), 0)
    w = lax.broadcasted_iota(jnp.int32, (192, 128), 1)
    wanted = jnp.where(j < 64, 2 * j - 1, jnp.where(j < 128, 2 * j - 128, 2 * j - 255))
    pick = (w == wanted).astype(F32).astype(BF)
    for t in range(2):
        for b in range(3):
            x = jnp.concatenate([frames[s, t * 3 + b] for s in sources], axis=0)
            picked = lax.dot_general(pick, x, (((1,), (1,)), ((), ())),
                                     preferred_element_type=F32).astype(BF)
            for e in range(3):
                taps[b, t * 64:(t + 1) * 64, e * 256:(e + 1) * 256] = picked[e * 64:(e + 1) * 64]
    own[...] = jnp.zeros(own.shape, F32)
    after[...] = jnp.zeros(after.shape, F32)

    def gates(a):
        parts = []
        for t in range(2):
            frame = slab * 2 + t
            allowed = frame >= clip_start_of(lengths, frame + 2 - a)
            parts.append(jnp.full((64, 768), jnp.where(allowed, 1.0, 0.0), F32).astype(BF))
        return jnp.concatenate(parts, axis=0)

    def row_tap(b, carry):
        lhs = taps[b]
        for a in range(3):
            tap = (a * 3 + b) * 3
            kernel = jnp.concatenate([ref[tap + e] for e in range(3) for ref in weights], axis=0)
            part = jnp.dot(lhs * gates(a), kernel, preferred_element_type=F32)
            if a == 0:
                after[...] += part
            elif a == 1:
                own[64:] += part[:64]
                after[:64] += part[64:]
            else:
                own[...] += part
        return carry

    lax.fori_loop(0, 3, row_tap, 0)


def group_matrix(channels_first):
    shape = (COUT, 128) if channels_first else (128, COUT)
    c = lax.broadcasted_iota(jnp.int32, shape, 0 if channels_first else 1)
    g = lax.broadcasted_iota(jnp.int32, shape, 1 if channels_first else 0)
    return (lax.shift_right_logical(c, 4) == g).astype(F32)


def member_of(lengths, frame):
    end = jnp.int32(0)
    flags = []
    for k in range(4):
        start = end
        end = end + lengths[k]
        flags.append(jnp.where((frame >= start) & (frame < end), 1.0, 0.0).astype(F32))
    return flags


def stat_kernel(lengths, near, before, conv_out, stats):
    slab = my_slab()
    conv = near[...] + before[...]
    conv_out[...] = conv
    rows = []
    for f in range(2):
        part = conv[f * 64:(f + 1) * 64]
        rows.append(jnp.sum(part, axis=0, keepdims=True))
        rows.append(jnp.sum(part * part, axis=0, keepdims=True))
    rows = jnp.concatenate(rows + rows, axis=0)
    grouped = jnp.dot(rows, group_matrix(True), precision=HIGHEST, preferred_element_type=F32)
    m0 = member_of(lengths, slab * 2)
    m1 = member_of(lengths, slab * 2 + 1)
    sums = [grouped[0:1] * m0[k] + grouped[2:3] * m1[k] for k in range(4)]
    squares = [grouped[1:2] * m0[k] + grouped[3:4] * m1[k] for k in range(4)]
    tile = jnp.concatenate(sums + squares, axis=0)
    stats[...] = jnp.broadcast_to(tile[None], stats.shape)


def middle_kernel(got, out):
    out[...] = jnp.broadcast_to(jnp.sum(got[...], axis=0)[None], out.shape)


def final_kernel(lengths, got, conv, gain, bias, out):
    slab = my_slab()
    total = jnp.sum(got[...], axis=0)
    spread = group_matrix(False)
    for f in range(2):
        flags = member_of(lengths, slab * 2 + f)
        sums = jnp.zeros((1, 128), F32)
        squares = jnp.zeros((1, 128), F32)
        frames = jnp.float32(0)
        for k in range(4):
            sums = sums + total[k:k + 1] * flags[k]
            squares = squares + total[4 + k:5 + k] * flags[k]
            frames = frames + flags[k] * lengths[k].astype(F32)
        entries = jnp.full((1, 128), frames * float(OUT_ROWS * 64 * GROUP_SIZE), F32)
        mean = sums / entries
        var = squares / entries - mean * mean
        scale = lax.rsqrt(var + EPSILON)
        both = jnp.concatenate([mean, scale] * 4, axis=0)
        wide = jnp.dot(both, spread, precision=HIGHEST, preferred_element_type=F32)
        part = conv[f * 64:(f + 1) * 64]
        v = ((part - wide[0:1]) * wide[1:2]) * gain[...] + bias[...]
        out[f] = (v / (1.0 + jnp.exp(-v))).astype(BF)


def shuffle(x, axis):
    return lax.all_to_all(x, axis, split_axis=0, concat_axis=0, tiled=True)


def gathered_weights(kernel):
    ring = [(c * NY + y, c * NY + (y + (1 if c == 0 else NY - 1)) % NY)
            for c in range(2) for y in range(NY)]
    swap = [(0, 1), (1, 0)]
    moved = [kernel]
    for _ in range(4):
        moved.append(lax.ppermute(moved[-1], ("co", "y"), ring))
    swapped = [lax.ppermute(shard, "co", swap) for shard in moved[1:4]]
    return moved, swapped


def convolve(lengths, frames, weights):
    return pl.pallas_call(
        conv_kernel,
        out_shape=[jax.ShapeDtypeStruct((128, COUT), F32)] * 2,
        in_specs=[SMEM] + [VMEM] * (1 + NY),
        out_specs=[VMEM, VMEM],
        scratch_shapes=[pltpu.VMEM((3, 128, 768), BF)],
        compiler_params=params(24),
    )(lengths, frames, *weights)


def body(arrived, row_target, clip_lengths, conv_weight, gn_gain, gn_bias):
    moved, swapped = gathered_weights(conv_weight.reshape(27, CH_DEV, COUT))
    send = pl.pallas_call(
        pack_kernel,
        out_shape=jax.ShapeDtypeStruct((SLABS, 144, 128), BF),
        in_specs=[SMEM, HBM],
        out_specs=HBM,
        scratch_shapes=[
            pltpu.SMEM((SLABS,), jnp.int32),
            pltpu.VMEM((SLABS, 16, 128), F32),
            pltpu.VMEM((SLABS, 16, 128), BF),
            pltpu.SemaphoreType.DMA((2,)),
        ],
        compiler_params=params(8),
    )(row_target, arrived)
    got = shuffle(send, TM)
    got, moved[3], swapped[0], swapped[1] = lax.optimization_barrier(
        (got, moved[3], swapped[0], swapped[1])
    )
    far, near = pl.pallas_call(
        place_kernel,
        out_shape=[jax.ShapeDtypeStruct((NY * 6, CH_DEV, 128), BF)] * 2,
        in_specs=[VMEM],
        out_specs=[HBM, HBM],
        scratch_shapes=[
            pltpu.VMEM((97, CH_DEV, 128), BF),
            pltpu.VMEM((16, 128), jnp.int32),
            pltpu.SMEM((16, 128), jnp.int32),
            pltpu.SemaphoreType.DMA((2,)),
        ],
        compiler_params=params(8),
    )(got)
    weights = [moved[0], moved[1], swapped[0], moved[2], swapped[1], moved[3], swapped[2], moved[4]]
    onward = [(i, i + 1) for i in range(SLABS - 1)]
    far = shuffle(far.reshape(NY, 6, CH_DEV, 128), "y")
    near = shuffle(near.reshape(NY, 6, CH_DEV, 128), "y")
    far, far_after = convolve(clip_lengths, far, weights)
    far_before = lax.ppermute(far_after, TM, onward)
    near, near_after = convolve(clip_lengths, near, weights)
    near_before = lax.ppermute(near_after, TM, onward)
    far = lax.ppermute(far + far_before, "zh", [(0, 1), (1, 0)])
    near = near + far
    conv, stats = pl.pallas_call(
        stat_kernel,
        out_shape=[jax.ShapeDtypeStruct((128, COUT), F32), jax.ShapeDtypeStruct((16, 8, 128), F32)],
        in_specs=[SMEM, VMEM, VMEM],
        out_specs=[VMEM, VMEM],
        compiler_params=params(16),
    )(clip_lengths, near, near_before)
    stats = shuffle(stats, ("y", "co"))
    stats = pl.pallas_call(
        middle_kernel,
        out_shape=jax.ShapeDtypeStruct((SLABS, 8, 128), F32),
        in_specs=[VMEM],
        out_specs=VMEM,
    )(stats)
    stats = shuffle(stats, ("zl", "zh", "x"))
    out = pl.pallas_call(
        final_kernel,
        out_shape=jax.ShapeDtypeStruct((2, 64, COUT), BF),
        in_specs=[SMEM, VMEM, VMEM, VMEM, VMEM],
        out_specs=VMEM,
        compiler_params=params(16),
    )(clip_lengths, stats, conv, gn_gain.reshape(1, COUT), gn_bias.reshape(1, COUT))
    return out.reshape(1, 2, 64, COUT)


def solution(mesh):
    fine = Mesh(mesh.devices.reshape(4, 4, 2, 2, 8), TM + CH)
    in_specs = (P(TM, CH, None), P(TM), P(), P(None, None, None, CH, None), P(), P())
    out_specs = P(CH, TM, None, None)
    return jax.shard_map(body, mesh=fine, in_specs=in_specs, out_specs=out_specs, check_vma=False)
```

```python
import functools

import jax
import jax.numpy as jnp
from jax import lax
from jax.experimental import pallas as pl
from jax.experimental.pallas import tpu as pltpu
from jax.sharding import Mesh, PartitionSpec as P

TM = ("zl", "x", "co")
CH = ("zh", "y")
SLABS = 32
ROWS = 64
CAP = 4
CH_DEV = 32
HALF = 16
NY = 8
OUT_ROWS = 16
COUT = 512
GROUPS = 32
GROUP_SIZE = 16
EPSILON = 1e-05
BF = jnp.bfloat16
F32 = jnp.float32
HIGHEST = lax.Precision.HIGHEST

VMEM = pl.BlockSpec(memory_space=pltpu.VMEM)
SMEM = pl.BlockSpec(memory_space=pltpu.SMEM)
HBM = pl.BlockSpec(memory_space=pltpu.HBM)


def params(mib):
    return pltpu.CompilerParams(vmem_limit_bytes=mib * 1024 * 1024)


def pack_kernel(target, arrived, send, counts, places, rounded, sems):
    places[...] = jnp.full(places.shape, float(ROWS), F32)

    def clear(i, carry):
        counts[i] = 0
        return carry

    lax.fori_loop(0, SLABS, clear, 0)

    def one(i, carry):
        t = target[i]
        owner = lax.shift_right_logical(t, 6)
        rank = counts[owner]
        counts[owner] = rank + 1
        slot = pl.ds(pl.multiple_of(rank * CH_DEV, CH_DEV), CH_DEV)
        pltpu.make_async_copy(arrived.at[i], send.at[owner, slot], sems.at[0]).start()
        place = lax.bitwise_and(t, ROWS - 1).astype(F32)
        places[owner, pl.ds(rank, 1), :] = jnp.full((1, 128), place, F32)
        return carry

    lax.fori_loop(0, ROWS, one, 0)
    rounded[...] = places[...].astype(BF)
    listed = pltpu.make_async_copy(rounded, send.at[:, pl.ds(CAP * CH_DEV, 16)], sems.at[1])
    listed.start()
    pltpu.make_async_copy(arrived, arrived, sems.at[0]).wait()
    listed.wait()


def my_slab():
    return (lax.axis_index("zl") * 4 + lax.axis_index("x")) * 2 + lax.axis_index("co")


def spot(zh, i, f, b):
    near = 1 - lax.bitwise_xor(lax.shift_right_logical(i, 3), zh)
    return near * 48 + lax.bitwise_and(i, NY - 1) * 6 + f * 3 + b


def place_kernel(got, far, near, both, table, moves, sems):
    zh = lax.axis_index("zh")
    lane = lax.broadcasted_iota(jnp.int32, (16, 128), 1)
    place = jnp.full((16, 128), float(ROWS), F32)
    for s in range(SLABS):
        place = jnp.where(lane == s, got[s, CAP * CH_DEV:, :].astype(F32), place)
    place = place.astype(jnp.int32)
    f = lax.shift_right_logical(place, 5)
    h = lax.bitwise_and(place, 31)
    odd = lax.bitwise_and(h, 1)
    i = lax.shift_right_logical(h, 1)
    first = spot(zh, i, f, 1 + odd)
    second = jnp.where((odd == 1) & (i < OUT_ROWS - 1), spot(zh, i + 1, f, 0), first)
    table[...] = jnp.where(place < ROWS, first * 128 + second, 96 * 128 + 96)
    copy = pltpu.make_async_copy(table, moves, sems.at[0])
    copy.start()
    for f in range(2):
        both[spot(zh, jnp.int32(0), f, 0)] = jnp.zeros((CH_DEV, 128), BF)
    copy.wait()

    def some(s, carry):
        for source in (2 * s, 2 * s + 1):
            for r in range(CAP):
                move = moves[r, source]
                row = got[source, r * CH_DEV:(r + 1) * CH_DEV, :]
                both[lax.shift_right_logical(move, 7)] = row
                both[lax.bitwise_and(move, 127)] = row
        return carry

    lax.fori_loop(0, SLABS // 2, some, 0)
    copies = [
        pltpu.make_async_copy(both.at[pl.ds(48 * k, 48)], out, sems.at[k])
        for k, out in enumerate((far, near))
    ]
    for copy in copies:
        copy.start()
    for copy in copies:
        copy.wait()


def clip_start_of(lengths, frame):
    first = jnp.int32(0)
    end = jnp.int32(0)
    for k in range(4):
        start = end
        end = end + lengths[k]
        first = jnp.where((frame >= start) & (frame < end), start, first)
    return first


def conv_kernel(lengths, frames, *rest):
    weights, (own, after, taps) = rest[:NY + 1], rest[NY + 1:]
    y = lax.axis_index("y")
    core = lax.axis_index("co")
    slab = my_slab()
    sign = 2 * core - 1
    sources = [y]
    for s in range(1, 4):
        sources += [y + sign * s, y - sign * s]
    sources += [y + 4, y + 4]
    sources = [lax.bitwise_and(s + NY, NY - 1) for s in sources]
    whole = pl.ds(0, CH_DEV)
    mine = pl.ds(pl.multiple_of(core * HALF, HALF), HALF)
    other = pl.ds(pl.multiple_of((1 - core) * HALF, HALF), HALF)
    sources = list(zip(sources, [whole] * 7 + [mine, other]))
    j = lax.broadcasted_iota(jnp.int32, (192, 128), 0)
    w = lax.broadcasted_iota(jnp.int32, (192, 128), 1)
    wanted = jnp.where(j < 64, 2 * j - 1, jnp.where(j < 128, 2 * j - 128, 2 * j - 255))
    pick = (w == wanted).astype(F32).astype(BF)
    for t in range(2):
        for b in range(3):
            x = jnp.concatenate([frames[s, t * 3 + b, c] for s, c in sources], axis=0)
            picked = lax.dot_general(pick, x, (((1,), (1,)), ((), ())),
                                     preferred_element_type=F32).astype(BF)
            for e in range(3):
                taps[b, t * 64:(t + 1) * 64, e * 256:(e + 1) * 256] = picked[e * 64:(e + 1) * 64]
    own[...] = jnp.zeros(own.shape, F32)
    after[...] = jnp.zeros(after.shape, F32)

    def gates(a):
        parts = []
        for t in range(2):
            frame = slab * 2 + t
            allowed = frame >= clip_start_of(lengths, frame + 2 - a)
            parts.append(jnp.full((64, 768), jnp.where(allowed, 1.0, 0.0), F32).astype(BF))
        return jnp.concatenate(parts, axis=0)

    def row_tap(b, carry):
        lhs = taps[b]
        for a in range(3):
            tap = (a * 3 + b) * 3
            kernel = jnp.concatenate([ref[tap + e] for e in range(3) for ref in weights], axis=0)
            part = jnp.dot(lhs * gates(a), kernel, preferred_element_type=F32)
            if a == 0:
                after[...] += part
            elif a == 1:
                own[64:] += part[:64]
                after[:64] += part[64:]
            else:
                own[...] += part
        return carry

    lax.fori_loop(0, 3, row_tap, 0)


def group_matrix(channels_first):
    shape = (COUT, 128) if channels_first else (128, COUT)
    c = lax.broadcasted_iota(jnp.int32, shape, 0 if channels_first else 1)
    g = lax.broadcasted_iota(jnp.int32, shape, 1 if channels_first else 0)
    return (lax.shift_right_logical(c, 4) == g).astype(F32)


def member_of(lengths, frame):
    end = jnp.int32(0)
    flags = []
    for k in range(4):
        start = end
        end = end + lengths[k]
        flags.append(jnp.where((frame >= start) & (frame < end), 1.0, 0.0).astype(F32))
    return flags


def stat_kernel(lengths, near, before, conv_out, stats):
    slab = my_slab()
    conv = near[...] + before[...]
    conv_out[...] = conv
    rows = []
    for f in range(2):
        part = conv[f * 64:(f + 1) * 64]
        rows.append(jnp.sum(part, axis=0, keepdims=True))
        rows.append(jnp.sum(part * part, axis=0, keepdims=True))
    rows = jnp.concatenate(rows + rows, axis=0)
    grouped = jnp.dot(rows, group_matrix(True), precision=HIGHEST, preferred_element_type=F32)
    m0 = member_of(lengths, slab * 2)
    m1 = member_of(lengths, slab * 2 + 1)
    sums = [grouped[0:1] * m0[k] + grouped[2:3] * m1[k] for k in range(4)]
    squares = [grouped[1:2] * m0[k] + grouped[3:4] * m1[k] for k in range(4)]
    tile = jnp.concatenate(sums + squares, axis=0)
    stats[...] = jnp.broadcast_to(tile[None], stats.shape)


def middle_kernel(got, out):
    out[...] = jnp.broadcast_to(jnp.sum(got[...], axis=0)[None], out.shape)


def final_kernel(lengths, got, conv, gain, bias, out):
    slab = my_slab()
    total = jnp.sum(got[...], axis=0)
    spread = group_matrix(False)
    for f in range(2):
        flags = member_of(lengths, slab * 2 + f)
        sums = jnp.zeros((1, 128), F32)
        squares = jnp.zeros((1, 128), F32)
        frames = jnp.float32(0)
        for k in range(4):
            sums = sums + total[k:k + 1] * flags[k]
            squares = squares + total[4 + k:5 + k] * flags[k]
            frames = frames + flags[k] * lengths[k].astype(F32)
        entries = jnp.full((1, 128), frames * float(OUT_ROWS * 64 * GROUP_SIZE), F32)
        mean = sums / entries
        var = squares / entries - mean * mean
        scale = lax.rsqrt(var + EPSILON)
        both = jnp.concatenate([mean, scale] * 4, axis=0)
        wide = jnp.dot(both, spread, precision=HIGHEST, preferred_element_type=F32)
        part = conv[f * 64:(f + 1) * 64]
        v = ((part - wide[0:1]) * wide[1:2]) * gain[...] + bias[...]
        out[f] = (v / (1.0 + jnp.exp(-v))).astype(BF)


def shuffle(x, axis):
    return lax.all_to_all(x, axis, split_axis=0, concat_axis=0, tiled=True)


def gathered_weights(kernel):
    ring = [(c * NY + y, c * NY + (y + (1 if c == 0 else NY - 1)) % NY)
            for c in range(2) for y in range(NY)]
    swap = [(0, 1), (1, 0)]
    moved = [kernel]
    for _ in range(3):
        moved.append(lax.ppermute(moved[-1], ("co", "y"), ring))
    first = lax.axis_index("co") * HALF
    half = lax.dynamic_slice_in_dim(moved[3], first, HALF, axis=1)
    moved.append(lax.ppermute(half, ("co", "y"), ring))
    swapped = [lax.ppermute(shard, "co", swap) for shard in moved[1:]]
    return moved, swapped


def convolve(lengths, frames, weights):
    return pl.pallas_call(
        conv_kernel,
        out_shape=[jax.ShapeDtypeStruct((128, COUT), F32)] * 2,
        in_specs=[SMEM] + [VMEM] * (2 + NY),
        out_specs=[VMEM, VMEM],
        scratch_shapes=[pltpu.VMEM((3, 128, 768), BF)],
        compiler_params=params(24),
    )(lengths, frames, *weights)


def body(arrived, row_target, clip_lengths, conv_weight, gn_gain, gn_bias):
    moved, swapped = gathered_weights(conv_weight.reshape(27, CH_DEV, COUT))
    send = pl.pallas_call(
        pack_kernel,
        out_shape=jax.ShapeDtypeStruct((SLABS, 144, 128), BF),
        in_specs=[SMEM, HBM],
        out_specs=HBM,
        scratch_shapes=[
            pltpu.SMEM((SLABS,), jnp.int32),
            pltpu.VMEM((SLABS, 16, 128), F32),
            pltpu.VMEM((SLABS, 16, 128), BF),
            pltpu.SemaphoreType.DMA((2,)),
        ],
        compiler_params=params(8),
    )(row_target, arrived)
    got = shuffle(send, TM)
    got, moved[2], swapped[0] = lax.optimization_barrier((got, moved[2], swapped[0]))
    far, near = pl.pallas_call(
        place_kernel,
        out_shape=[jax.ShapeDtypeStruct((NY * 6, CH_DEV, 128), BF)] * 2,
        in_specs=[VMEM],
        out_specs=[HBM, HBM],
        scratch_shapes=[
            pltpu.VMEM((97, CH_DEV, 128), BF),
            pltpu.VMEM((16, 128), jnp.int32),
            pltpu.SMEM((16, 128), jnp.int32),
            pltpu.SemaphoreType.DMA((2,)),
        ],
        compiler_params=params(8),
    )(got)
    weights = [moved[0], moved[1], swapped[0], moved[2], swapped[1], moved[3], swapped[2]]
    weights += [moved[4], swapped[3]]
    onward = [(i, i + 1) for i in range(SLABS - 1)]
    far = shuffle(far.reshape(NY, 6, CH_DEV, 128), "y")
    near = shuffle(near.reshape(NY, 6, CH_DEV, 128), "y")
    far, far_after = convolve(clip_lengths, far, weights)
    far_before = lax.ppermute(far_after, TM, onward)
    near, near_after = convolve(clip_lengths, near, weights)
    near_before = lax.ppermute(near_after, TM, onward)
    far = lax.ppermute(far + far_before, "zh", [(0, 1), (1, 0)])
    near = near + far
    conv, stats = pl.pallas_call(
        stat_kernel,
        out_shape=[jax.ShapeDtypeStruct((128, COUT), F32), jax.ShapeDtypeStruct((16, 8, 128), F32)],
        in_specs=[SMEM, VMEM, VMEM],
        out_specs=[VMEM, VMEM],
        compiler_params=params(16),
    )(clip_lengths, near, near_before)
    stats = shuffle(stats, ("y", "co"))
    stats = pl.pallas_call(
        middle_kernel,
        out_shape=jax.ShapeDtypeStruct((SLABS, 8, 128), F32),
        in_specs=[VMEM],
        out_specs=VMEM,
    )(stats)
    stats = shuffle(stats, ("zl", "zh", "x"))
    out = pl.pallas_call(
        final_kernel,
        out_shape=jax.ShapeDtypeStruct((2, 64, COUT), BF),
        in_specs=[SMEM, VMEM, VMEM, VMEM, VMEM],
        out_specs=VMEM,
        compiler_params=params(16),
    )(clip_lengths, stats, conv, gn_gain.reshape(1, COUT), gn_bias.reshape(1, COUT))
    return out.reshape(1, 2, 64, COUT)


def solution(mesh):
    fine = Mesh(mesh.devices.reshape(4, 4, 2, 2, 8), TM + CH)
    in_specs = (P(TM, CH, None), P(TM), P(), P(None, None, None, CH, None), P(), P())
    out_specs = P(CH, TM, None, None)
    return jax.shard_map(body, mesh=fine, in_specs=in_specs, out_specs=out_specs, check_vma=False)
```

```python
import functools

import jax
import jax.numpy as jnp
from jax import lax
from jax.experimental import pallas as pl
from jax.experimental.pallas import tpu as pltpu
from jax.sharding import Mesh, PartitionSpec as P

TM = ("zl", "x", "co")
CH = ("zh", "y")
SLABS = 32
ROWS = 64
CAP = 4
CH_DEV = 32
HALF = 16
NY = 8
OUT_ROWS = 16
COUT = 512
GROUPS = 32
GROUP_SIZE = 16
EPSILON = 1e-05
BF = jnp.bfloat16
F32 = jnp.float32
HIGHEST = lax.Precision.HIGHEST

VMEM = pl.BlockSpec(memory_space=pltpu.VMEM)
SMEM = pl.BlockSpec(memory_space=pltpu.SMEM)
HBM = pl.BlockSpec(memory_space=pltpu.HBM)


def params(mib):
    return pltpu.CompilerParams(vmem_limit_bytes=mib * 1024 * 1024)


def pack_kernel(target, arrived, send, rows, counts, places, rounded, sems):
    fetch = pltpu.make_async_copy(arrived, rows, sems.at[0])
    fetch.start()
    places[...] = jnp.full(places.shape, float(ROWS), F32)

    def clear(i, carry):
        counts[i] = 0
        return carry

    lax.fori_loop(0, SLABS, clear, 0)
    fetch.wait()

    def one(i, carry):
        t = target[i]
        owner = lax.shift_right_logical(t, 6)
        rank = counts[owner]
        counts[owner] = rank + 1
        slot = pl.ds(pl.multiple_of(rank * CH_DEV, CH_DEV), CH_DEV)
        pltpu.make_async_copy(rows.at[i], send.at[owner, slot], sems.at[0]).start()
        place = lax.bitwise_and(t, ROWS - 1).astype(F32)
        places[owner, pl.ds(rank, 1), :] = jnp.full((1, 128), place, F32)
        return carry

    lax.fori_loop(0, ROWS, one, 0)
    rounded[...] = places[...].astype(BF)
    listed = pltpu.make_async_copy(rounded, send.at[:, pl.ds(CAP * CH_DEV, 16)], sems.at[1])
    listed.start()
    pltpu.make_async_copy(rows, rows, sems.at[0]).wait()
    listed.wait()


def my_slab():
    return (lax.axis_index("zl") * 4 + lax.axis_index("x")) * 2 + lax.axis_index("co")


def spot(zh, i, f, b):
    near = 1 - lax.bitwise_xor(lax.shift_right_logical(i, 3), zh)
    return near * 48 + lax.bitwise_and(i, NY - 1) * 6 + f * 3 + b


def place_kernel(arrived, far, near, got, both, table, moves, sems):
    fetches = [
        pltpu.make_async_copy(arrived.at[:, part], got.at[:, part], sems.at[k])
        for k, part in enumerate((pl.ds(CAP * CH_DEV, 16), pl.ds(0, CAP * CH_DEV)))
    ]
    for fetch in fetches:
        fetch.start()
    zh = lax.axis_index("zh")
    fetches[0].wait()
    lane = lax.broadcasted_iota(jnp.int32, (16, 128), 1)
    place = jnp.full((16, 128), float(ROWS), F32)
    for s in range(SLABS):
        place = jnp.where(lane == s, got[s, CAP * CH_DEV:, :].astype(F32), place)
    place = place.astype(jnp.int32)
    f = lax.shift_right_logical(place, 5)
    h = lax.bitwise_and(place, 31)
    odd = lax.bitwise_and(h, 1)
    i = lax.shift_right_logical(h, 1)
    first = spot(zh, i, f, 1 + odd)
    second = jnp.where((odd == 1) & (i < OUT_ROWS - 1), spot(zh, i + 1, f, 0), first)
    table[...] = jnp.where(place < ROWS, first * 128 + second, 96 * 128 + 96)
    copy = pltpu.make_async_copy(table, moves, sems.at[0])
    copy.start()
    for f in range(2):
        both[spot(zh, jnp.int32(0), f, 0)] = jnp.zeros((CH_DEV, 128), BF)
    copy.wait()
    fetches[1].wait()

    def some(s, carry):
        for source in (2 * s, 2 * s + 1):
            for r in range(CAP):
                move = moves[r, source]
                row = got[source, r * CH_DEV:(r + 1) * CH_DEV, :]
                both[lax.shift_right_logical(move, 7)] = row
                both[lax.bitwise_and(move, 127)] = row
        return carry

    lax.fori_loop(0, SLABS // 2, some, 0)
    copies = [
        pltpu.make_async_copy(both.at[pl.ds(48 * k, 48)], out, sems.at[k])
        for k, out in enumerate((far, near))
    ]
    for copy in copies:
        copy.start()
    for copy in copies:
        copy.wait()


def clip_start_of(lengths, frame):
    first = jnp.int32(0)
    end = jnp.int32(0)
    for k in range(4):
        start = end
        end = end + lengths[k]
        first = jnp.where((frame >= start) & (frame < end), start, first)
    return first


def conv_kernel(lengths, frames, *rest):
    weights, (own, after, taps) = rest[:NY + 1], rest[NY + 1:]
    y = lax.axis_index("y")
    core = lax.axis_index("co")
    slab = my_slab()
    sign = 2 * core - 1
    sources = [y]
    for s in range(1, 4):
        sources += [y + sign * s, y - sign * s]
    sources += [y + 4, y + 4]
    sources = [lax.bitwise_and(s + NY, NY - 1) for s in sources]
    whole = pl.ds(0, CH_DEV)
    mine = pl.ds(pl.multiple_of(core * HALF, HALF), HALF)
    other = pl.ds(pl.multiple_of((1 - core) * HALF, HALF), HALF)
    sources = list(zip(sources, [whole] * 7 + [mine, other]))
    j = lax.broadcasted_iota(jnp.int32, (192, 128), 0)
    w = lax.broadcasted_iota(jnp.int32, (192, 128), 1)
    wanted = jnp.where(j < 64, 2 * j - 1, jnp.where(j < 128, 2 * j - 128, 2 * j - 255))
    pick = (w == wanted).astype(F32).astype(BF)
    for t in range(2):
        for b in range(3):
            x = jnp.concatenate([frames[s, t * 3 + b, c] for s, c in sources], axis=0)
            picked = lax.dot_general(pick, x, (((1,), (1,)), ((), ())),
                                     preferred_element_type=F32).astype(BF)
            for e in range(3):
                taps[b, t * 64:(t + 1) * 64, e * 256:(e + 1) * 256] = picked[e * 64:(e + 1) * 64]
    own[...] = jnp.zeros(own.shape, F32)
    after[...] = jnp.zeros(after.shape, F32)

    def gates(a):
        parts = []
        for t in range(2):
            frame = slab * 2 + t
            allowed = frame >= clip_start_of(lengths, frame + 2 - a)
            parts.append(jnp.full((64, 768), jnp.where(allowed, 1.0, 0.0), F32).astype(BF))
        return jnp.concatenate(parts, axis=0)

    def row_tap(b, carry):
        lhs = taps[b]
        for a in range(3):
            tap = (a * 3 + b) * 3
            kernel = jnp.concatenate([ref[tap + e] for e in range(3) for ref in weights], axis=0)
            part = jnp.dot(lhs * gates(a), kernel, preferred_element_type=F32)
            if a == 0:
                after[...] += part
            elif a == 1:
                own[64:] += part[:64]
                after[:64] += part[64:]
            else:
                own[...] += part
        return carry

    lax.fori_loop(0, 3, row_tap, 0)


def group_matrix(channels_first):
    shape = (COUT, 128) if channels_first else (128, COUT)
    c = lax.broadcasted_iota(jnp.int32, shape, 0 if channels_first else 1)
    g = lax.broadcasted_iota(jnp.int32, shape, 1 if channels_first else 0)
    return (lax.shift_right_logical(c, 4) == g).astype(F32)


def member_of(lengths, frame):
    end = jnp.int32(0)
    flags = []
    for k in range(4):
        start = end
        end = end + lengths[k]
        flags.append(jnp.where((frame >= start) & (frame < end), 1.0, 0.0).astype(F32))
    return flags


def stat_kernel(lengths, near, before, conv_out, stats):
    slab = my_slab()
    conv = near[...] + before[...]
    conv_out[...] = conv
    rows = []
    for f in range(2):
        part = conv[f * 64:(f + 1) * 64]
        rows.append(jnp.sum(part, axis=0, keepdims=True))
        rows.append(jnp.sum(part * part, axis=0, keepdims=True))
    rows = jnp.concatenate(rows + rows, axis=0)
    grouped = jnp.dot(rows, group_matrix(True), precision=HIGHEST, preferred_element_type=F32)
    m0 = member_of(lengths, slab * 2)
    m1 = member_of(lengths, slab * 2 + 1)
    sums = [grouped[0:1] * m0[k] + grouped[2:3] * m1[k] for k in range(4)]
    squares = [grouped[1:2] * m0[k] + grouped[3:4] * m1[k] for k in range(4)]
    tile = jnp.concatenate(sums + squares, axis=0)
    stats[...] = jnp.broadcast_to(tile[None], stats.shape)


def middle_kernel(got, out):
    out[...] = jnp.broadcast_to(jnp.sum(got[...], axis=0)[None], out.shape)


def final_kernel(lengths, got, conv, gain, bias, out):
    slab = my_slab()
    total = jnp.sum(got[...], axis=0)
    spread = group_matrix(False)
    for f in range(2):
        flags = member_of(lengths, slab * 2 + f)
        sums = jnp.zeros((1, 128), F32)
        squares = jnp.zeros((1, 128), F32)
        frames = jnp.float32(0)
        for k in range(4):
            sums = sums + total[k:k + 1] * flags[k]
            squares = squares + total[4 + k:5 + k] * flags[k]
            frames = frames + flags[k] * lengths[k].astype(F32)
        entries = jnp.full((1, 128), frames * float(OUT_ROWS * 64 * GROUP_SIZE), F32)
        mean = sums / entries
        var = squares / entries - mean * mean
        scale = lax.rsqrt(var + EPSILON)
        both = jnp.concatenate([mean, scale] * 4, axis=0)
        wide = jnp.dot(both, spread, precision=HIGHEST, preferred_element_type=F32)
        part = conv[f * 64:(f + 1) * 64]
        v = ((part - wide[0:1]) * wide[1:2]) * gain[...] + bias[...]
        out[f] = (v / (1.0 + jnp.exp(-v))).astype(BF)


def shuffle(x, axis):
    return lax.all_to_all(x, axis, split_axis=0, concat_axis=0, tiled=True)


def gathered_weights(kernel):
    ring = [(c * NY + y, c * NY + (y + (1 if c == 0 else NY - 1)) % NY)
            for c in range(2) for y in range(NY)]
    swap = [(0, 1), (1, 0)]
    moved = [kernel]
    for _ in range(3):
        moved.append(lax.ppermute(moved[-1], ("co", "y"), ring))
    first = lax.axis_index("co") * HALF
    half = lax.dynamic_slice_in_dim(moved[3], first, HALF, axis=1)
    moved.append(lax.ppermute(half, ("co", "y"), ring))
    swapped = [lax.ppermute(shard, "co", swap) for shard in moved[1:]]
    return moved, swapped


def convolve(lengths, frames, weights):
    return pl.pallas_call(
        conv_kernel,
        out_shape=[jax.ShapeDtypeStruct((128, COUT), F32)] * 2,
        in_specs=[SMEM] + [VMEM] * (2 + NY),
        out_specs=[VMEM, VMEM],
        scratch_shapes=[pltpu.VMEM((3, 128, 768), BF)],
        compiler_params=params(24),
    )(lengths, frames, *weights)


def body(arrived, row_target, clip_lengths, conv_weight, gn_gain, gn_bias):
    moved, swapped = gathered_weights(conv_weight.reshape(27, CH_DEV, COUT))
    send = pl.pallas_call(
        pack_kernel,
        out_shape=jax.ShapeDtypeStruct((SLABS, 144, 128), BF),
        in_specs=[SMEM, HBM],
        out_specs=HBM,
        scratch_shapes=[
            pltpu.VMEM((ROWS, CH_DEV, 128), BF),
            pltpu.SMEM((SLABS,), jnp.int32),
            pltpu.VMEM((SLABS, 16, 128), F32),
            pltpu.VMEM((SLABS, 16, 128), BF),
            pltpu.SemaphoreType.DMA((2,)),
        ],
        compiler_params=params(60),
    )(row_target, arrived)
    got = shuffle(send, TM)
    got, moved[2], swapped[0], swapped[1] = lax.optimization_barrier(
        (got, moved[2], swapped[0], swapped[1])
    )
    far, near = pl.pallas_call(
        place_kernel,
        out_shape=[jax.ShapeDtypeStruct((NY * 6, CH_DEV, 128), BF)] * 2,
        in_specs=[HBM],
        out_specs=[HBM, HBM],
        scratch_shapes=[
            pltpu.VMEM((SLABS, 144, 128), BF),
            pltpu.VMEM((97, CH_DEV, 128), BF),
            pltpu.VMEM((16, 128), jnp.int32),
            pltpu.SMEM((16, 128), jnp.int32),
            pltpu.SemaphoreType.DMA((2,)),
        ],
        compiler_params=params(60),
    )(got)
    weights = [moved[0], moved[1], swapped[0], moved[2], swapped[1], moved[3], swapped[2]]
    weights += [moved[4], swapped[3]]
    onward = [(i, i + 1) for i in range(SLABS - 1)]
    far = shuffle(far.reshape(NY, 6, CH_DEV, 128), "y")
    near, weights[-1] = lax.optimization_barrier((near, weights[-1]))
    near = shuffle(near.reshape(NY, 6, CH_DEV, 128), "y")
    far, far_after = convolve(clip_lengths, far, weights)
    far_before = lax.ppermute(far_after, TM, onward)
    near, near_after = convolve(clip_lengths, near, weights)
    near_before = lax.ppermute(near_after, TM, onward)
    far = lax.ppermute(far + far_before, "zh", [(0, 1), (1, 0)])
    near = near + far
    conv, stats = pl.pallas_call(
        stat_kernel,
        out_shape=[jax.ShapeDtypeStruct((128, COUT), F32), jax.ShapeDtypeStruct((16, 8, 128), F32)],
        in_specs=[SMEM, VMEM, VMEM],
        out_specs=[VMEM, VMEM],
        compiler_params=params(16),
    )(clip_lengths, near, near_before)
    stats = shuffle(stats, ("y", "co"))
    stats = pl.pallas_call(
        middle_kernel,
        out_shape=jax.ShapeDtypeStruct((SLABS, 8, 128), F32),
        in_specs=[VMEM],
        out_specs=VMEM,
    )(stats)
    stats = shuffle(stats, ("zl", "zh", "x"))
    out = pl.pallas_call(
        final_kernel,
        out_shape=jax.ShapeDtypeStruct((2, 64, COUT), BF),
        in_specs=[SMEM, VMEM, VMEM, VMEM, VMEM],
        out_specs=VMEM,
        compiler_params=params(16),
    )(clip_lengths, stats, conv, gn_gain.reshape(1, COUT), gn_bias.reshape(1, COUT))
    return out.reshape(1, 2, 64, COUT)


def solution(mesh):
    fine = Mesh(mesh.devices.reshape(4, 4, 2, 2, 8), TM + CH)
    in_specs = (P(TM, CH, None), P(TM), P(), P(None, None, None, CH, None), P(), P())
    out_specs = P(CH, TM, None, None)
    return jax.shard_map(body, mesh=fine, in_specs=in_specs, out_specs=out_specs, check_vma=False)
```

```python
import functools

import jax
import jax.numpy as jnp
from jax import lax
from jax.experimental import pallas as pl
from jax.experimental.pallas import tpu as pltpu
from jax.sharding import Mesh, PartitionSpec as P

TM = ("zl", "x", "co")
CH = ("zh", "y")
SLABS = 32
ROWS = 64
CAP = 4
CH_DEV = 32
HALF = 16
NY = 8
OUT_ROWS = 16
COUT = 512
GROUPS = 32
GROUP_SIZE = 16
DEVICES = 512
EPSILON = 1e-05
BF = jnp.bfloat16
F32 = jnp.float32
HIGHEST = lax.Precision.HIGHEST

VMEM = pl.BlockSpec(memory_space=pltpu.VMEM)
SMEM = pl.BlockSpec(memory_space=pltpu.SMEM)
HBM = pl.BlockSpec(memory_space=pltpu.HBM)


def params(mib):
    return pltpu.CompilerParams(vmem_limit_bytes=mib * 1024 * 1024)


def pack_kernel(target, arrived, send, rows, counts, places, rounded, sems):
    fetch = pltpu.make_async_copy(arrived, rows, sems.at[0])
    fetch.start()
    places[...] = jnp.full(places.shape, float(ROWS), F32)

    def clear(i, carry):
        counts[i] = 0
        return carry

    lax.fori_loop(0, SLABS, clear, 0)
    fetch.wait()

    def one(i, carry):
        t = target[i]
        owner = lax.shift_right_logical(t, 6)
        rank = counts[owner]
        counts[owner] = rank + 1
        slot = pl.ds(pl.multiple_of(rank * CH_DEV, CH_DEV), CH_DEV)
        pltpu.make_async_copy(rows.at[i], send.at[owner, slot], sems.at[0]).start()
        place = lax.bitwise_and(t, ROWS - 1).astype(F32)
        places[owner, pl.ds(rank, 1), :] = jnp.full((1, 128), place, F32)
        return carry

    lax.fori_loop(0, ROWS, one, 0)
    rounded[...] = places[...].astype(BF)
    listed = pltpu.make_async_copy(rounded, send.at[:, pl.ds(CAP * CH_DEV, 16)], sems.at[1])
    listed.start()
    pltpu.make_async_copy(rows, rows, sems.at[0]).wait()
    listed.wait()


def my_slab():
    return (lax.axis_index("zl") * 4 + lax.axis_index("x")) * 2 + lax.axis_index("co")


def spot(zh, i, f, b):
    near = 1 - lax.bitwise_xor(lax.shift_right_logical(i, 3), zh)
    return near * 48 + lax.bitwise_and(i, NY - 1) * 6 + f * 3 + b


def place_kernel(got, far, near, both, table, moves, sems):
    zh = lax.axis_index("zh")
    lane = lax.broadcasted_iota(jnp.int32, (16, 128), 1)
    place = jnp.full((16, 128), float(ROWS), F32)
    for s in range(SLABS):
        place = jnp.where(lane == s, got[s, CAP * CH_DEV:, :].astype(F32), place)
    place = place.astype(jnp.int32)
    f = lax.shift_right_logical(place, 5)
    h = lax.bitwise_and(place, 31)
    odd = lax.bitwise_and(h, 1)
    i = lax.shift_right_logical(h, 1)
    first = spot(zh, i, f, 1 + odd)
    second = jnp.where((odd == 1) & (i < OUT_ROWS - 1), spot(zh, i + 1, f, 0), first)
    table[...] = jnp.where(place < ROWS, first * 128 + second, 96 * 128 + 96)
    copy = pltpu.make_async_copy(table, moves, sems.at[0])
    copy.start()
    for f in range(2):
        both[spot(zh, jnp.int32(0), f, 0)] = jnp.zeros((CH_DEV, 128), BF)
    copy.wait()

    def some(s, carry):
        for source in (2 * s, 2 * s + 1):
            for r in range(CAP):
                move = moves[r, source]
                row = got[source, r * CH_DEV:(r + 1) * CH_DEV, :]
                both[lax.shift_right_logical(move, 7)] = row
                both[lax.bitwise_and(move, 127)] = row
        return carry

    lax.fori_loop(0, SLABS // 2, some, 0)
    copies = [
        pltpu.make_async_copy(both.at[pl.ds(48 * k, 48)], out, sems.at[k])
        for k, out in enumerate((far, near))
    ]
    for copy in copies:
        copy.start()
    for copy in copies:
        copy.wait()


def clip_start_of(lengths, frame):
    first = jnp.int32(0)
    end = jnp.int32(0)
    for k in range(4):
        start = end
        end = end + lengths[k]
        first = jnp.where((frame >= start) & (frame < end), start, first)
    return first


def conv_kernel(lengths, frames, *rest):
    weights, (own, after, taps) = rest[:NY + 1], rest[NY + 1:]
    y = lax.axis_index("y")
    core = lax.axis_index("co")
    slab = my_slab()
    sign = 2 * core - 1
    sources = [y]
    for s in range(1, 4):
        sources += [y + sign * s, y - sign * s]
    sources += [y + 4, y + 4]
    sources = [lax.bitwise_and(s + NY, NY - 1) for s in sources]
    whole = pl.ds(0, CH_DEV)
    mine = pl.ds(pl.multiple_of(core * HALF, HALF), HALF)
    other = pl.ds(pl.multiple_of((1 - core) * HALF, HALF), HALF)
    sources = list(zip(sources, [whole] * 7 + [mine, other]))
    j = lax.broadcasted_iota(jnp.int32, (192, 128), 0)
    w = lax.broadcasted_iota(jnp.int32, (192, 128), 1)
    wanted = jnp.where(j < 64, 2 * j - 1, jnp.where(j < 128, 2 * j - 128, 2 * j - 255))
    pick = (w == wanted).astype(F32).astype(BF)
    for t in range(2):
        for b in range(3):
            x = jnp.concatenate([frames[s, t * 3 + b, c] for s, c in sources], axis=0)
            picked = lax.dot_general(pick, x, (((1,), (1,)), ((), ())),
                                     preferred_element_type=F32).astype(BF)
            for e in range(3):
                taps[b, t * 64:(t + 1) * 64, e * 256:(e + 1) * 256] = picked[e * 64:(e + 1) * 64]
    own[...] = jnp.zeros(own.shape, F32)
    after[...] = jnp.zeros(after.shape, F32)

    def gates(a):
        parts = []
        for t in range(2):
            frame = slab * 2 + t
            allowed = frame >= clip_start_of(lengths, frame + 2 - a)
            parts.append(jnp.full((64, 768), jnp.where(allowed, 1.0, 0.0), F32).astype(BF))
        return jnp.concatenate(parts, axis=0)

    def row_tap(b, carry):
        lhs = taps[b]
        for a in range(3):
            tap = (a * 3 + b) * 3
            kernel = jnp.concatenate([ref[tap + e] for e in range(3) for ref in weights], axis=0)
            part = jnp.dot(lhs * gates(a), kernel, preferred_element_type=F32)
            if a == 0:
                after[...] += part
            elif a == 1:
                own[64:] += part[:64]
                after[:64] += part[64:]
            else:
                own[...] += part
        return carry

    lax.fori_loop(0, 3, row_tap, 0)


def group_matrix():
    c = lax.broadcasted_iota(jnp.int32, (COUT, 128), 0)
    g = lax.broadcasted_iota(jnp.int32, (COUT, 128), 1)
    return (lax.shift_right_logical(c, 4) == lax.bitwise_and(g, GROUPS - 1)).astype(F32)


def spread_matrix():
    g = lax.broadcasted_iota(jnp.int32, (128, COUT), 0)
    c = lax.broadcasted_iota(jnp.int32, (128, COUT), 1)
    return (lax.shift_right_logical(c, 4) == lax.bitwise_and(g, GROUPS - 1)).astype(F32)


def member_of(lengths, frame):
    end = jnp.int32(0)
    flags = []
    for k in range(4):
        start = end
        end = end + lengths[k]
        flags.append(jnp.where((frame >= start) & (frame < end), 1.0, 0.0).astype(F32))
    return flags


def stat_kernel(lengths, near, before, conv_out, stats):
    slab = my_slab()
    conv = near[...] + before[...]
    conv_out[...] = conv
    rows = []
    for f in range(2):
        part = conv[f * 64:(f + 1) * 64]
        rows.append(jnp.sum(part, axis=0, keepdims=True))
        rows.append(jnp.sum(part * part, axis=0, keepdims=True))
    rows = jnp.concatenate(rows + rows, axis=0)
    grouped = jnp.dot(rows, group_matrix(), precision=HIGHEST, preferred_element_type=F32)
    m0 = member_of(lengths, slab * 2)
    m1 = member_of(lengths, slab * 2 + 1)
    sums = [grouped[0:1] * m0[k] + grouped[2:3] * m1[k] for k in range(4)]
    squares = [grouped[1:2] * m0[k] + grouped[3:4] * m1[k] for k in range(4)]
    lane = lax.broadcasted_iota(jnp.int32, (1, 128), 1)
    clip_of = lax.shift_right_logical(lane, 5)
    halves = []
    for part in (sums, squares):
        row = jnp.zeros((1, 128), F32)
        for k in range(4):
            row = jnp.where(clip_of == k, part[k], row)
        halves.append(row)
    tile = jnp.concatenate(halves, axis=1)
    stats[...] = jnp.broadcast_to(tile[None], stats.shape)


def final_kernel(lengths, got, conv, gain, bias, out):
    slab = my_slab()
    total = jnp.sum(got[...], axis=0)
    spread = spread_matrix()
    lane = lax.broadcasted_iota(jnp.int32, (1, 128), 1)
    clip_of = lax.shift_right_logical(lane, 5)
    for f in range(2):
        flags = member_of(lengths, slab * 2 + f)
        chosen = jnp.zeros((1, 128), F32)
        frames = jnp.float32(0)
        for k in range(4):
            chosen = jnp.where(clip_of == k, jnp.full((1, 128), flags[k], F32), chosen)
            frames = frames + flags[k] * lengths[k].astype(F32)
        entries = jnp.full((1, 128), frames * float(OUT_ROWS * 64 * GROUP_SIZE), F32)
        mean = total[:, :128] * chosen / entries
        var = total[:, 128:] * chosen / entries - mean * mean
        scale = lax.rsqrt(var + EPSILON) * chosen
        both = jnp.concatenate([mean, scale] * 4, axis=0)
        wide = jnp.dot(both, spread, precision=HIGHEST, preferred_element_type=F32)
        part = conv[f * 64:(f + 1) * 64]
        v = ((part - wide[0:1]) * wide[1:2]) * gain[...] + bias[...]
        out[f] = (v / (1.0 + jnp.exp(-v))).astype(BF)


def shuffle(x, axis):
    return lax.all_to_all(x, axis, split_axis=0, concat_axis=0, tiled=True)


def gathered_weights(kernel):
    ring = [(c * NY + y, c * NY + (y + (1 if c == 0 else NY - 1)) % NY)
            for c in range(2) for y in range(NY)]
    swap = [(0, 1), (1, 0)]
    moved = [kernel]
    for _ in range(3):
        moved.append(lax.ppermute(moved[-1], ("co", "y"), ring))
    first = lax.axis_index("co") * HALF
    half = lax.dynamic_slice_in_dim(moved[3], first, HALF, axis=1)
    moved.append(lax.ppermute(half, ("co", "y"), ring))
    swapped = [lax.ppermute(shard, "co", swap) for shard in moved[1:]]
    return moved, swapped


def convolve(lengths, frames, weights):
    return pl.pallas_call(
        conv_kernel,
        out_shape=[jax.ShapeDtypeStruct((128, COUT), F32)] * 2,
        in_specs=[SMEM] + [VMEM] * (2 + NY),
        out_specs=[VMEM, VMEM],
        scratch_shapes=[pltpu.VMEM((3, 128, 768), BF)],
        compiler_params=params(24),
    )(lengths, frames, *weights)


def body(arrived, row_target, clip_lengths, conv_weight, gn_gain, gn_bias):
    moved, swapped = gathered_weights(conv_weight.reshape(27, CH_DEV, COUT))
    send = pl.pallas_call(
        pack_kernel,
        out_shape=jax.ShapeDtypeStruct((SLABS, 144, 128), BF),
        in_specs=[SMEM, HBM],
        out_specs=HBM,
        scratch_shapes=[
            pltpu.VMEM((ROWS, CH_DEV, 128), BF),
            pltpu.SMEM((SLABS,), jnp.int32),
            pltpu.VMEM((SLABS, 16, 128), F32),
            pltpu.VMEM((SLABS, 16, 128), BF),
            pltpu.SemaphoreType.DMA((2,)),
        ],
        compiler_params=params(60),
    )(row_target, arrived)
    got = shuffle(send, TM)
    got, moved[2], swapped[0] = lax.optimization_barrier(
        (got, moved[2], swapped[0])
    )
    far, near = pl.pallas_call(
        place_kernel,
        out_shape=[jax.ShapeDtypeStruct((NY * 6, CH_DEV, 128), BF)] * 2,
        in_specs=[VMEM],
        out_specs=[HBM, HBM],
        scratch_shapes=[
            pltpu.VMEM((97, CH_DEV, 128), BF),
            pltpu.VMEM((16, 128), jnp.int32),
            pltpu.SMEM((16, 128), jnp.int32),
            pltpu.SemaphoreType.DMA((2,)),
        ],
        compiler_params=params(8),
    )(got)
    weights = [moved[0], moved[1], swapped[0], moved[2], swapped[1], moved[3], swapped[2]]
    weights += [moved[4], swapped[3]]
    onward = [(i, i + 1) for i in range(SLABS - 1)]
    far = shuffle(far.reshape(NY, 6, CH_DEV, 128), "y")
    near = shuffle(near.reshape(NY, 6, CH_DEV, 128), "y")
    far, far_after = convolve(clip_lengths, far, weights)
    far_before = lax.ppermute(far_after, TM, onward)
    near, near_after = convolve(clip_lengths, near, weights)
    near_before = lax.ppermute(near_after, TM, onward)
    far = lax.ppermute(far + far_before, "zh", [(0, 1), (1, 0)])
    near = near + far
    conv, stats = pl.pallas_call(
        stat_kernel,
        out_shape=[jax.ShapeDtypeStruct((128, COUT), F32), jax.ShapeDtypeStruct((DEVICES, 1, 256), F32)],
        in_specs=[SMEM, VMEM, VMEM],
        out_specs=[VMEM, VMEM],
        compiler_params=params(16),
    )(clip_lengths, near, near_before)
    stats = shuffle(stats, TM + CH)
    out = pl.pallas_call(
        final_kernel,
        out_shape=jax.ShapeDtypeStruct((2, 64, COUT), BF),
        in_specs=[SMEM, VMEM, VMEM, VMEM, VMEM],
        out_specs=VMEM,
        compiler_params=params(16),
    )(clip_lengths, stats, conv, gn_gain.reshape(1, COUT), gn_bias.reshape(1, COUT))
    return out.reshape(1, 2, 64, COUT)


def solution(mesh):
    fine = Mesh(mesh.devices.reshape(4, 4, 2, 2, 8), TM + CH)
    in_specs = (P(TM, CH, None), P(TM), P(), P(None, None, None, CH, None), P(), P())
    out_specs = P(CH, TM, None, None)
    return jax.shard_map(body, mesh=fine, in_specs=in_specs, out_specs=out_specs, check_vma=False)
```

```python
import functools

import jax
import jax.numpy as jnp
from jax import lax
from jax.experimental import pallas as pl
from jax.experimental.pallas import tpu as pltpu
from jax.sharding import Mesh, PartitionSpec as P

TM = ("zl", "x", "co")
CH = ("zh", "y")
SLABS = 32
ROWS = 64
CAP = 4
CH_DEV = 32
HALF = 16
NY = 8
OUT_ROWS = 16
COUT = 512
GROUPS = 32
GROUP_SIZE = 16
EPSILON = 1e-05
BF = jnp.bfloat16
F32 = jnp.float32
HIGHEST = lax.Precision.HIGHEST

VMEM = pl.BlockSpec(memory_space=pltpu.VMEM)
SMEM = pl.BlockSpec(memory_space=pltpu.SMEM)
HBM = pl.BlockSpec(memory_space=pltpu.HBM)


def params(mib):
    return pltpu.CompilerParams(vmem_limit_bytes=mib * 1024 * 1024)


def pack_kernel(target, arrived, send, rows, counts, places, sem):
    fetch = pltpu.make_async_copy(arrived, rows, sem)
    fetch.start()
    places[...] = jnp.full(places.shape, float(ROWS), F32)

    def clear(i, carry):
        counts[i] = 0
        return carry

    lax.fori_loop(0, SLABS, clear, 0)
    fetch.wait()

    def some(n, carry):
        for k in range(4):
            i = n * 4 + k
            t = target[i]
            owner = lax.shift_right_logical(t, 6)
            rank = counts[owner]
            counts[owner] = rank + 1
            slot = pl.ds(pl.multiple_of(rank * CH_DEV, CH_DEV), CH_DEV)
            send[owner, slot, :] = rows[i]
            place = lax.bitwise_and(t, ROWS - 1).astype(F32)
            places[owner, pl.ds(rank, 1), :] = jnp.full((1, 128), place, F32)
        return carry

    lax.fori_loop(0, ROWS // 4, some, 0)
    send[:, CAP * CH_DEV:, :] = places[...].astype(BF)


def my_slab():
    return (lax.axis_index("zl") * 4 + lax.axis_index("x")) * 2 + lax.axis_index("co")


def spot(zh, i, f, b):
    near = 1 - lax.bitwise_xor(lax.shift_right_logical(i, 3), zh)
    return near * 48 + lax.bitwise_and(i, NY - 1) * 6 + f * 3 + b


def place_kernel(got, far, near, both, table, moves, sems):
    zh = lax.axis_index("zh")
    lane = lax.broadcasted_iota(jnp.int32, (8, 128), 1)
    place = jnp.full((8, 128), float(ROWS), F32)
    for s in range(SLABS):
        place = jnp.where(lane == s, got[s, CAP * CH_DEV:, :].astype(F32), place)
    place = place.astype(jnp.int32)
    f = lax.shift_right_logical(place, 5)
    h = lax.bitwise_and(place, 31)
    odd = lax.bitwise_and(h, 1)
    i = lax.shift_right_logical(h, 1)
    first = spot(zh, i, f, 1 + odd)
    second = jnp.where((odd == 1) & (i < OUT_ROWS - 1), spot(zh, i + 1, f, 0), first)
    table[...] = jnp.where(place < ROWS, first * 128 + second, 96 * 128 + 96)
    copy = pltpu.make_async_copy(table, moves, sems.at[0])
    copy.start()
    for f in range(2):
        both[spot(zh, jnp.int32(0), f, 0)] = jnp.zeros((CH_DEV, 128), BF)
    copy.wait()

    def some(s, carry):
        for source in (2 * s, 2 * s + 1):
            for r in range(CAP):
                move = moves[r, source]
                row = got[source, r * CH_DEV:(r + 1) * CH_DEV, :]
                both[lax.shift_right_logical(move, 7)] = row
                both[lax.bitwise_and(move, 127)] = row
        return carry

    lax.fori_loop(0, SLABS // 2, some, 0)
    copies = [
        pltpu.make_async_copy(both.at[pl.ds(48 * k, 48)], out, sems.at[k])
        for k, out in enumerate((far, near))
    ]
    for copy in copies:
        copy.start()
    for copy in copies:
        copy.wait()


def clip_start_of(lengths, frame):
    first = jnp.int32(0)
    end = jnp.int32(0)
    for k in range(4):
        start = end
        end = end + lengths[k]
        first = jnp.where((frame >= start) & (frame < end), start, first)
    return first


def conv_kernel(lengths, frames, *rest):
    weights, (own, after, taps) = rest[:NY + 1], rest[NY + 1:]
    y = lax.axis_index("y")
    core = lax.axis_index("co")
    slab = my_slab()
    sign = 2 * core - 1
    sources = [y]
    for s in range(1, 4):
        sources += [y + sign * s, y - sign * s]
    sources += [y + 4, y + 4]
    sources = [lax.bitwise_and(s + NY, NY - 1) for s in sources]
    whole = pl.ds(0, CH_DEV)
    mine = pl.ds(pl.multiple_of(core * HALF, HALF), HALF)
    other = pl.ds(pl.multiple_of((1 - core) * HALF, HALF), HALF)
    sources = list(zip(sources, [whole] * 7 + [mine, other]))
    j = lax.broadcasted_iota(jnp.int32, (192, 128), 0)
    w = lax.broadcasted_iota(jnp.int32, (192, 128), 1)
    wanted = jnp.where(j < 64, 2 * j - 1, jnp.where(j < 128, 2 * j - 128, 2 * j - 255))
    pick = (w == wanted).astype(F32).astype(BF)
    for t in range(2):
        for b in range(3):
            x = jnp.concatenate([frames[s, t * 3 + b, c] for s, c in sources], axis=0)
            picked = lax.dot_general(pick, x, (((1,), (1,)), ((), ())),
                                     preferred_element_type=F32).astype(BF)
            for e in range(3):
                taps[b, t * 64:(t + 1) * 64, e * 256:(e + 1) * 256] = picked[e * 64:(e + 1) * 64]
    own[...] = jnp.zeros(own.shape, F32)
    after[...] = jnp.zeros(after.shape, F32)

    def gates(a):
        parts = []
        for t in range(2):
            frame = slab * 2 + t
            allowed = frame >= clip_start_of(lengths, frame + 2 - a)
            parts.append(jnp.full((64, 768), jnp.where(allowed, 1.0, 0.0), F32).astype(BF))
        return jnp.concatenate(parts, axis=0)

    def row_tap(b, carry):
        lhs = taps[b]
        for a in range(3):
            tap = (a * 3 + b) * 3
            kernel = jnp.concatenate([ref[tap + e] for e in range(3) for ref in weights], axis=0)
            part = jnp.dot(lhs * gates(a), kernel, preferred_element_type=F32)
            if a == 0:
                after[...] += part
            elif a == 1:
                own[64:] += part[:64]
                after[:64] += part[64:]
            else:
                own[...] += part
        return carry

    lax.fori_loop(0, 3, row_tap, 0)


def group_matrix(channels_first):
    shape = (COUT, 128) if channels_first else (128, COUT)
    c = lax.broadcasted_iota(jnp.int32, shape, 0 if channels_first else 1)
    g = lax.broadcasted_iota(jnp.int32, shape, 1 if channels_first else 0)
    return (lax.shift_right_logical(c, 4) == g).astype(F32)


def member_of(lengths, frame):
    end = jnp.int32(0)
    flags = []
    for k in range(4):
        start = end
        end = end + lengths[k]
        flags.append(jnp.where((frame >= start) & (frame < end), 1.0, 0.0).astype(F32))
    return flags


def stat_kernel(lengths, near, before, conv_out, stats):
    slab = my_slab()
    conv = near[...] + before[...]
    conv_out[...] = conv
    rows = []
    for f in range(2):
        part = conv[f * 64:(f + 1) * 64]
        rows.append(jnp.sum(part, axis=0, keepdims=True))
        rows.append(jnp.sum(part * part, axis=0, keepdims=True))
    rows = jnp.concatenate(rows + rows, axis=0)
    grouped = jnp.dot(rows, group_matrix(True), precision=HIGHEST, preferred_element_type=F32)
    m0 = member_of(lengths, slab * 2)
    m1 = member_of(lengths, slab * 2 + 1)
    sums = [grouped[0:1] * m0[k] + grouped[2:3] * m1[k] for k in range(4)]
    squares = [grouped[1:2] * m0[k] + grouped[3:4] * m1[k] for k in range(4)]
    tile = jnp.concatenate(sums + squares, axis=0)
    stats[...] = jnp.broadcast_to(tile[None], stats.shape)


def middle_kernel(got, out):
    out[...] = jnp.broadcast_to(jnp.sum(got[...], axis=0)[None], out.shape)


def final_kernel(lengths, got, conv, gain, bias, out):
    slab = my_slab()
    total = jnp.sum(got[...], axis=0)
    spread = group_matrix(False)
    for f in range(2):
        flags = member_of(lengths, slab * 2 + f)
        sums = jnp.zeros((1, 128), F32)
        squares = jnp.zeros((1, 128), F32)
        frames = jnp.float32(0)
        for k in range(4):
            sums = sums + total[k:k + 1] * flags[k]
            squares = squares + total[4 + k:5 + k] * flags[k]
            frames = frames + flags[k] * lengths[k].astype(F32)
        entries = jnp.full((1, 128), frames * float(OUT_ROWS * 64 * GROUP_SIZE), F32)
        mean = sums / entries
        var = squares / entries - mean * mean
        scale = lax.rsqrt(var + EPSILON)
        both = jnp.concatenate([mean, scale] * 4, axis=0)
        wide = jnp.dot(both, spread, precision=HIGHEST, preferred_element_type=F32)
        part = conv[f * 64:(f + 1) * 64]
        v = ((part - wide[0:1]) * wide[1:2]) * gain[...] + bias[...]
        out[f] = (v / (1.0 + jnp.exp(-v))).astype(BF)


def shuffle(x, axis):
    return lax.all_to_all(x, axis, split_axis=0, concat_axis=0, tiled=True)


def gathered_weights(kernel):
    ring = [(c * NY + y, c * NY + (y + (1 if c == 0 else NY - 1)) % NY)
            for c in range(2) for y in range(NY)]
    swap = [(0, 1), (1, 0)]
    moved = [kernel]
    for _ in range(3):
        moved.append(lax.ppermute(moved[-1], ("co", "y"), ring))
    first = lax.axis_index("co") * HALF
    half = lax.dynamic_slice_in_dim(moved[3], first, HALF, axis=1)
    moved.append(lax.ppermute(half, ("co", "y"), ring))
    swapped = [lax.ppermute(shard, "co", swap) for shard in moved[1:]]
    return moved, swapped


def convolve(lengths, frames, weights):
    return pl.pallas_call(
        conv_kernel,
        out_shape=[jax.ShapeDtypeStruct((128, COUT), F32)] * 2,
        in_specs=[SMEM] + [VMEM] * (2 + NY),
        out_specs=[VMEM, VMEM],
        scratch_shapes=[pltpu.VMEM((3, 128, 768), BF)],
        compiler_params=params(24),
    )(lengths, frames, *weights)


def body(arrived, row_target, clip_lengths, conv_weight, gn_gain, gn_bias):
    moved, swapped = gathered_weights(conv_weight.reshape(27, CH_DEV, COUT))
    send = pl.pallas_call(
        pack_kernel,
        out_shape=jax.ShapeDtypeStruct((SLABS, 136, 128), BF),
        in_specs=[SMEM, HBM],
        out_specs=VMEM,
        scratch_shapes=[
            pltpu.VMEM((ROWS, CH_DEV, 128), BF),
            pltpu.SMEM((SLABS,), jnp.int32),
            pltpu.VMEM((SLABS, 8, 128), F32),
            pltpu.SemaphoreType.DMA,
        ],
        compiler_params=params(60),
    )(row_target, arrived)
    got = shuffle(send, TM)
    got, moved[2], swapped[0] = lax.optimization_barrier(
        (got, moved[2], swapped[0])
    )
    far, near = pl.pallas_call(
        place_kernel,
        out_shape=[jax.ShapeDtypeStruct((NY * 6, CH_DEV, 128), BF)] * 2,
        in_specs=[VMEM],
        out_specs=[HBM, HBM],
        scratch_shapes=[
            pltpu.VMEM((97, CH_DEV, 128), BF),
            pltpu.VMEM((8, 128), jnp.int32),
            pltpu.SMEM((8, 128), jnp.int32),
            pltpu.SemaphoreType.DMA((2,)),
        ],
        compiler_params=params(8),
    )(got)
    weights = [moved[0], moved[1], swapped[0], moved[2], swapped[1], moved[3], swapped[2]]
    weights += [moved[4], swapped[3]]
    onward = [(i, i + 1) for i in range(SLABS - 1)]
    far = shuffle(far.reshape(NY, 6, CH_DEV, 128), "y")
    near = shuffle(near.reshape(NY, 6, CH_DEV, 128), "y")
    far, far_after = convolve(clip_lengths, far, weights)
    far_before = lax.ppermute(far_after, TM, onward)
    near, near_after = convolve(clip_lengths, near, weights)
    near_before = lax.ppermute(near_after, TM, onward)
    far = lax.ppermute(far + far_before, "zh", [(0, 1), (1, 0)])
    near = near + far
    conv, stats = pl.pallas_call(
        stat_kernel,
        out_shape=[jax.ShapeDtypeStruct((128, COUT), F32), jax.ShapeDtypeStruct((16, 8, 128), F32)],
        in_specs=[SMEM, VMEM, VMEM],
        out_specs=[VMEM, VMEM],
        compiler_params=params(16),
    )(clip_lengths, near, near_before)
    stats = shuffle(stats, ("y", "co"))
    stats = pl.pallas_call(
        middle_kernel,
        out_shape=jax.ShapeDtypeStruct((SLABS, 8, 128), F32),
        in_specs=[VMEM],
        out_specs=VMEM,
    )(stats)
    stats = shuffle(stats, ("zl", "zh", "x"))
    out = pl.pallas_call(
        final_kernel,
        out_shape=jax.ShapeDtypeStruct((2, 64, COUT), BF),
        in_specs=[SMEM, VMEM, VMEM, VMEM, VMEM],
        out_specs=VMEM,
        compiler_params=params(16),
    )(clip_lengths, stats, conv, gn_gain.reshape(1, COUT), gn_bias.reshape(1, COUT))
    return out.reshape(1, 2, 64, COUT)


def solution(mesh):
    fine = Mesh(mesh.devices.reshape(4, 4, 2, 2, 8), TM + CH)
    in_specs = (P(TM, CH, None), P(TM), P(), P(None, None, None, CH, None), P(), P())
    out_specs = P(CH, TM, None, None)
    return jax.shard_map(body, mesh=fine, in_specs=in_specs, out_specs=out_specs, check_vma=False)
```

```python
import functools

import jax
import jax.numpy as jnp
from jax import lax
from jax.experimental import pallas as pl
from jax.experimental.pallas import tpu as pltpu
from jax.sharding import Mesh, PartitionSpec as P

TM = ("zl", "x", "co")
CH = ("zh", "y")
SLABS = 32
ROWS = 64
CAP = 4
CH_DEV = 32
HALF = 16
SHARDS = 11
NY = 8
OUT_ROWS = 16
COUT = 512
GROUPS = 32
GROUP_SIZE = 16
EPSILON = 1e-05
BF = jnp.bfloat16
F32 = jnp.float32
HIGHEST = lax.Precision.HIGHEST

VMEM = pl.BlockSpec(memory_space=pltpu.VMEM)
SMEM = pl.BlockSpec(memory_space=pltpu.SMEM)
HBM = pl.BlockSpec(memory_space=pltpu.HBM)


def params(mib):
    return pltpu.CompilerParams(vmem_limit_bytes=mib * 1024 * 1024)


def pack_kernel(target, arrived, send, rows, counts, places, sem):
    fetch = pltpu.make_async_copy(arrived, rows, sem)
    fetch.start()
    places[...] = jnp.full(places.shape, float(ROWS), F32)

    def clear(i, carry):
        counts[i] = 0
        return carry

    lax.fori_loop(0, SLABS, clear, 0)
    fetch.wait()

    def some(n, carry):
        for k in range(4):
            i = n * 4 + k
            t = target[i]
            owner = lax.shift_right_logical(t, 6)
            rank = counts[owner]
            counts[owner] = rank + 1
            slot = pl.ds(pl.multiple_of(rank * CH_DEV, CH_DEV), CH_DEV)
            send[owner, slot, :] = rows[i]
            place = lax.bitwise_and(t, ROWS - 1).astype(F32)
            places[owner, pl.ds(rank, 1), :] = jnp.full((1, 128), place, F32)
        return carry

    lax.fori_loop(0, ROWS // 4, some, 0)
    send[:, CAP * CH_DEV:, :] = places[...].astype(BF)


def my_slab():
    return (lax.axis_index("zl") * 4 + lax.axis_index("x")) * 2 + lax.axis_index("co")


def spot(zh, i, f, b):
    near = 1 - lax.bitwise_xor(lax.shift_right_logical(i, 3), zh)
    return near * 48 + lax.bitwise_and(i, NY - 1) * 6 + f * 3 + b


def place_kernel(got, far, near, both, table, moves, sems):
    zh = lax.axis_index("zh")
    lane = lax.broadcasted_iota(jnp.int32, (8, 128), 1)
    place = jnp.full((8, 128), float(ROWS), F32)
    for s in range(SLABS):
        place = jnp.where(lane == s, got[s, CAP * CH_DEV:, :].astype(F32), place)
    place = place.astype(jnp.int32)
    f = lax.shift_right_logical(place, 5)
    h = lax.bitwise_and(place, 31)
    odd = lax.bitwise_and(h, 1)
    i = lax.shift_right_logical(h, 1)
    first = spot(zh, i, f, 1 + odd)
    second = jnp.where((odd == 1) & (i < OUT_ROWS - 1), spot(zh, i + 1, f, 0), first)
    table[...] = jnp.where(place < ROWS, first * 128 + second, 96 * 128 + 96)
    copy = pltpu.make_async_copy(table, moves, sems.at[0])
    copy.start()
    for f in range(2):
        both[spot(zh, jnp.int32(0), f, 0)] = jnp.zeros((CH_DEV, 128), BF)
    copy.wait()

    def some(s, carry):
        for source in (2 * s, 2 * s + 1):
            for r in range(CAP):
                move = moves[r, source]
                row = got[source, r * CH_DEV:(r + 1) * CH_DEV, :]
                both[lax.shift_right_logical(move, 7)] = row
                both[lax.bitwise_and(move, 127)] = row
        return carry

    lax.fori_loop(0, SLABS // 2, some, 0)
    copies = [
        pltpu.make_async_copy(both.at[pl.ds(48 * k, 48)], out, sems.at[k])
        for k, out in enumerate((far, near))
    ]
    for copy in copies:
        copy.start()
    for copy in copies:
        copy.wait()


def clip_start_of(lengths, frame):
    first = jnp.int32(0)
    end = jnp.int32(0)
    for k in range(4):
        start = end
        end = end + lengths[k]
        first = jnp.where((frame >= start) & (frame < end), start, first)
    return first


def conv_kernel(lengths, frames, *rest):
    weights, (own, after, taps) = rest[:SHARDS], rest[SHARDS:]
    y = lax.axis_index("y")
    core = lax.axis_index("co")
    slab = my_slab()
    sign = 2 * core - 1
    whole = pl.ds(0, CH_DEV)
    mine = pl.ds(pl.multiple_of(core * HALF, HALF), HALF)
    other = pl.ds(pl.multiple_of((1 - core) * HALF, HALF), HALF)
    sources = [(y, whole)]
    for s in (sign, 2 * sign):
        sources += [(y + s, whole), (y - s, whole)]
    s = 3 * sign
    sources += [(y + s, mine), (y + s, other), (y - s, other), (y - s, mine)]
    sources += [(y + 4, mine), (y + 4, other)]
    sources = [(lax.bitwise_and(s + NY, NY - 1), c) for s, c in sources]
    j = lax.broadcasted_iota(jnp.int32, (192, 128), 0)
    w = lax.broadcasted_iota(jnp.int32, (192, 128), 1)
    wanted = jnp.where(j < 64, 2 * j - 1, jnp.where(j < 128, 2 * j - 128, 2 * j - 255))
    pick = (w == wanted).astype(F32).astype(BF)
    for t in range(2):
        for b in range(3):
            x = jnp.concatenate([frames[s, t * 3 + b, c] for s, c in sources], axis=0)
            picked = lax.dot_general(pick, x, (((1,), (1,)), ((), ())),
                                     preferred_element_type=F32).astype(BF)
            for e in range(3):
                taps[b, t * 64:(t + 1) * 64, e * 256:(e + 1) * 256] = picked[e * 64:(e + 1) * 64]
    own[...] = jnp.zeros(own.shape, F32)
    after[...] = jnp.zeros(after.shape, F32)

    def gates(a):
        parts = []
        for t in range(2):
            frame = slab * 2 + t
            allowed = frame >= clip_start_of(lengths, frame + 2 - a)
            parts.append(jnp.full((64, 768), jnp.where(allowed, 1.0, 0.0), F32).astype(BF))
        return jnp.concatenate(parts, axis=0)

    def row_tap(b, carry):
        lhs = taps[b]
        for a in range(3):
            tap = (a * 3 + b) * 3
            kernel = jnp.concatenate([ref[tap + e] for e in range(3) for ref in weights], axis=0)
            part = jnp.dot(lhs * gates(a), kernel, preferred_element_type=F32)
            if a == 0:
                after[...] += part
            elif a == 1:
                own[64:] += part[:64]
                after[:64] += part[64:]
            else:
                own[...] += part
        return carry

    lax.fori_loop(0, 3, row_tap, 0)


def group_matrix(channels_first):
    shape = (COUT, 128) if channels_first else (128, COUT)
    c = lax.broadcasted_iota(jnp.int32, shape, 0 if channels_first else 1)
    g = lax.broadcasted_iota(jnp.int32, shape, 1 if channels_first else 0)
    return (lax.shift_right_logical(c, 4) == g).astype(F32)


def member_of(lengths, frame):
    end = jnp.int32(0)
    flags = []
    for k in range(4):
        start = end
        end = end + lengths[k]
        flags.append(jnp.where((frame >= start) & (frame < end), 1.0, 0.0).astype(F32))
    return flags


def stat_kernel(lengths, near, before, conv_out, stats):
    slab = my_slab()
    conv = near[...] + before[...]
    conv_out[...] = conv
    rows = []
    for f in range(2):
        part = conv[f * 64:(f + 1) * 64]
        rows.append(jnp.sum(part, axis=0, keepdims=True))
        rows.append(jnp.sum(part * part, axis=0, keepdims=True))
    rows = jnp.concatenate(rows + rows, axis=0)
    grouped = jnp.dot(rows, group_matrix(True), precision=HIGHEST, preferred_element_type=F32)
    m0 = member_of(lengths, slab * 2)
    m1 = member_of(lengths, slab * 2 + 1)
    sums = [grouped[0:1] * m0[k] + grouped[2:3] * m1[k] for k in range(4)]
    squares = [grouped[1:2] * m0[k] + grouped[3:4] * m1[k] for k in range(4)]
    tile = jnp.concatenate(sums + squares, axis=0)
    stats[...] = jnp.broadcast_to(tile[None], stats.shape)


def middle_kernel(got, out):
    out[...] = jnp.broadcast_to(jnp.sum(got[...], axis=0)[None], out.shape)


def final_kernel(lengths, got, conv, gain, bias, out):
    slab = my_slab()
    total = jnp.sum(got[...], axis=0)
    spread = group_matrix(False)
    for f in range(2):
        flags = member_of(lengths, slab * 2 + f)
        sums = jnp.zeros((1, 128), F32)
        squares = jnp.zeros((1, 128), F32)
        frames = jnp.float32(0)
        for k in range(4):
            sums = sums + total[k:k + 1] * flags[k]
            squares = squares + total[4 + k:5 + k] * flags[k]
            frames = frames + flags[k] * lengths[k].astype(F32)
        entries = jnp.full((1, 128), frames * float(OUT_ROWS * 64 * GROUP_SIZE), F32)
        mean = sums / entries
        var = squares / entries - mean * mean
        scale = lax.rsqrt(var + EPSILON)
        both = jnp.concatenate([mean, scale] * 4, axis=0)
        wide = jnp.dot(both, spread, precision=HIGHEST, preferred_element_type=F32)
        part = conv[f * 64:(f + 1) * 64]
        v = ((part - wide[0:1]) * wide[1:2]) * gain[...] + bias[...]
        out[f] = (v / (1.0 + jnp.exp(-v))).astype(BF)


def shuffle(x, axis):
    return lax.all_to_all(x, axis, split_axis=0, concat_axis=0, tiled=True)


def gathered_weights(kernel):
    ring = [(c * NY + y, c * NY + (y + (1 if c == 0 else NY - 1)) % NY)
            for c in range(2) for y in range(NY)]
    core = lax.axis_index("co")

    def step(shard):
        return lax.ppermute(shard, ("co", "y"), ring)

    def swap(shard):
        return lax.ppermute(shard, "co", [(0, 1), (1, 0)])

    first = step(kernel)
    second = step(first)
    mine = step(lax.dynamic_slice_in_dim(second, core * HALF, HALF, axis=1))
    other = step(lax.dynamic_slice_in_dim(second, (1 - core) * HALF, HALF, axis=1))
    last = step(mine)
    swapped = [swap(shard) for shard in (first, second, mine, other, last)]
    return [kernel, first, swapped[0], second, swapped[1], mine, other] + swapped[2:4] + [
        last, swapped[4]
    ]


def convolve(lengths, frames, weights):
    return pl.pallas_call(
        conv_kernel,
        out_shape=[jax.ShapeDtypeStruct((128, COUT), F32)] * 2,
        in_specs=[SMEM] + [VMEM] * (1 + SHARDS),
        out_specs=[VMEM, VMEM],
        scratch_shapes=[pltpu.VMEM((3, 128, 768), BF)],
        compiler_params=params(24),
    )(lengths, frames, *weights)


def body(arrived, row_target, clip_lengths, conv_weight, gn_gain, gn_bias):
    weights = gathered_weights(conv_weight.reshape(27, CH_DEV, COUT))
    send = pl.pallas_call(
        pack_kernel,
        out_shape=jax.ShapeDtypeStruct((SLABS, 136, 128), BF),
        in_specs=[SMEM, HBM],
        out_specs=VMEM,
        scratch_shapes=[
            pltpu.VMEM((ROWS, CH_DEV, 128), BF),
            pltpu.SMEM((SLABS,), jnp.int32),
            pltpu.VMEM((SLABS, 8, 128), F32),
            pltpu.SemaphoreType.DMA,
        ],
        compiler_params=params(60),
    )(row_target, arrived)
    got = shuffle(send, TM)
    got, weights[2], weights[4] = lax.optimization_barrier(
        (got, weights[2], weights[4])
    )
    far, near = pl.pallas_call(
        place_kernel,
        out_shape=[jax.ShapeDtypeStruct((NY * 6, CH_DEV, 128), BF)] * 2,
        in_specs=[VMEM],
        out_specs=[HBM, HBM],
        scratch_shapes=[
            pltpu.VMEM((97, CH_DEV, 128), BF),
            pltpu.VMEM((8, 128), jnp.int32),
            pltpu.SMEM((8, 128), jnp.int32),
            pltpu.SemaphoreType.DMA((2,)),
        ],
        compiler_params=params(8),
    )(got)
    onward = [(i, i + 1) for i in range(SLABS - 1)]
    far = shuffle(far.reshape(NY, 6, CH_DEV, 128), "y")
    near, weights[8], weights[10] = lax.optimization_barrier((near, weights[8], weights[10]))
    near = shuffle(near.reshape(NY, 6, CH_DEV, 128), "y")
    far, far_after = convolve(clip_lengths, far, weights)
    far_before = lax.ppermute(far_after, TM, onward)
    near, near_after = convolve(clip_lengths, near, weights)
    near_before = lax.ppermute(near_after, TM, onward)
    far = lax.ppermute(far + far_before, "zh", [(0, 1), (1, 0)])
    near = near + far
    conv, stats = pl.pallas_call(
        stat_kernel,
        out_shape=[jax.ShapeDtypeStruct((128, COUT), F32), jax.ShapeDtypeStruct((16, 8, 128), F32)],
        in_specs=[SMEM, VMEM, VMEM],
        out_specs=[VMEM, VMEM],
        compiler_params=params(16),
    )(clip_lengths, near, near_before)
    stats = shuffle(stats, ("y", "co"))
    stats = pl.pallas_call(
        middle_kernel,
        out_shape=jax.ShapeDtypeStruct((SLABS, 8, 128), F32),
        in_specs=[VMEM],
        out_specs=VMEM,
    )(stats)
    stats = shuffle(stats, ("zl", "zh", "x"))
    out = pl.pallas_call(
        final_kernel,
        out_shape=jax.ShapeDtypeStruct((2, 64, COUT), BF),
        in_specs=[SMEM, VMEM, VMEM, VMEM, VMEM],
        out_specs=VMEM,
        compiler_params=params(16),
    )(clip_lengths, stats, conv, gn_gain.reshape(1, COUT), gn_bias.reshape(1, COUT))
    return out.reshape(1, 2, 64, COUT)


def solution(mesh):
    fine = Mesh(mesh.devices.reshape(4, 4, 2, 2, 8), TM + CH)
    in_specs = (P(TM, CH, None), P(TM), P(), P(None, None, None, CH, None), P(), P())
    out_specs = P(CH, TM, None, None)
    return jax.shard_map(body, mesh=fine, in_specs=in_specs, out_specs=out_specs, check_vma=False)
```

```python
import functools

import jax
import jax.numpy as jnp
from jax import lax
from jax.experimental import pallas as pl
from jax.experimental.pallas import tpu as pltpu
from jax.sharding import Mesh, PartitionSpec as P

TM = ("zl", "x", "co")
CH = ("zh", "y")
SLABS = 32
ROWS = 64
CAP = 4
CH_DEV = 32
HALF = 16
NY = 8
OUT_ROWS = 16
COUT = 512
GROUPS = 32
GROUP_SIZE = 16
EPSILON = 1e-05
BF = jnp.bfloat16
F32 = jnp.float32
HIGHEST = lax.Precision.HIGHEST

VMEM = pl.BlockSpec(memory_space=pltpu.VMEM)
SMEM = pl.BlockSpec(memory_space=pltpu.SMEM)
HBM = pl.BlockSpec(memory_space=pltpu.HBM)


def params(mib):
    return pltpu.CompilerParams(vmem_limit_bytes=mib * 1024 * 1024)


def pack_kernel(target, arrived, send, rows, counts, places, sem):
    fetch = pltpu.make_async_copy(arrived, rows, sem)
    fetch.start()
    places[...] = jnp.full(places.shape, float(ROWS), F32)

    def clear(i, carry):
        counts[i] = 0
        return carry

    lax.fori_loop(0, SLABS, clear, 0)
    fetch.wait()

    def some(n, carry):
        for k in range(4):
            i = n * 4 + k
            t = target[i]
            owner = lax.shift_right_logical(t, 6)
            rank = counts[owner]
            counts[owner] = rank + 1
            slot = pl.ds(pl.multiple_of(rank * CH_DEV, CH_DEV), CH_DEV)
            send[owner, slot, :] = rows[i]
            place = lax.bitwise_and(t, ROWS - 1).astype(F32)
            places[owner, pl.ds(rank, 1), :] = jnp.full((1, 128), place, F32)
        return carry

    lax.fori_loop(0, ROWS // 4, some, 0)
    send[:, CAP * CH_DEV:, :] = places[...].astype(BF)


def my_slab():
    return (lax.axis_index("zl") * 4 + lax.axis_index("x")) * 2 + lax.axis_index("co")


def spot(zh, i, f, b):
    near = 1 - lax.bitwise_xor(lax.shift_right_logical(i, 3), zh)
    return near * 48 + lax.bitwise_and(i, NY - 1) * 6 + f * 3 + b


def place_kernel(got, far, near, both, table, moves, sems):
    zh = lax.axis_index("zh")
    lane = lax.broadcasted_iota(jnp.int32, (8, 128), 1)
    place = jnp.full((8, 128), float(ROWS), F32)
    for s in range(SLABS):
        place = jnp.where(lane == s, got[s, CAP * CH_DEV:, :].astype(F32), place)
    place = place.astype(jnp.int32)
    f = lax.shift_right_logical(place, 5)
    h = lax.bitwise_and(place, 31)
    odd = lax.bitwise_and(h, 1)
    i = lax.shift_right_logical(h, 1)
    first = spot(zh, i, f, 1 + odd)
    second = jnp.where((odd == 1) & (i < OUT_ROWS - 1), spot(zh, i + 1, f, 0), first)
    table[...] = jnp.where(place < ROWS, first * 128 + second, 96 * 128 + 96)
    copy = pltpu.make_async_copy(table, moves, sems.at[0])
    copy.start()
    for f in range(2):
        both[spot(zh, jnp.int32(0), f, 0)] = jnp.zeros((CH_DEV, 128), BF)
    copy.wait()

    def some(s, carry):
        for source in (2 * s, 2 * s + 1):
            for r in range(CAP):
                move = moves[r, source]
                row = got[source, r * CH_DEV:(r + 1) * CH_DEV, :]
                both[lax.shift_right_logical(move, 7)] = row
                both[lax.bitwise_and(move, 127)] = row
        return carry

    lax.fori_loop(0, SLABS // 2, some, 0)
    copies = [
        pltpu.make_async_copy(both.at[pl.ds(48 * k, 48)], out, sems.at[k])
        for k, out in enumerate((far, near))
    ]
    for copy in copies:
        copy.start()
    for copy in copies:
        copy.wait()


def clip_start_of(lengths, frame):
    first = jnp.int32(0)
    end = jnp.int32(0)
    for k in range(4):
        start = end
        end = end + lengths[k]
        first = jnp.where((frame >= start) & (frame < end), start, first)
    return first


def conv_kernel(lengths, frames, *rest):
    weights, (own, after, taps) = rest[:NY + 1], rest[NY + 1:]
    y = lax.axis_index("y")
    core = lax.axis_index("co")
    slab = my_slab()
    sign = 2 * core - 1
    sources = [y]
    for s in range(1, 4):
        sources += [y + sign * s, y - sign * s]
    sources += [y + 4, y + 4]
    sources = [lax.bitwise_and(s + NY, NY - 1) for s in sources]
    whole = pl.ds(0, CH_DEV)
    mine = pl.ds(pl.multiple_of(core * HALF, HALF), HALF)
    other = pl.ds(pl.multiple_of((1 - core) * HALF, HALF), HALF)
    sources = list(zip(sources, [whole] * 7 + [mine, other]))
    j = lax.broadcasted_iota(jnp.int32, (192, 128), 0)
    w = lax.broadcasted_iota(jnp.int32, (192, 128), 1)
    wanted = jnp.where(j < 64, 2 * j - 1, jnp.where(j < 128, 2 * j - 128, 2 * j - 255))
    pick = (w == wanted).astype(F32).astype(BF)
    for t in range(2):
        for b in range(3):
            x = jnp.concatenate([frames[s, t * 3 + b, c] for s, c in sources], axis=0)
            picked = lax.dot_general(pick, x, (((1,), (1,)), ((), ())),
                                     preferred_element_type=F32).astype(BF)
            for e in range(3):
                taps[b, t * 64:(t + 1) * 64, e * 256:(e + 1) * 256] = picked[e * 64:(e + 1) * 64]
    own[...] = jnp.zeros(own.shape, F32)
    after[...] = jnp.zeros(after.shape, F32)

    def gates(a):
        parts = []
        for t in range(2):
            frame = slab * 2 + t
            allowed = frame >= clip_start_of(lengths, frame + 2 - a)
            parts.append(jnp.full((64, 768), jnp.where(allowed, 1.0, 0.0), F32).astype(BF))
        return jnp.concatenate(parts, axis=0)

    def row_tap(b, carry):
        lhs = taps[b]
        for a in range(3):
            tap = (a * 3 + b) * 3
            kernel = jnp.concatenate([ref[tap + e] for e in range(3) for ref in weights], axis=0)
            part = jnp.dot(lhs * gates(a), kernel, preferred_element_type=F32)
            if a == 0:
                after[...] += part
            elif a == 1:
                own[64:] += part[:64]
                after[:64] += part[64:]
            else:
                own[...] += part
        return carry

    lax.fori_loop(0, 3, row_tap, 0)


def group_matrix(channels_first):
    shape = (COUT, 128) if channels_first else (128, COUT)
    c = lax.broadcasted_iota(jnp.int32, shape, 0 if channels_first else 1)
    g = lax.broadcasted_iota(jnp.int32, shape, 1 if channels_first else 0)
    return (lax.shift_right_logical(c, 4) == g).astype(F32)


def member_of(lengths, frame):
    end = jnp.int32(0)
    flags = []
    for k in range(4):
        start = end
        end = end + lengths[k]
        flags.append(jnp.where((frame >= start) & (frame < end), 1.0, 0.0).astype(F32))
    return flags


def stat_kernel(lengths, near, before, conv_out, stats):
    slab = my_slab()
    conv = near[...] + before[...]
    conv_out[...] = conv
    rows = []
    for f in range(2):
        part = conv[f * 64:(f + 1) * 64]
        rows.append(jnp.sum(part, axis=0, keepdims=True))
        rows.append(jnp.sum(part * part, axis=0, keepdims=True))
    rows = jnp.concatenate(rows + rows, axis=0)
    grouped = jnp.dot(rows, group_matrix(True), precision=HIGHEST, preferred_element_type=F32)
    m0 = member_of(lengths, slab * 2)
    m1 = member_of(lengths, slab * 2 + 1)
    sums = [grouped[0:1] * m0[k] + grouped[2:3] * m1[k] for k in range(4)]
    squares = [grouped[1:2] * m0[k] + grouped[3:4] * m1[k] for k in range(4)]
    tile = jnp.concatenate(sums + squares, axis=0)
    stats[...] = jnp.broadcast_to(tile[None], stats.shape)


def middle_kernel(got, out):
    out[...] = jnp.broadcast_to(jnp.sum(got[...], axis=0)[None], out.shape)


def final_kernel(lengths, got, conv, gain, bias, out):
    slab = my_slab()
    total = jnp.sum(got[...], axis=0)
    spread = group_matrix(False)
    for f in range(2):
        flags = member_of(lengths, slab * 2 + f)
        sums = jnp.zeros((1, 128), F32)
        squares = jnp.zeros((1, 128), F32)
        frames = jnp.float32(0)
        for k in range(4):
            sums = sums + total[k:k + 1] * flags[k]
            squares = squares + total[4 + k:5 + k] * flags[k]
            frames = frames + flags[k] * lengths[k].astype(F32)
        entries = jnp.full((1, 128), frames * float(OUT_ROWS * 64 * GROUP_SIZE), F32)
        mean = sums / entries
        var = squares / entries - mean * mean
        scale = lax.rsqrt(var + EPSILON)
        both = jnp.concatenate([mean, scale] * 4, axis=0)
        wide = jnp.dot(both, spread, precision=HIGHEST, preferred_element_type=F32)
        part = conv[f * 64:(f + 1) * 64]
        v = ((part - wide[0:1]) * wide[1:2]) * gain[...] + bias[...]
        out[f] = (v / (1.0 + jnp.exp(-v))).astype(BF)


def shuffle(x, axis):
    return lax.all_to_all(x, axis, split_axis=0, concat_axis=0, tiled=True)


def gathered_weights(kernel):
    ring = [(c * NY + y, c * NY + (y + (1 if c == 0 else NY - 1)) % NY)
            for c in range(2) for y in range(NY)]
    swap = [(0, 1), (1, 0)]
    moved = [kernel]
    for _ in range(3):
        moved.append(lax.ppermute(moved[-1], ("co", "y"), ring))
    first = lax.axis_index("co") * HALF
    half = lax.dynamic_slice_in_dim(moved[3], first, HALF, axis=1)
    second, half = lax.optimization_barrier((moved[2], half))
    moved.append(lax.ppermute(half, ("co", "y"), ring))
    swapped = [lax.ppermute(shard, "co", swap) for shard in (moved[1], second, moved[3], moved[4])]
    return moved, swapped


def convolve(lengths, frames, weights):
    return pl.pallas_call(
        conv_kernel,
        out_shape=[jax.ShapeDtypeStruct((128, COUT), F32)] * 2,
        in_specs=[SMEM] + [VMEM] * (2 + NY),
        out_specs=[VMEM, VMEM],
        scratch_shapes=[pltpu.VMEM((3, 128, 768), BF)],
        compiler_params=params(24),
    )(lengths, frames, *weights)


def body(arrived, row_target, clip_lengths, conv_weight, gn_gain, gn_bias):
    moved, swapped = gathered_weights(conv_weight.reshape(27, CH_DEV, COUT))
    send = pl.pallas_call(
        pack_kernel,
        out_shape=jax.ShapeDtypeStruct((SLABS, 136, 128), BF),
        in_specs=[SMEM, HBM],
        out_specs=VMEM,
        scratch_shapes=[
            pltpu.VMEM((ROWS, CH_DEV, 128), BF),
            pltpu.SMEM((SLABS,), jnp.int32),
            pltpu.VMEM((SLABS, 8, 128), F32),
            pltpu.SemaphoreType.DMA,
        ],
        compiler_params=params(60),
    )(row_target, arrived)
    got = shuffle(send, TM)
    got, moved[2], swapped[0] = lax.optimization_barrier(
        (got, moved[2], swapped[0])
    )
    far, near = pl.pallas_call(
        place_kernel,
        out_shape=[jax.ShapeDtypeStruct((NY * 6, CH_DEV, 128), BF)] * 2,
        in_specs=[VMEM],
        out_specs=[HBM, HBM],
        scratch_shapes=[
            pltpu.VMEM((97, CH_DEV, 128), BF),
            pltpu.VMEM((8, 128), jnp.int32),
            pltpu.SMEM((8, 128), jnp.int32),
            pltpu.SemaphoreType.DMA((2,)),
        ],
        compiler_params=params(8),
    )(got)
    weights = [moved[0], moved[1], swapped[0], moved[2], swapped[1], moved[3], swapped[2]]
    weights += [moved[4], swapped[3]]
    onward = [(i, i + 1) for i in range(SLABS - 1)]
    far = shuffle(far.reshape(NY, 6, CH_DEV, 128), "y")
    near = shuffle(near.reshape(NY, 6, CH_DEV, 128), "y")
    far, far_after = convolve(clip_lengths, far, weights)
    far_before = lax.ppermute(far_after, TM, onward)
    near, near_after = convolve(clip_lengths, near, weights)
    near_before = lax.ppermute(near_after, TM, onward)
    far = lax.ppermute(far + far_before, "zh", [(0, 1), (1, 0)])
    near = near + far
    conv, stats = pl.pallas_call(
        stat_kernel,
        out_shape=[jax.ShapeDtypeStruct((128, COUT), F32), jax.ShapeDtypeStruct((16, 8, 128), F32)],
        in_specs=[SMEM, VMEM, VMEM],
        out_specs=[VMEM, VMEM],
        compiler_params=params(16),
    )(clip_lengths, near, near_before)
    stats = shuffle(stats, ("y", "co"))
    stats = pl.pallas_call(
        middle_kernel,
        out_shape=jax.ShapeDtypeStruct((SLABS, 8, 128), F32),
        in_specs=[VMEM],
        out_specs=VMEM,
    )(stats)
    stats = shuffle(stats, ("zl", "zh", "x"))
    out = pl.pallas_call(
        final_kernel,
        out_shape=jax.ShapeDtypeStruct((2, 64, COUT), BF),
        in_specs=[SMEM, VMEM, VMEM, VMEM, VMEM],
        out_specs=VMEM,
        compiler_params=params(16),
    )(clip_lengths, stats, conv, gn_gain.reshape(1, COUT), gn_bias.reshape(1, COUT))
    return out.reshape(1, 2, 64, COUT)


def solution(mesh):
    fine = Mesh(mesh.devices.reshape(4, 4, 2, 2, 8), TM + CH)
    in_specs = (P(TM, CH, None), P(TM), P(), P(None, None, None, CH, None), P(), P())
    out_specs = P(CH, TM, None, None)
    return jax.shard_map(body, mesh=fine, in_specs=in_specs, out_specs=out_specs, check_vma=False)
```

```python
import functools

import jax
import jax.numpy as jnp
from jax import lax
from jax.experimental import pallas as pl
from jax.experimental.pallas import tpu as pltpu
from jax.sharding import Mesh, PartitionSpec as P

TM = ("zl", "x", "co")
CH = ("zh", "y")
SLABS = 32
ROWS = 64
CAP = 4
CH_DEV = 32
HALF = 16
NY = 8
OUT_ROWS = 16
COUT = 512
GROUPS = 32
GROUP_SIZE = 16
EPSILON = 1e-05
BF = jnp.bfloat16
F32 = jnp.float32
HIGHEST = lax.Precision.HIGHEST

VMEM = pl.BlockSpec(memory_space=pltpu.VMEM)
SMEM = pl.BlockSpec(memory_space=pltpu.SMEM)
HBM = pl.BlockSpec(memory_space=pltpu.HBM)


def params(mib):
    return pltpu.CompilerParams(vmem_limit_bytes=mib * 1024 * 1024)


def pack_kernel(target, arrived, send, rows, counts, places, sem):
    fetch = pltpu.make_async_copy(arrived, rows, sem)
    fetch.start()
    places[...] = jnp.full(places.shape, float(ROWS), F32)

    def clear(i, carry):
        counts[i] = 0
        return carry

    lax.fori_loop(0, SLABS, clear, 0)
    fetch.wait()

    def some(n, carry):
        for k in range(4):
            i = n * 4 + k
            t = target[i]
            owner = lax.shift_right_logical(t, 6)
            rank = counts[owner]
            counts[owner] = rank + 1
            slot = pl.ds(pl.multiple_of(rank * CH_DEV, CH_DEV), CH_DEV)
            send[owner, slot, :] = rows[i]
            place = lax.bitwise_and(t, ROWS - 1).astype(F32)
            places[owner, pl.ds(rank, 1), :] = jnp.full((1, 128), place, F32)
        return carry

    lax.fori_loop(0, ROWS // 4, some, 0)
    send[:, CAP * CH_DEV:, :] = places[...].astype(BF)


def my_slab():
    return (lax.axis_index("zl") * 4 + lax.axis_index("x")) * 2 + lax.axis_index("co")


def spot(zh, i, f, b):
    near = 1 - lax.bitwise_xor(lax.shift_right_logical(i, 3), zh)
    return near * 48 + lax.bitwise_and(i, NY - 1) * 6 + f * 3 + b


def place_kernel(got, far, near, both, table, moves, sems):
    zh = lax.axis_index("zh")
    lane = lax.broadcasted_iota(jnp.int32, (8, 128), 1)
    place = jnp.full((8, 128), float(ROWS), F32)
    for s in range(SLABS):
        place = jnp.where(lane == s, got[s, CAP * CH_DEV:, :].astype(F32), place)
    place = place.astype(jnp.int32)
    f = lax.shift_right_logical(place, 5)
    h = lax.bitwise_and(place, 31)
    odd = lax.bitwise_and(h, 1)
    i = lax.shift_right_logical(h, 1)
    first = spot(zh, i, f, 1 + odd)
    second = jnp.where((odd == 1) & (i < OUT_ROWS - 1), spot(zh, i + 1, f, 0), first)
    table[...] = jnp.where(place < ROWS, first * 128 + second, 96 * 128 + 96)
    copy = pltpu.make_async_copy(table, moves, sems.at[0])
    copy.start()
    for f in range(2):
        both[spot(zh, jnp.int32(0), f, 0)] = jnp.zeros((CH_DEV, 128), BF)
    copy.wait()

    def some(s, carry):
        for source in (2 * s, 2 * s + 1):
            for r in range(CAP):
                move = moves[r, source]
                row = got[source, r * CH_DEV:(r + 1) * CH_DEV, :]
                both[lax.shift_right_logical(move, 7)] = row
                both[lax.bitwise_and(move, 127)] = row
        return carry

    lax.fori_loop(0, SLABS // 2, some, 0)
    copies = [
        pltpu.make_async_copy(both.at[pl.ds(48 * k, 48)], out, sems.at[k])
        for k, out in enumerate((far, near))
    ]
    for copy in copies:
        copy.start()
    for copy in copies:
        copy.wait()


def clip_start_of(lengths, frame):
    first = jnp.int32(0)
    end = jnp.int32(0)
    for k in range(4):
        start = end
        end = end + lengths[k]
        first = jnp.where((frame >= start) & (frame < end), start, first)
    return first


def conv_kernel(lengths, frames, *rest):
    weights, (own, after, taps) = rest[:NY + 1], rest[NY + 1:]
    y = lax.axis_index("y")
    core = lax.axis_index("co")
    slab = my_slab()
    sign = 2 * core - 1
    sources = [y]
    for s in range(1, 4):
        sources += [y + sign * s, y - sign * s]
    sources += [y + 4, y + 4]
    sources = [lax.bitwise_and(s + NY, NY - 1) for s in sources]
    whole = pl.ds(0, CH_DEV)
    mine = pl.ds(pl.multiple_of(core * HALF, HALF), HALF)
    other = pl.ds(pl.multiple_of((1 - core) * HALF, HALF), HALF)
    sources = list(zip(sources, [whole] * 7 + [mine, other]))
    j = lax.broadcasted_iota(jnp.int32, (192, 128), 0)
    w = lax.broadcasted_iota(jnp.int32, (192, 128), 1)
    wanted = jnp.where(j < 64, 2 * j - 1, jnp.where(j < 128, 2 * j - 128, 2 * j - 255))
    pick = (w == wanted).astype(F32).astype(BF)
    for t in range(2):
        for b in range(3):
            x = jnp.concatenate([frames[s, t * 3 + b, c] for s, c in sources], axis=0)
            picked = lax.dot_general(pick, x, (((1,), (1,)), ((), ())),
                                     preferred_element_type=F32).astype(BF)
            for e in range(3):
                taps[b, t * 64:(t + 1) * 64, e * 256:(e + 1) * 256] = picked[e * 64:(e + 1) * 64]
    own[...] = jnp.zeros(own.shape, F32)
    after[...] = jnp.zeros(after.shape, F32)

    def gates(a):
        parts = []
        for t in range(2):
            frame = slab * 2 + t
            allowed = frame >= clip_start_of(lengths, frame + 2 - a)
            parts.append(jnp.full((64, 768), jnp.where(allowed, 1.0, 0.0), F32).astype(BF))
        return jnp.concatenate(parts, axis=0)

    def row_tap(b, carry):
        lhs = taps[b]
        for a in range(3):
            tap = (a * 3 + b) * 3
            kernel = jnp.concatenate([ref[tap + e] for e in range(3) for ref in weights], axis=0)
            part = jnp.dot(lhs * gates(a), kernel, preferred_element_type=F32)
            if a == 0:
                after[...] += part
            elif a == 1:
                own[64:] += part[:64]
                after[:64] += part[64:]
            else:
                own[...] += part
        return carry

    lax.fori_loop(0, 3, row_tap, 0)


def group_matrix(channels_first):
    shape = (COUT, 128) if channels_first else (128, COUT)
    c = lax.broadcasted_iota(jnp.int32, shape, 0 if channels_first else 1)
    g = lax.broadcasted_iota(jnp.int32, shape, 1 if channels_first else 0)
    return (lax.shift_right_logical(c, 4) == g).astype(F32)


def member_of(lengths, frame):
    end = jnp.int32(0)
    flags = []
    for k in range(4):
        start = end
        end = end + lengths[k]
        flags.append(jnp.where((frame >= start) & (frame < end), 1.0, 0.0).astype(F32))
    return flags


def stat_kernel(lengths, near, before, conv_out, stats):
    slab = my_slab()
    conv = near[...] + before[...]
    conv_out[...] = conv
    rows = []
    for f in range(2):
        part = conv[f * 64:(f + 1) * 64]
        rows.append(jnp.sum(part, axis=0, keepdims=True))
        rows.append(jnp.sum(part * part, axis=0, keepdims=True))
    rows = jnp.concatenate(rows + rows, axis=0)
    grouped = jnp.dot(rows, group_matrix(True), precision=HIGHEST, preferred_element_type=F32)
    m0 = member_of(lengths, slab * 2)
    m1 = member_of(lengths, slab * 2 + 1)
    sums = [grouped[0:1] * m0[k] + grouped[2:3] * m1[k] for k in range(4)]
    squares = [grouped[1:2] * m0[k] + grouped[3:4] * m1[k] for k in range(4)]
    tile = jnp.concatenate(sums + squares, axis=0)
    stats[...] = jnp.broadcast_to(tile[None], stats.shape)


def middle_kernel(got, out):
    out[...] = jnp.broadcast_to(jnp.sum(got[...], axis=0)[None], out.shape)


def final_kernel(lengths, got, conv, gain, bias, out):
    slab = my_slab()
    total = jnp.sum(got[...], axis=0)
    spread = group_matrix(False)
    for f in range(2):
        flags = member_of(lengths, slab * 2 + f)
        sums = jnp.zeros((1, 128), F32)
        squares = jnp.zeros((1, 128), F32)
        frames = jnp.float32(0)
        for k in range(4):
            sums = sums + total[k:k + 1] * flags[k]
            squares = squares + total[4 + k:5 + k] * flags[k]
            frames = frames + flags[k] * lengths[k].astype(F32)
        entries = jnp.full((1, 128), frames * float(OUT_ROWS * 64 * GROUP_SIZE), F32)
        mean = sums / entries
        var = squares / entries - mean * mean
        scale = lax.rsqrt(var + EPSILON)
        both = jnp.concatenate([mean, scale] * 4, axis=0)
        wide = jnp.dot(both, spread, precision=HIGHEST, preferred_element_type=F32)
        part = conv[f * 64:(f + 1) * 64]
        v = ((part - wide[0:1]) * wide[1:2]) * gain[...] + bias[...]
        out[f] = (v / (1.0 + jnp.exp(-v))).astype(BF)


def shuffle(x, axis):
    return lax.all_to_all(x, axis, split_axis=0, concat_axis=0, tiled=True)


def gathered_weights(kernel):
    ring = [(c * NY + y, c * NY + (y + (1 if c == 0 else NY - 1)) % NY)
            for c in range(2) for y in range(NY)]
    swap = [(0, 1), (1, 0)]
    moved = [kernel]
    for _ in range(3):
        moved.append(lax.ppermute(moved[-1], ("co", "y"), ring))
    first = lax.axis_index("co") * HALF
    half = lax.dynamic_slice_in_dim(moved[3], first, HALF, axis=1)
    second, half = lax.optimization_barrier((moved[2], half))
    moved.append(lax.ppermute(half, ("co", "y"), ring))
    swapped = [lax.ppermute(shard, "co", swap) for shard in (moved[1], second, moved[3], moved[4])]
    return moved, swapped


def convolve(lengths, frames, weights):
    return pl.pallas_call(
        conv_kernel,
        out_shape=[jax.ShapeDtypeStruct((128, COUT), F32)] * 2,
        in_specs=[SMEM] + [VMEM] * (2 + NY),
        out_specs=[VMEM, VMEM],
        scratch_shapes=[pltpu.VMEM((3, 128, 768), BF)],
        compiler_params=params(24),
    )(lengths, frames, *weights)


def body(arrived, row_target, clip_lengths, conv_weight, gn_gain, gn_bias):
    moved, swapped = gathered_weights(conv_weight.reshape(27, CH_DEV, COUT))
    send = pl.pallas_call(
        pack_kernel,
        out_shape=jax.ShapeDtypeStruct((SLABS, 136, 128), BF),
        in_specs=[SMEM, HBM],
        out_specs=VMEM,
        scratch_shapes=[
            pltpu.VMEM((ROWS, CH_DEV, 128), BF),
            pltpu.SMEM((SLABS,), jnp.int32),
            pltpu.VMEM((SLABS, 8, 128), F32),
            pltpu.SemaphoreType.DMA,
        ],
        compiler_params=params(60),
    )(row_target, arrived)
    got = shuffle(send, TM)
    got, moved[2] = lax.optimization_barrier((got, moved[2]))
    far, near = pl.pallas_call(
        place_kernel,
        out_shape=[jax.ShapeDtypeStruct((NY * 6, CH_DEV, 128), BF)] * 2,
        in_specs=[VMEM],
        out_specs=[HBM, HBM],
        scratch_shapes=[
            pltpu.VMEM((97, CH_DEV, 128), BF),
            pltpu.VMEM((8, 128), jnp.int32),
            pltpu.SMEM((8, 128), jnp.int32),
            pltpu.SemaphoreType.DMA((2,)),
        ],
        compiler_params=params(8),
    )(got)
    weights = [moved[0], moved[1], swapped[0], moved[2], swapped[1], moved[3], swapped[2]]
    weights += [moved[4], swapped[3]]
    onward = [(i, i + 1) for i in range(SLABS - 1)]
    far = shuffle(far.reshape(NY, 6, CH_DEV, 128), "y")
    near = shuffle(near.reshape(NY, 6, CH_DEV, 128), "y")
    far, far_after = convolve(clip_lengths, far, weights)
    far_before = lax.ppermute(far_after, TM, onward)
    near, near_after = convolve(clip_lengths, near, weights)
    near_before = lax.ppermute(near_after, TM, onward)
    far = lax.ppermute(far + far_before, "zh", [(0, 1), (1, 0)])
    near = near + far
    conv, stats = pl.pallas_call(
        stat_kernel,
        out_shape=[jax.ShapeDtypeStruct((128, COUT), F32), jax.ShapeDtypeStruct((16, 8, 128), F32)],
        in_specs=[SMEM, VMEM, VMEM],
        out_specs=[VMEM, VMEM],
        compiler_params=params(16),
    )(clip_lengths, near, near_before)
    stats = shuffle(stats, ("y", "co"))
    stats = pl.pallas_call(
        middle_kernel,
        out_shape=jax.ShapeDtypeStruct((SLABS, 8, 128), F32),
        in_specs=[VMEM],
        out_specs=VMEM,
    )(stats)
    stats = shuffle(stats, ("zl", "zh", "x"))
    out = pl.pallas_call(
        final_kernel,
        out_shape=jax.ShapeDtypeStruct((2, 64, COUT), BF),
        in_specs=[SMEM, VMEM, VMEM, VMEM, VMEM],
        out_specs=VMEM,
        compiler_params=params(16),
    )(clip_lengths, stats, conv, gn_gain.reshape(1, COUT), gn_bias.reshape(1, COUT))
    return out.reshape(1, 2, 64, COUT)


def solution(mesh):
    fine = Mesh(mesh.devices.reshape(4, 4, 2, 2, 8), TM + CH)
    in_specs = (P(TM, CH, None), P(TM), P(), P(None, None, None, CH, None), P(), P())
    out_specs = P(CH, TM, None, None)
    return jax.shard_map(body, mesh=fine, in_specs=in_specs, out_specs=out_specs, check_vma=False)
```

```python
import functools

import jax
import jax.numpy as jnp
from jax import lax
from jax.experimental import pallas as pl
from jax.experimental.pallas import tpu as pltpu
from jax.sharding import Mesh, PartitionSpec as P

TM = ("zl", "x", "co")
CH = ("zh", "y")
SLABS = 32
ROWS = 64
CAP = 4
CH_DEV = 32
HALF = 16
NY = 8
OUT_ROWS = 16
COUT = 512
GROUPS = 32
GROUP_SIZE = 16
EPSILON = 1e-05
BF = jnp.bfloat16
F32 = jnp.float32
HIGHEST = lax.Precision.HIGHEST

VMEM = pl.BlockSpec(memory_space=pltpu.VMEM)
SMEM = pl.BlockSpec(memory_space=pltpu.SMEM)
HBM = pl.BlockSpec(memory_space=pltpu.HBM)


def params(mib):
    return pltpu.CompilerParams(vmem_limit_bytes=mib * 1024 * 1024)


def pack_kernel(target, arrived, send, rows, counts, places, sem):
    fetch = pltpu.make_async_copy(arrived, rows, sem)
    fetch.start()
    places[...] = jnp.full(places.shape, float(ROWS), F32)

    def clear(i, carry):
        counts[i] = 0
        return carry

    lax.fori_loop(0, SLABS, clear, 0)
    fetch.wait()

    def some(n, carry):
        for k in range(4):
            i = n * 4 + k
            t = target[i]
            owner = lax.shift_right_logical(t, 6)
            rank = counts[owner]
            counts[owner] = rank + 1
            slot = pl.ds(pl.multiple_of(rank * CH_DEV, CH_DEV), CH_DEV)
            send[owner, slot, :] = rows[i]
            place = lax.bitwise_and(t, ROWS - 1).astype(F32)
            places[owner, pl.ds(rank, 1), :] = jnp.full((1, 128), place, F32)
        return carry

    lax.fori_loop(0, ROWS // 4, some, 0)
    send[:, CAP * CH_DEV:, :] = places[...].astype(BF)


def my_slab():
    return (lax.axis_index("zl") * 4 + lax.axis_index("x")) * 2 + lax.axis_index("co")


def spot(zh, i, f, b):
    near = 1 - lax.bitwise_xor(lax.shift_right_logical(i, 3), zh)
    return near * 48 + lax.bitwise_and(i, NY - 1) * 6 + f * 3 + b


def place_kernel(got, far, near, both, table, moves, sems):
    zh = lax.axis_index("zh")
    lane = lax.broadcasted_iota(jnp.int32, (8, 128), 1)
    place = jnp.full((8, 128), float(ROWS), F32)
    for s in range(SLABS):
        place = jnp.where(lane == s, got[s, CAP * CH_DEV:, :].astype(F32), place)
    place = place.astype(jnp.int32)
    f = lax.shift_right_logical(place, 5)
    h = lax.bitwise_and(place, 31)
    odd = lax.bitwise_and(h, 1)
    i = lax.shift_right_logical(h, 1)
    first = spot(zh, i, f, 1 + odd)
    second = jnp.where((odd == 1) & (i < OUT_ROWS - 1), spot(zh, i + 1, f, 0), first)
    table[...] = jnp.where(place < ROWS, first * 128 + second, 96 * 128 + 96)
    copy = pltpu.make_async_copy(table, moves, sems.at[0])
    copy.start()
    for f in range(2):
        both[spot(zh, jnp.int32(0), f, 0)] = jnp.zeros((CH_DEV, 128), BF)
    copy.wait()

    def some(s, carry):
        for source in (2 * s, 2 * s + 1):
            for r in range(CAP):
                move = moves[r, source]
                row = got[source, r * CH_DEV:(r + 1) * CH_DEV, :]
                both[lax.shift_right_logical(move, 7)] = row
                both[lax.bitwise_and(move, 127)] = row
        return carry

    lax.fori_loop(0, SLABS // 2, some, 0)
    copies = [
        pltpu.make_async_copy(both.at[pl.ds(48 * k, 48)], out, sems.at[k])
        for k, out in enumerate((far, near))
    ]
    for copy in copies:
        copy.start()
    for copy in copies:
        copy.wait()


def clip_start_of(lengths, frame):
    first = jnp.int32(0)
    end = jnp.int32(0)
    for k in range(4):
        start = end
        end = end + lengths[k]
        first = jnp.where((frame >= start) & (frame < end), start, first)
    return first


def conv_kernel(ahead, lengths, frames, *rest):
    weights, (out, taps) = rest[:NY + 1], rest[NY + 1:]
    y = lax.axis_index("y")
    core = lax.axis_index("co")
    slab = my_slab()
    sign = 2 * core - 1
    sources = [y]
    for s in range(1, 4):
        sources += [y + sign * s, y - sign * s]
    sources += [y + 4, y + 4]
    sources = [lax.bitwise_and(s + NY, NY - 1) for s in sources]
    whole = pl.ds(0, CH_DEV)
    mine = pl.ds(pl.multiple_of(core * HALF, HALF), HALF)
    other = pl.ds(pl.multiple_of((1 - core) * HALF, HALF), HALF)
    sources = list(zip(sources, [whole] * 7 + [mine, other]))
    j = lax.broadcasted_iota(jnp.int32, (192, 128), 0)
    w = lax.broadcasted_iota(jnp.int32, (192, 128), 1)
    wanted = jnp.where(j < 64, 2 * j - 1, jnp.where(j < 128, 2 * j - 128, 2 * j - 255))
    pick = (w == wanted).astype(F32).astype(BF)
    for t in range(2):
        for b in range(3):
            x = jnp.concatenate([frames[s, t * 3 + b, c] for s, c in sources], axis=0)
            picked = lax.dot_general(pick, x, (((1,), (1,)), ((), ())),
                                     preferred_element_type=F32).astype(BF)
            for e in range(3):
                taps[b, t * 64:(t + 1) * 64, e * 256:(e + 1) * 256] = picked[e * 64:(e + 1) * 64]
    out[...] = jnp.zeros(out.shape, F32)

    def gates(a):
        parts = []
        for t in range(2):
            frame = slab * 2 + t
            allowed = frame >= clip_start_of(lengths, frame + 2 - a)
            parts.append(jnp.full((64, 768), jnp.where(allowed, 1.0, 0.0), F32).astype(BF))
        return jnp.concatenate(parts, axis=0)

    first, second, both = slice(0, 64), slice(64, 128), slice(0, 128)
    plan = [(0, both, both), (1, second, first)] if ahead else [(1, first, second), (2, both, both)]

    def row_tap(b, carry):
        for a, meant, rows in plan:
            tap = (a * 3 + b) * 3
            kernel = jnp.concatenate([ref[tap + e] for e in range(3) for ref in weights], axis=0)
            lhs = taps[b][meant] * gates(a)[meant]
            out[rows] += jnp.dot(lhs, kernel, preferred_element_type=F32)
        return carry

    lax.fori_loop(0, 3, row_tap, 0)


def group_matrix(channels_first):
    shape = (COUT, 128) if channels_first else (128, COUT)
    c = lax.broadcasted_iota(jnp.int32, shape, 0 if channels_first else 1)
    g = lax.broadcasted_iota(jnp.int32, shape, 1 if channels_first else 0)
    return (lax.shift_right_logical(c, 4) == g).astype(F32)


def member_of(lengths, frame):
    end = jnp.int32(0)
    flags = []
    for k in range(4):
        start = end
        end = end + lengths[k]
        flags.append(jnp.where((frame >= start) & (frame < end), 1.0, 0.0).astype(F32))
    return flags


def stat_kernel(lengths, near, before, conv_out, stats):
    slab = my_slab()
    conv = near[...] + before[...]
    conv_out[...] = conv
    rows = []
    for f in range(2):
        part = conv[f * 64:(f + 1) * 64]
        rows.append(jnp.sum(part, axis=0, keepdims=True))
        rows.append(jnp.sum(part * part, axis=0, keepdims=True))
    rows = jnp.concatenate(rows + rows, axis=0)
    grouped = jnp.dot(rows, group_matrix(True), precision=HIGHEST, preferred_element_type=F32)
    m0 = member_of(lengths, slab * 2)
    m1 = member_of(lengths, slab * 2 + 1)
    sums = [grouped[0:1] * m0[k] + grouped[2:3] * m1[k] for k in range(4)]
    squares = [grouped[1:2] * m0[k] + grouped[3:4] * m1[k] for k in range(4)]
    tile = jnp.concatenate(sums + squares, axis=0)
    stats[...] = jnp.broadcast_to(tile[None], stats.shape)


def middle_kernel(got, out):
    out[...] = jnp.broadcast_to(jnp.sum(got[...], axis=0)[None], out.shape)


def final_kernel(lengths, got, conv, gain, bias, out):
    slab = my_slab()
    total = jnp.sum(got[...], axis=0)
    spread = group_matrix(False)
    for f in range(2):
        flags = member_of(lengths, slab * 2 + f)
        sums = jnp.zeros((1, 128), F32)
        squares = jnp.zeros((1, 128), F32)
        frames = jnp.float32(0)
        for k in range(4):
            sums = sums + total[k:k + 1] * flags[k]
            squares = squares + total[4 + k:5 + k] * flags[k]
            frames = frames + flags[k] * lengths[k].astype(F32)
        entries = jnp.full((1, 128), frames * float(OUT_ROWS * 64 * GROUP_SIZE), F32)
        mean = sums / entries
        var = squares / entries - mean * mean
        scale = lax.rsqrt(var + EPSILON)
        both = jnp.concatenate([mean, scale] * 4, axis=0)
        wide = jnp.dot(both, spread, precision=HIGHEST, preferred_element_type=F32)
        part = conv[f * 64:(f + 1) * 64]
        v = ((part - wide[0:1]) * wide[1:2]) * gain[...] + bias[...]
        out[f] = (v / (1.0 + jnp.exp(-v))).astype(BF)


def shuffle(x, axis):
    return lax.all_to_all(x, axis, split_axis=0, concat_axis=0, tiled=True)


def gathered_weights(kernel):
    ring = [(c * NY + y, c * NY + (y + (1 if c == 0 else NY - 1)) % NY)
            for c in range(2) for y in range(NY)]
    swap = [(0, 1), (1, 0)]
    moved = [kernel]
    for _ in range(3):
        moved.append(lax.ppermute(moved[-1], ("co", "y"), ring))
    first = lax.axis_index("co") * HALF
    half = lax.dynamic_slice_in_dim(moved[3], first, HALF, axis=1)
    second, half = lax.optimization_barrier((moved[2], half))
    moved.append(lax.ppermute(half, ("co", "y"), ring))
    swapped = [lax.ppermute(shard, "co", swap) for shard in (moved[1], second, moved[3], moved[4])]
    return moved, swapped


def convolve(ahead, lengths, frames, weights):
    return pl.pallas_call(
        functools.partial(conv_kernel, ahead),
        out_shape=jax.ShapeDtypeStruct((128, COUT), F32),
        in_specs=[SMEM] + [VMEM] * (2 + NY),
        out_specs=VMEM,
        scratch_shapes=[pltpu.VMEM((3, 128, 768), BF)],
        compiler_params=params(24),
    )(lengths, frames, *weights)


def body(arrived, row_target, clip_lengths, conv_weight, gn_gain, gn_bias):
    moved, swapped = gathered_weights(conv_weight.reshape(27, CH_DEV, COUT))
    send = pl.pallas_call(
        pack_kernel,
        out_shape=jax.ShapeDtypeStruct((SLABS, 136, 128), BF),
        in_specs=[SMEM, HBM],
        out_specs=VMEM,
        scratch_shapes=[
            pltpu.VMEM((ROWS, CH_DEV, 128), BF),
            pltpu.SMEM((SLABS,), jnp.int32),
            pltpu.VMEM((SLABS, 8, 128), F32),
            pltpu.SemaphoreType.DMA,
        ],
        compiler_params=params(60),
    )(row_target, arrived)
    got = shuffle(send, TM)
    got, moved[2] = lax.optimization_barrier((got, moved[2]))
    far, near = pl.pallas_call(
        place_kernel,
        out_shape=[jax.ShapeDtypeStruct((NY * 6, CH_DEV, 128), BF)] * 2,
        in_specs=[VMEM],
        out_specs=[HBM, HBM],
        scratch_shapes=[
            pltpu.VMEM((97, CH_DEV, 128), BF),
            pltpu.VMEM((8, 128), jnp.int32),
            pltpu.SMEM((8, 128), jnp.int32),
            pltpu.SemaphoreType.DMA((2,)),
        ],
        compiler_params=params(60),
    )(got)
    weights = [moved[0], moved[1], swapped[0], moved[2], swapped[1], moved[3], swapped[2]]
    weights += [moved[4], swapped[3]]
    onward = [(i, i + 1) for i in range(SLABS - 1)]
    far = shuffle(far.reshape(NY, 6, CH_DEV, 128), "y")
    near = shuffle(near.reshape(NY, 6, CH_DEV, 128), "y")
    far_before = lax.ppermute(convolve(True, clip_lengths, far, weights), TM, onward)
    far = convolve(False, clip_lengths, far, weights)
    near_before = lax.ppermute(convolve(True, clip_lengths, near, weights), TM, onward)
    near = convolve(False, clip_lengths, near, weights)
    far = lax.ppermute(far + far_before, "zh", [(0, 1), (1, 0)])
    near = near + far
    conv, stats = pl.pallas_call(
        stat_kernel,
        out_shape=[jax.ShapeDtypeStruct((128, COUT), F32), jax.ShapeDtypeStruct((16, 8, 128), F32)],
        in_specs=[SMEM, VMEM, VMEM],
        out_specs=[VMEM, VMEM],
        compiler_params=params(16),
    )(clip_lengths, near, near_before)
    stats = shuffle(stats, ("y", "co"))
    stats = pl.pallas_call(
        middle_kernel,
        out_shape=jax.ShapeDtypeStruct((SLABS, 8, 128), F32),
        in_specs=[VMEM],
        out_specs=VMEM,
    )(stats)
    stats = shuffle(stats, ("zl", "zh", "x"))
    out = pl.pallas_call(
        final_kernel,
        out_shape=jax.ShapeDtypeStruct((2, 64, COUT), BF),
        in_specs=[SMEM, VMEM, VMEM, VMEM, VMEM],
        out_specs=VMEM,
        compiler_params=params(16),
    )(clip_lengths, stats, conv, gn_gain.reshape(1, COUT), gn_bias.reshape(1, COUT))
    return out.reshape(1, 2, 64, COUT)


def solution(mesh):
    fine = Mesh(mesh.devices.reshape(4, 4, 2, 2, 8), TM + CH)
    in_specs = (P(TM, CH, None), P(TM), P(), P(None, None, None, CH, None), P(), P())
    out_specs = P(CH, TM, None, None)
    return jax.shard_map(body, mesh=fine, in_specs=in_specs, out_specs=out_specs, check_vma=False)
```

```python
import functools

import jax
import jax.numpy as jnp
from jax import lax
from jax.experimental import pallas as pl
from jax.experimental.pallas import tpu as pltpu
from jax.sharding import Mesh, PartitionSpec as P

TM = ("zl", "x", "co")
CH = ("zh", "y")
SLABS = 32
ROWS = 64
CAP = 4
CH_DEV = 32
HALF = 16
NY = 8
OUT_ROWS = 16
COUT = 512
GROUPS = 32
GROUP_SIZE = 16
EPSILON = 1e-05
BF = jnp.bfloat16
F32 = jnp.float32
HIGHEST = lax.Precision.HIGHEST

VMEM = pl.BlockSpec(memory_space=pltpu.VMEM)
SMEM = pl.BlockSpec(memory_space=pltpu.SMEM)
HBM = pl.BlockSpec(memory_space=pltpu.HBM)


def params(mib):
    return pltpu.CompilerParams(vmem_limit_bytes=mib * 1024 * 1024)


def pack_kernel(target, arrived, send, rows, counts, places, sem):
    fetch = pltpu.make_async_copy(arrived, rows, sem)
    fetch.start()
    places[...] = jnp.full(places.shape, float(ROWS), F32)

    def clear(i, carry):
        counts[i] = 0
        return carry

    lax.fori_loop(0, SLABS, clear, 0)
    fetch.wait()

    def some(n, carry):
        for k in range(4):
            i = n * 4 + k
            t = target[i]
            owner = lax.shift_right_logical(t, 6)
            rank = counts[owner]
            counts[owner] = rank + 1
            slot = pl.ds(pl.multiple_of(rank * CH_DEV, CH_DEV), CH_DEV)
            send[owner, slot, :] = rows[i]
            place = lax.bitwise_and(t, ROWS - 1).astype(F32)
            places[owner, pl.ds(rank, 1), :] = jnp.full((1, 128), place, F32)
        return carry

    lax.fori_loop(0, ROWS // 4, some, 0)
    send[:, CAP * CH_DEV:, :] = places[...].astype(BF)


def my_slab():
    return (lax.axis_index("zl") * 4 + lax.axis_index("x")) * 2 + lax.axis_index("co")


def spot(zh, i, f, b):
    near = 1 - lax.bitwise_xor(lax.shift_right_logical(i, 3), zh)
    return near * 48 + lax.bitwise_and(i, NY - 1) * 6 + f * 3 + b


def place_kernel(got, far, near, both, table, moves, sems):
    zh = lax.axis_index("zh")
    lane = lax.broadcasted_iota(jnp.int32, (8, 128), 1)
    place = jnp.full((8, 128), float(ROWS), F32)
    for s in range(SLABS):
        place = jnp.where(lane == s, got[s, CAP * CH_DEV:, :].astype(F32), place)
    place = place.astype(jnp.int32)
    f = lax.shift_right_logical(place, 5)
    h = lax.bitwise_and(place, 31)
    odd = lax.bitwise_and(h, 1)
    i = lax.shift_right_logical(h, 1)
    first = spot(zh, i, f, 1 + odd)
    second = jnp.where((odd == 1) & (i < OUT_ROWS - 1), spot(zh, i + 1, f, 0), first)
    table[...] = jnp.where(place < ROWS, first * 128 + second, 96 * 128 + 96)
    copy = pltpu.make_async_copy(table, moves, sems.at[0])
    copy.start()
    for f in range(2):
        both[spot(zh, jnp.int32(0), f, 0)] = jnp.zeros((CH_DEV, 128), BF)
    copy.wait()

    def some(s, carry):
        for source in (2 * s, 2 * s + 1):
            for r in range(CAP):
                move = moves[r, source]
                row = got[source, r * CH_DEV:(r + 1) * CH_DEV, :]
                both[lax.shift_right_logical(move, 7)] = row
                both[lax.bitwise_and(move, 127)] = row
        return carry

    lax.fori_loop(0, SLABS // 2, some, 0)
    copies = [
        pltpu.make_async_copy(both.at[pl.ds(48 * k, 48)], out, sems.at[k])
        for k, out in enumerate((far, near))
    ]
    for copy in copies:
        copy.start()
    for copy in copies:
        copy.wait()


def clip_start_of(lengths, frame):
    first = jnp.int32(0)
    end = jnp.int32(0)
    for k in range(4):
        start = end
        end = end + lengths[k]
        first = jnp.where((frame >= start) & (frame < end), start, first)
    return first


def conv_kernel(lengths, frames, *rest):
    weights, (own, after, taps) = rest[:NY + 1], rest[NY + 1:]
    y = lax.axis_index("y")
    core = lax.axis_index("co")
    slab = my_slab()
    sign = 2 * core - 1
    sources = [y]
    for s in range(1, 4):
        sources += [y + sign * s, y - sign * s]
    sources += [y + 4, y + 4]
    sources = [lax.bitwise_and(s + NY, NY - 1) for s in sources]
    whole = pl.ds(0, CH_DEV)
    mine = pl.ds(pl.multiple_of(core * HALF, HALF), HALF)
    other = pl.ds(pl.multiple_of((1 - core) * HALF, HALF), HALF)
    sources = list(zip(sources, [whole] * 7 + [mine, other]))
    j = lax.broadcasted_iota(jnp.int32, (192, 128), 0)
    w = lax.broadcasted_iota(jnp.int32, (192, 128), 1)
    wanted = jnp.where(j < 64, 2 * j - 1, jnp.where(j < 128, 2 * j - 128, 2 * j - 255))
    pick = (w == wanted).astype(F32).astype(BF)
    for t in range(2):
        for b in range(3):
            x = jnp.concatenate([frames[s, t * 3 + b, c] for s, c in sources], axis=0)
            picked = lax.dot_general(pick, x, (((1,), (1,)), ((), ())),
                                     preferred_element_type=F32).astype(BF)
            for e in range(3):
                taps[b, t * 64:(t + 1) * 64, e * 256:(e + 1) * 256] = picked[e * 64:(e + 1) * 64]
    own[...] = jnp.zeros(own.shape, F32)
    after[...] = jnp.zeros(after.shape, F32)

    def gates(a):
        parts = []
        for t in range(2):
            frame = slab * 2 + t
            allowed = frame >= clip_start_of(lengths, frame + 2 - a)
            parts.append(jnp.full((64, 768), jnp.where(allowed, 1.0, 0.0), F32).astype(BF))
        return jnp.concatenate(parts, axis=0)

    def row_tap(b, carry):
        lhs = taps[b]
        for a in range(3):
            tap = (a * 3 + b) * 3
            kernel = jnp.concatenate([ref[tap + e] for e in range(3) for ref in weights], axis=0)
            part = jnp.dot(lhs * gates(a), kernel, preferred_element_type=F32)
            if a == 0:
                after[...] += part
            elif a == 1:
                own[64:] += part[:64]
                after[:64] += part[64:]
            else:
                own[...] += part
        return carry

    lax.fori_loop(0, 3, row_tap, 0)


def group_matrix(channels_first):
    shape = (COUT, 128) if channels_first else (128, COUT)
    c = lax.broadcasted_iota(jnp.int32, shape, 0 if channels_first else 1)
    g = lax.broadcasted_iota(jnp.int32, shape, 1 if channels_first else 0)
    return (lax.shift_right_logical(c, 4) == g).astype(F32)


def member_of(lengths, frame):
    end = jnp.int32(0)
    flags = []
    for k in range(4):
        start = end
        end = end + lengths[k]
        flags.append(jnp.where((frame >= start) & (frame < end), 1.0, 0.0).astype(F32))
    return flags


def stat_kernel(lengths, near, far, token, before, conv_out, stats):
    slab = my_slab()
    conv = near[...] + before[...] + far[...]
    conv_out[...] = conv
    rows = []
    for f in range(2):
        part = conv[f * 64:(f + 1) * 64]
        rows.append(jnp.sum(part, axis=0, keepdims=True))
        rows.append(jnp.sum(part * part, axis=0, keepdims=True))
    rows = jnp.concatenate(rows + rows, axis=0)
    grouped = jnp.dot(rows, group_matrix(True), precision=HIGHEST, preferred_element_type=F32)
    m0 = member_of(lengths, slab * 2)
    m1 = member_of(lengths, slab * 2 + 1)
    sums = [grouped[0:1] * m0[k] + grouped[2:3] * m1[k] for k in range(4)]
    squares = [grouped[1:2] * m0[k] + grouped[3:4] * m1[k] for k in range(4)]
    tile = jnp.concatenate(sums + squares, axis=0)
    stats[...] = jnp.broadcast_to(tile[None], stats.shape)


def middle_kernel(got, out):
    out[...] = jnp.broadcast_to(jnp.sum(got[...], axis=0)[None], out.shape)


def final_kernel(lengths, got, conv, gain, bias, out):
    slab = my_slab()
    total = jnp.sum(got[...], axis=0)
    spread = group_matrix(False)
    for f in range(2):
        flags = member_of(lengths, slab * 2 + f)
        sums = jnp.zeros((1, 128), F32)
        squares = jnp.zeros((1, 128), F32)
        frames = jnp.float32(0)
        for k in range(4):
            sums = sums + total[k:k + 1] * flags[k]
            squares = squares + total[4 + k:5 + k] * flags[k]
            frames = frames + flags[k] * lengths[k].astype(F32)
        entries = jnp.full((1, 128), frames * float(OUT_ROWS * 64 * GROUP_SIZE), F32)
        mean = sums / entries
        var = squares / entries - mean * mean
        scale = lax.rsqrt(var + EPSILON)
        both = jnp.concatenate([mean, scale] * 4, axis=0)
        wide = jnp.dot(both, spread, precision=HIGHEST, preferred_element_type=F32)
        part = conv[f * 64:(f + 1) * 64]
        v = ((part - wide[0:1]) * wide[1:2]) * gain[...] + bias[...]
        out[f] = (v / (1.0 + jnp.exp(-v))).astype(BF)


def shuffle(x, axis):
    return lax.all_to_all(x, axis, split_axis=0, concat_axis=0, tiled=True)


def gathered_weights(kernel):
    ring = [(c * NY + y, c * NY + (y + (1 if c == 0 else NY - 1)) % NY)
            for c in range(2) for y in range(NY)]
    swap = [(0, 1), (1, 0)]
    moved = [kernel]
    for _ in range(3):
        moved.append(lax.ppermute(moved[-1], ("co", "y"), ring))
    first = lax.axis_index("co") * HALF
    half = lax.dynamic_slice_in_dim(moved[3], first, HALF, axis=1)
    second, half = lax.optimization_barrier((moved[2], half))
    moved.append(lax.ppermute(half, ("co", "y"), ring))
    swapped = [lax.ppermute(shard, "co", swap) for shard in (moved[1], second, moved[3], moved[4])]
    return moved, swapped


def convolve(lengths, frames, weights):
    return pl.pallas_call(
        conv_kernel,
        out_shape=[jax.ShapeDtypeStruct((128, COUT), F32)] * 2,
        in_specs=[SMEM] + [VMEM] * (2 + NY),
        out_specs=[VMEM, VMEM],
        scratch_shapes=[pltpu.VMEM((3, 128, 768), BF)],
        compiler_params=params(24),
    )(lengths, frames, *weights)


def body(arrived, row_target, clip_lengths, conv_weight, gn_gain, gn_bias):
    moved, swapped = gathered_weights(conv_weight.reshape(27, CH_DEV, COUT))
    send = pl.pallas_call(
        pack_kernel,
        out_shape=jax.ShapeDtypeStruct((SLABS, 136, 128), BF),
        in_specs=[SMEM, HBM],
        out_specs=VMEM,
        scratch_shapes=[
            pltpu.VMEM((ROWS, CH_DEV, 128), BF),
            pltpu.SMEM((SLABS,), jnp.int32),
            pltpu.VMEM((SLABS, 8, 128), F32),
            pltpu.SemaphoreType.DMA,
        ],
        compiler_params=params(60),
    )(row_target, arrived)
    got = shuffle(send, TM)
    got, moved[2] = lax.optimization_barrier((got, moved[2]))
    far, near = pl.pallas_call(
        place_kernel,
        out_shape=[jax.ShapeDtypeStruct((NY * 6, CH_DEV, 128), BF)] * 2,
        in_specs=[VMEM],
        out_specs=[HBM, HBM],
        scratch_shapes=[
            pltpu.VMEM((97, CH_DEV, 128), BF),
            pltpu.VMEM((8, 128), jnp.int32),
            pltpu.SMEM((8, 128), jnp.int32),
            pltpu.SemaphoreType.DMA((2,)),
        ],
        compiler_params=params(8),
    )(got)
    weights = [moved[0], moved[1], swapped[0], moved[2], swapped[1], moved[3], swapped[2]]
    weights += [moved[4], swapped[3]]
    onward = [(i, i + 1) for i in range(SLABS - 1)]
    far = shuffle(far.reshape(NY, 6, CH_DEV, 128), "y")
    near = shuffle(near.reshape(NY, 6, CH_DEV, 128), "y")
    far, far_after = convolve(clip_lengths, far, weights)
    far_before = lax.ppermute(far_after, TM, onward)
    near, far_sum = lax.optimization_barrier((near, far + far_before))
    near, near_after = convolve(clip_lengths, near, weights)
    near_before = lax.ppermute(near_after, TM, onward)
    far = lax.ppermute(far_sum, "zh", [(0, 1), (1, 0)])
    token = far[:8, :128]
    conv, stats = pl.pallas_call(
        stat_kernel,
        out_shape=[jax.ShapeDtypeStruct((128, COUT), F32), jax.ShapeDtypeStruct((16, 8, 128), F32)],
        in_specs=[SMEM, VMEM, VMEM, VMEM, VMEM],
        out_specs=[VMEM, VMEM],
        compiler_params=params(16),
    )(clip_lengths, near, far, token, near_before)
    stats = shuffle(stats, ("y", "co"))
    stats = pl.pallas_call(
        middle_kernel,
        out_shape=jax.ShapeDtypeStruct((SLABS, 8, 128), F32),
        in_specs=[VMEM],
        out_specs=VMEM,
    )(stats)
    stats = shuffle(stats, ("zl", "zh", "x"))
    out = pl.pallas_call(
        final_kernel,
        out_shape=jax.ShapeDtypeStruct((2, 64, COUT), BF),
        in_specs=[SMEM, VMEM, VMEM, VMEM, VMEM],
        out_specs=VMEM,
        compiler_params=params(16),
    )(clip_lengths, stats, conv, gn_gain.reshape(1, COUT), gn_bias.reshape(1, COUT))
    return out.reshape(1, 2, 64, COUT)


def solution(mesh):
    fine = Mesh(mesh.devices.reshape(4, 4, 2, 2, 8), TM + CH)
    in_specs = (P(TM, CH, None), P(TM), P(), P(None, None, None, CH, None), P(), P())
    out_specs = P(CH, TM, None, None)
    return jax.shard_map(body, mesh=fine, in_specs=in_specs, out_specs=out_specs, check_vma=False)
```

```python
import functools

import jax
import jax.numpy as jnp
from jax import lax
from jax.experimental import pallas as pl
from jax.experimental.pallas import tpu as pltpu
from jax.sharding import Mesh, PartitionSpec as P

TM = ("zl", "x", "co")
CH = ("zh", "y")
SLABS = 32
ROWS = 64
CAP = 4
CH_DEV = 32
HALF = 16
NY = 8
OUT_ROWS = 16
COUT = 512
GROUPS = 32
GROUP_SIZE = 16
EPSILON = 1e-05
BF = jnp.bfloat16
F32 = jnp.float32
HIGHEST = lax.Precision.HIGHEST

VMEM = pl.BlockSpec(memory_space=pltpu.VMEM)
SMEM = pl.BlockSpec(memory_space=pltpu.SMEM)
HBM = pl.BlockSpec(memory_space=pltpu.HBM)


def params(mib):
    return pltpu.CompilerParams(vmem_limit_bytes=mib * 1024 * 1024)


def pack_kernel(target, arrived, send, rows, counts, places, sem):
    fetch = pltpu.make_async_copy(arrived, rows, sem)
    fetch.start()
    places[...] = jnp.full(places.shape, float(ROWS), F32)

    def clear(i, carry):
        counts[i] = 0
        return carry

    lax.fori_loop(0, SLABS, clear, 0)
    fetch.wait()

    def some(n, carry):
        for k in range(4):
            i = n * 4 + k
            t = target[i]
            owner = lax.shift_right_logical(t, 6)
            rank = counts[owner]
            counts[owner] = rank + 1
            slot = pl.ds(pl.multiple_of(rank * CH_DEV, CH_DEV), CH_DEV)
            send[owner, slot, :] = rows[i]
            place = lax.bitwise_and(t, ROWS - 1).astype(F32)
            places[owner, pl.ds(rank, 1), :] = jnp.full((1, 128), place, F32)
        return carry

    lax.fori_loop(0, ROWS // 4, some, 0)
    send[:, CAP * CH_DEV:, :] = places[...].astype(BF)


def my_slab():
    return (lax.axis_index("zl") * 4 + lax.axis_index("x")) * 2 + lax.axis_index("co")


def spot(zh, i, f, b):
    near = 1 - lax.bitwise_xor(lax.shift_right_logical(i, 3), zh)
    return near * 48 + lax.bitwise_and(i, NY - 1) * 6 + f * 3 + b


def place_kernel(got, far, near, both, table, moves, sems):
    zh = lax.axis_index("zh")
    lane = lax.broadcasted_iota(jnp.int32, (8, 128), 1)
    place = jnp.full((8, 128), float(ROWS), F32)
    for s in range(SLABS):
        place = jnp.where(lane == s, got[s, CAP * CH_DEV:, :].astype(F32), place)
    place = place.astype(jnp.int32)
    f = lax.shift_right_logical(place, 5)
    h = lax.bitwise_and(place, 31)
    odd = lax.bitwise_and(h, 1)
    i = lax.shift_right_logical(h, 1)
    first = spot(zh, i, f, 1 + odd)
    second = jnp.where((odd == 1) & (i < OUT_ROWS - 1), spot(zh, i + 1, f, 0), first)
    table[...] = jnp.where(place < ROWS, first * 128 + second, 96 * 128 + 96)
    copy = pltpu.make_async_copy(table, moves, sems.at[0])
    copy.start()
    for f in range(2):
        both[spot(zh, jnp.int32(0), f, 0)] = jnp.zeros((CH_DEV, 128), BF)
    copy.wait()

    def some(s, carry):
        for source in (2 * s, 2 * s + 1):
            for r in range(CAP):
                move = moves[r, source]
                row = got[source, r * CH_DEV:(r + 1) * CH_DEV, :]
                both[lax.shift_right_logical(move, 7)] = row
                both[lax.bitwise_and(move, 127)] = row
        return carry

    lax.fori_loop(0, SLABS // 2, some, 0)
    copies = [
        pltpu.make_async_copy(both.at[pl.ds(48 * k, 48)], out, sems.at[k])
        for k, out in enumerate((far, near))
    ]
    for copy in copies:
        copy.start()
    for copy in copies:
        copy.wait()


def clip_start_of(lengths, frame):
    first = jnp.int32(0)
    end = jnp.int32(0)
    for k in range(4):
        start = end
        end = end + lengths[k]
        first = jnp.where((frame >= start) & (frame < end), start, first)
    return first


def conv_kernel(lengths, frames, *rest):
    weights, (own, after, taps) = rest[:NY + 1], rest[NY + 1:]
    y = lax.axis_index("y")
    core = lax.axis_index("co")
    slab = my_slab()
    sign = 2 * core - 1
    sources = [y]
    for s in range(1, 4):
        sources += [y + sign * s, y - sign * s]
    sources += [y + 4, y + 4]
    sources = [lax.bitwise_and(s + NY, NY - 1) for s in sources]
    whole = pl.ds(0, CH_DEV)
    mine = pl.ds(pl.multiple_of(core * HALF, HALF), HALF)
    other = pl.ds(pl.multiple_of((1 - core) * HALF, HALF), HALF)
    sources = list(zip(sources, [whole] * 7 + [mine, other]))
    j = lax.broadcasted_iota(jnp.int32, (192, 128), 0)
    w = lax.broadcasted_iota(jnp.int32, (192, 128), 1)
    wanted = jnp.where(j < 64, 2 * j - 1, jnp.where(j < 128, 2 * j - 128, 2 * j - 255))
    pick = (w == wanted).astype(F32).astype(BF)
    for t in range(2):
        for b in range(3):
            x = jnp.concatenate([frames[s, t * 3 + b, c] for s, c in sources], axis=0)
            picked = lax.dot_general(pick, x, (((1,), (1,)), ((), ())),
                                     preferred_element_type=F32).astype(BF)
            for e in range(3):
                taps[b, t * 64:(t + 1) * 64, e * 256:(e + 1) * 256] = picked[e * 64:(e + 1) * 64]
    own[...] = jnp.zeros(own.shape, F32)
    after[...] = jnp.zeros(after.shape, F32)

    def gates(a):
        parts = []
        for t in range(2):
            frame = slab * 2 + t
            allowed = frame >= clip_start_of(lengths, frame + 2 - a)
            parts.append(jnp.full((64, 768), jnp.where(allowed, 1.0, 0.0), F32).astype(BF))
        return jnp.concatenate(parts, axis=0)

    def row_tap(b, carry):
        lhs = taps[b]
        for a in range(3):
            tap = (a * 3 + b) * 3
            kernel = jnp.concatenate([ref[tap + e] for e in range(3) for ref in weights], axis=0)
            part = jnp.dot(lhs * gates(a), kernel, preferred_element_type=F32)
            if a == 0:
                after[...] += part
            elif a == 1:
                own[64:] += part[:64]
                after[:64] += part[64:]
            else:
                own[...] += part
        return carry

    lax.fori_loop(0, 3, row_tap, 0)


def group_matrix(channels_first):
    shape = (COUT, 128) if channels_first else (128, COUT)
    c = lax.broadcasted_iota(jnp.int32, shape, 0 if channels_first else 1)
    g = lax.broadcasted_iota(jnp.int32, shape, 1 if channels_first else 0)
    return (lax.shift_right_logical(c, 4) == g).astype(F32)


def member_of(lengths, frame):
    end = jnp.int32(0)
    flags = []
    for k in range(4):
        start = end
        end = end + lengths[k]
        flags.append(jnp.where((frame >= start) & (frame < end), 1.0, 0.0).astype(F32))
    return flags


def stat_kernel(lengths, near, before, conv_out, stats):
    slab = my_slab()
    conv = near[...] + before[...]
    conv_out[...] = conv
    rows = []
    for f in range(2):
        part = conv[f * 64:(f + 1) * 64]
        rows.append(jnp.sum(part, axis=0, keepdims=True))
        rows.append(jnp.sum(part * part, axis=0, keepdims=True))
    rows = jnp.concatenate(rows + rows, axis=0)
    grouped = jnp.dot(rows, group_matrix(True), precision=HIGHEST, preferred_element_type=F32)
    m0 = member_of(lengths, slab * 2)
    m1 = member_of(lengths, slab * 2 + 1)
    sums = [grouped[0:1] * m0[k] + grouped[2:3] * m1[k] for k in range(4)]
    squares = [grouped[1:2] * m0[k] + grouped[3:4] * m1[k] for k in range(4)]
    tile = jnp.concatenate(sums + squares, axis=0)
    stats[...] = jnp.broadcast_to(tile[None], stats.shape)


def middle_kernel(got, out):
    out[...] = jnp.broadcast_to(jnp.sum(got[...], axis=0)[None], out.shape)


def final_kernel(lengths, got, conv, gain, bias, out):
    slab = my_slab()
    total = jnp.sum(got[...], axis=0)
    spread = group_matrix(False)
    for f in range(2):
        flags = member_of(lengths, slab * 2 + f)
        sums = jnp.zeros((1, 128), F32)
        squares = jnp.zeros((1, 128), F32)
        frames = jnp.float32(0)
        for k in range(4):
            sums = sums + total[k:k + 1] * flags[k]
            squares = squares + total[4 + k:5 + k] * flags[k]
            frames = frames + flags[k] * lengths[k].astype(F32)
        entries = jnp.full((1, 128), frames * float(OUT_ROWS * 64 * GROUP_SIZE), F32)
        mean = sums / entries
        var = squares / entries - mean * mean
        scale = lax.rsqrt(var + EPSILON)
        both = jnp.concatenate([mean, scale] * 4, axis=0)
        wide = jnp.dot(both, spread, precision=HIGHEST, preferred_element_type=F32)
        part = conv[f * 64:(f + 1) * 64]
        v = ((part - wide[0:1]) * wide[1:2]) * gain[...] + bias[...]
        out[f] = (v / (1.0 + jnp.exp(-v))).astype(BF)


def shuffle(x, axis):
    return lax.all_to_all(x, axis, split_axis=0, concat_axis=0, tiled=True)


def gathered_weights(kernel):
    ring = [(c * NY + y, c * NY + (y + (1 if c == 0 else NY - 1)) % NY)
            for c in range(2) for y in range(NY)]
    swap = [(0, 1), (1, 0)]
    moved = [kernel]
    for _ in range(3):
        moved.append(lax.ppermute(moved[-1], ("co", "y"), ring))
    first = lax.axis_index("co") * HALF
    half = lax.dynamic_slice_in_dim(moved[3], first, HALF, axis=1)
    second, half = lax.optimization_barrier((moved[2], half))
    moved.append(lax.ppermute(half, ("co", "y"), ring))
    swapped = [lax.ppermute(shard, "co", swap) for shard in (moved[1], second, moved[3], moved[4])]
    return moved, swapped


def convolve(lengths, frames, weights):
    return pl.pallas_call(
        conv_kernel,
        out_shape=[jax.ShapeDtypeStruct((128, COUT), F32)] * 2,
        in_specs=[SMEM] + [VMEM] * (2 + NY),
        out_specs=[VMEM, VMEM],
        scratch_shapes=[pltpu.VMEM((3, 128, 768), BF)],
        compiler_params=params(24),
    )(lengths, frames, *weights)


def body(arrived, row_target, clip_lengths, conv_weight, gn_gain, gn_bias):
    moved, swapped = gathered_weights(conv_weight.reshape(27, CH_DEV, COUT))
    send = pl.pallas_call(
        pack_kernel,
        out_shape=jax.ShapeDtypeStruct((SLABS, 136, 128), BF),
        in_specs=[SMEM, HBM],
        out_specs=VMEM,
        scratch_shapes=[
            pltpu.VMEM((ROWS, CH_DEV, 128), BF),
            pltpu.SMEM((SLABS,), jnp.int32),
            pltpu.VMEM((SLABS, 8, 128), F32),
            pltpu.SemaphoreType.DMA,
        ],
        compiler_params=params(60),
    )(row_target, arrived)
    got = shuffle(send, TM)
    got, moved[2] = lax.optimization_barrier((got, moved[2]))
    far, near = pl.pallas_call(
        place_kernel,
        out_shape=[jax.ShapeDtypeStruct((NY * 6, CH_DEV, 128), BF)] * 2,
        in_specs=[VMEM],
        out_specs=[HBM, HBM],
        scratch_shapes=[
            pltpu.VMEM((97, CH_DEV, 128), BF),
            pltpu.VMEM((8, 128), jnp.int32),
            pltpu.SMEM((8, 128), jnp.int32),
            pltpu.SemaphoreType.DMA((2,)),
        ],
        compiler_params=params(8),
    )(got)
    weights = [moved[0], moved[1], swapped[0], moved[2], swapped[1], moved[3], swapped[2]]
    weights += [moved[4], swapped[3]]
    onward = [(i, i + 1) for i in range(SLABS - 1)]
    far = shuffle(far.reshape(NY, 6, CH_DEV, 128), "y")
    near = shuffle(near.reshape(NY, 6, CH_DEV, 128), "y")
    far, far_after = convolve(clip_lengths, far, weights)
    far_before = lax.ppermute(far_after, TM, onward)
    near, near_after = convolve(clip_lengths, near, weights)
    near_before = lax.ppermute(near_after, TM, onward)
    far = lax.ppermute(far + far_before, "zh", [(0, 1), (1, 0)])
    near = near + far
    conv, stats = pl.pallas_call(
        stat_kernel,
        out_shape=[jax.ShapeDtypeStruct((128, COUT), F32), jax.ShapeDtypeStruct((32, 8, 128), F32)],
        in_specs=[SMEM, VMEM, VMEM],
        out_specs=[VMEM, VMEM],
        compiler_params=params(16),
    )(clip_lengths, near, near_before)
    stats = shuffle(stats, ("zl", "zh", "x"))
    stats = pl.pallas_call(
        middle_kernel,
        out_shape=jax.ShapeDtypeStruct((16, 8, 128), F32),
        in_specs=[VMEM],
        out_specs=VMEM,
    )(stats)
    stats = shuffle(stats, ("y", "co"))
    out = pl.pallas_call(
        final_kernel,
        out_shape=jax.ShapeDtypeStruct((2, 64, COUT), BF),
        in_specs=[SMEM, VMEM, VMEM, VMEM, VMEM],
        out_specs=VMEM,
        compiler_params=params(16),
    )(clip_lengths, stats, conv, gn_gain.reshape(1, COUT), gn_bias.reshape(1, COUT))
    return out.reshape(1, 2, 64, COUT)


def solution(mesh):
    fine = Mesh(mesh.devices.reshape(4, 4, 2, 2, 8), TM + CH)
    in_specs = (P(TM, CH, None), P(TM), P(), P(None, None, None, CH, None), P(), P())
    out_specs = P(CH, TM, None, None)
    return jax.shard_map(body, mesh=fine, in_specs=in_specs, out_specs=out_specs, check_vma=False)
```

```python
import functools

import jax
import jax.numpy as jnp
from jax import lax
from jax.experimental import pallas as pl
from jax.experimental.pallas import tpu as pltpu
from jax.sharding import Mesh, PartitionSpec as P

TM = ("zl", "x", "co")
CH = ("zh", "y")
SLABS = 32
ROWS = 64
CAP = 4
CH_DEV = 32
HALF = 16
NY = 8
OUT_ROWS = 16
COUT = 512
GROUPS = 32
GROUP_SIZE = 16
EPSILON = 1e-05
BF = jnp.bfloat16
F32 = jnp.float32
HIGHEST = lax.Precision.HIGHEST

VMEM = pl.BlockSpec(memory_space=pltpu.VMEM)
SMEM = pl.BlockSpec(memory_space=pltpu.SMEM)
HBM = pl.BlockSpec(memory_space=pltpu.HBM)


def params(mib):
    return pltpu.CompilerParams(vmem_limit_bytes=mib * 1024 * 1024)


def pack_kernel(target, arrived, send, rows, counts, places, sem):
    fetch = pltpu.make_async_copy(arrived, rows, sem)
    fetch.start()
    places[...] = jnp.full(places.shape, float(ROWS), F32)

    def clear(i, carry):
        counts[i] = 0
        return carry

    lax.fori_loop(0, SLABS, clear, 0)
    fetch.wait()

    def some(n, carry):
        for k in range(4):
            i = n * 4 + k
            t = target[i]
            owner = lax.shift_right_logical(t, 6)
            rank = counts[owner]
            counts[owner] = rank + 1
            slot = pl.ds(pl.multiple_of(rank * CH_DEV, CH_DEV), CH_DEV)
            send[owner, slot, :] = rows[i]
            place = lax.bitwise_and(t, ROWS - 1).astype(F32)
            places[owner, pl.ds(rank, 1), :] = jnp.full((1, 128), place, F32)
        return carry

    lax.fori_loop(0, ROWS // 4, some, 0)
    send[:, CAP * CH_DEV:, :] = places[...].astype(BF)


def my_slab():
    return (lax.axis_index("zl") * 4 + lax.axis_index("x")) * 2 + lax.axis_index("co")


def spot(zh, i, f, b):
    near = 1 - lax.bitwise_xor(lax.shift_right_logical(i, 3), zh)
    return near * 48 + lax.bitwise_and(i, NY - 1) * 6 + f * 3 + b


def place_kernel(got, far, near, both, table, moves, sems):
    zh = lax.axis_index("zh")
    lane = lax.broadcasted_iota(jnp.int32, (8, 128), 1)
    place = jnp.full((8, 128), float(ROWS), F32)
    for s in range(SLABS):
        place = jnp.where(lane == s, got[s, CAP * CH_DEV:, :].astype(F32), place)
    place = place.astype(jnp.int32)
    f = lax.shift_right_logical(place, 5)
    h = lax.bitwise_and(place, 31)
    odd = lax.bitwise_and(h, 1)
    i = lax.shift_right_logical(h, 1)
    first = spot(zh, i, f, 1 + odd)
    second = jnp.where((odd == 1) & (i < OUT_ROWS - 1), spot(zh, i + 1, f, 0), first)
    table[...] = jnp.where(place < ROWS, first * 128 + second, 96 * 128 + 96)
    copy = pltpu.make_async_copy(table, moves, sems.at[0])
    copy.start()
    for f in range(2):
        both[spot(zh, jnp.int32(0), f, 0)] = jnp.zeros((CH_DEV, 128), BF)
    copy.wait()

    def some(s, carry):
        for source in (2 * s, 2 * s + 1):
            for r in range(CAP):
                move = moves[r, source]
                row = got[source, r * CH_DEV:(r + 1) * CH_DEV, :]
                both[lax.shift_right_logical(move, 7)] = row
                both[lax.bitwise_and(move, 127)] = row
        return carry

    lax.fori_loop(0, SLABS // 2, some, 0)
    copies = [
        pltpu.make_async_copy(both.at[pl.ds(48 * k, 48)], out, sems.at[k])
        for k, out in enumerate((far, near))
    ]
    for copy in copies:
        copy.start()
    for copy in copies:
        copy.wait()


def clip_start_of(lengths, frame):
    first = jnp.int32(0)
    end = jnp.int32(0)
    for k in range(4):
        start = end
        end = end + lengths[k]
        first = jnp.where((frame >= start) & (frame < end), start, first)
    return first


def conv_kernel(lengths, frames, *rest):
    weights, (own, after, taps) = rest[:NY + 1], rest[NY + 1:]
    y = lax.axis_index("y")
    core = lax.axis_index("co")
    slab = my_slab()
    sign = 2 * core - 1
    sources = [y]
    for s in range(1, 4):
        sources += [y + sign * s, y - sign * s]
    sources += [y + 4, y + 4]
    sources = [lax.bitwise_and(s + NY, NY - 1) for s in sources]
    whole = pl.ds(0, CH_DEV)
    mine = pl.ds(pl.multiple_of(core * HALF, HALF), HALF)
    other = pl.ds(pl.multiple_of((1 - core) * HALF, HALF), HALF)
    sources = list(zip(sources, [whole] * 7 + [mine, other]))
    j = lax.broadcasted_iota(jnp.int32, (192, 128), 0)
    w = lax.broadcasted_iota(jnp.int32, (192, 128), 1)
    wanted = jnp.where(j < 64, 2 * j - 1, jnp.where(j < 128, 2 * j - 128, 2 * j - 255))
    pick = (w == wanted).astype(F32).astype(BF)
    for t in range(2):
        for b in range(3):
            x = jnp.concatenate([frames[s, t * 3 + b, c] for s, c in sources], axis=0)
            picked = lax.dot_general(pick, x, (((1,), (1,)), ((), ())),
                                     preferred_element_type=F32).astype(BF)
            for e in range(3):
                taps[b, t * 64:(t + 1) * 64, e * 256:(e + 1) * 256] = picked[e * 64:(e + 1) * 64]
    own[...] = jnp.zeros(own.shape, F32)
    after[...] = jnp.zeros(after.shape, F32)

    def gates(a):
        parts = []
        for t in range(2):
            frame = slab * 2 + t
            allowed = frame >= clip_start_of(lengths, frame + 2 - a)
            parts.append(jnp.full((64, 768), jnp.where(allowed, 1.0, 0.0), F32).astype(BF))
        return jnp.concatenate(parts, axis=0)

    def row_tap(b, carry):
        lhs = taps[b]
        for a in range(3):
            tap = (a * 3 + b) * 3
            kernel = jnp.concatenate([ref[tap + e] for e in range(3) for ref in weights], axis=0)
            part = jnp.dot(lhs * gates(a), kernel, preferred_element_type=F32)
            if a == 0:
                after[...] += part
            elif a == 1:
                own[64:] += part[:64]
                after[:64] += part[64:]
            else:
                own[...] += part
        return carry

    lax.fori_loop(0, 3, row_tap, 0)


def group_matrix(channels_first):
    shape = (COUT, 128) if channels_first else (128, COUT)
    c = lax.broadcasted_iota(jnp.int32, shape, 0 if channels_first else 1)
    g = lax.broadcasted_iota(jnp.int32, shape, 1 if channels_first else 0)
    return (lax.shift_right_logical(c, 4) == g).astype(F32)


def member_of(lengths, frame):
    end = jnp.int32(0)
    flags = []
    for k in range(4):
        start = end
        end = end + lengths[k]
        flags.append(jnp.where((frame >= start) & (frame < end), 1.0, 0.0).astype(F32))
    return flags


def stat_kernel(lengths, near, before, conv_out, stats):
    slab = my_slab()
    conv = near[...] + before[...]
    conv_out[...] = conv
    rows = []
    for f in range(2):
        part = conv[f * 64:(f + 1) * 64]
        rows.append(jnp.sum(part, axis=0, keepdims=True))
        rows.append(jnp.sum(part * part, axis=0, keepdims=True))
    rows = jnp.concatenate(rows + rows, axis=0)
    grouped = jnp.dot(rows, group_matrix(True), precision=HIGHEST, preferred_element_type=F32)
    m0 = member_of(lengths, slab * 2)
    m1 = member_of(lengths, slab * 2 + 1)
    sums = [grouped[0:1] * m0[k] + grouped[2:3] * m1[k] for k in range(4)]
    squares = [grouped[1:2] * m0[k] + grouped[3:4] * m1[k] for k in range(4)]
    tile = jnp.concatenate(sums + squares, axis=0)
    stats[...] = jnp.broadcast_to(tile[None], stats.shape)


def middle_kernel(got, out):
    out[...] = jnp.broadcast_to(jnp.sum(got[...], axis=0)[None], out.shape)


def final_kernel(lengths, got, conv, gain, bias, out):
    slab = my_slab()
    total = jnp.sum(got[...], axis=0)
    spread = group_matrix(False)
    for f in range(2):
        flags = member_of(lengths, slab * 2 + f)
        sums = jnp.zeros((1, 128), F32)
        squares = jnp.zeros((1, 128), F32)
        frames = jnp.float32(0)
        for k in range(4):
            sums = sums + total[k:k + 1] * flags[k]
            squares = squares + total[4 + k:5 + k] * flags[k]
            frames = frames + flags[k] * lengths[k].astype(F32)
        entries = jnp.full((1, 128), frames * float(OUT_ROWS * 64 * GROUP_SIZE), F32)
        mean = sums / entries
        var = squares / entries - mean * mean
        scale = lax.rsqrt(var + EPSILON)
        both = jnp.concatenate([mean, scale] * 4, axis=0)
        wide = jnp.dot(both, spread, precision=HIGHEST, preferred_element_type=F32)
        part = conv[f * 64:(f + 1) * 64]
        v = ((part - wide[0:1]) * wide[1:2]) * gain[...] + bias[...]
        out[f] = (v / (1.0 + jnp.exp(-v))).astype(BF)


def shuffle(x, axis):
    return lax.all_to_all(x, axis, split_axis=0, concat_axis=0, tiled=True)


def gathered_weights(kernel):
    ring = [(c * NY + y, c * NY + (y + (1 if c == 0 else NY - 1)) % NY)
            for c in range(2) for y in range(NY)]
    swap = [(0, 1), (1, 0)]
    moved = [kernel]
    for _ in range(3):
        moved.append(lax.ppermute(moved[-1], ("co", "y"), ring))
    first = lax.axis_index("co") * HALF
    half = lax.dynamic_slice_in_dim(moved[3], first, HALF, axis=1)
    second, half = lax.optimization_barrier((moved[2], half))
    moved.append(lax.ppermute(half, ("co", "y"), ring))
    swapped = [lax.ppermute(shard, "co", swap) for shard in (moved[1], second, moved[3], moved[4])]
    return moved, swapped


def convolve(lengths, frames, weights):
    return pl.pallas_call(
        conv_kernel,
        out_shape=[jax.ShapeDtypeStruct((128, COUT), F32)] * 2,
        in_specs=[SMEM] + [VMEM] * (2 + NY),
        out_specs=[VMEM, VMEM],
        scratch_shapes=[pltpu.VMEM((3, 128, 768), BF)],
        compiler_params=params(24),
    )(lengths, frames, *weights)


def body(arrived, row_target, clip_lengths, conv_weight, gn_gain, gn_bias):
    moved, swapped = gathered_weights(conv_weight.reshape(27, CH_DEV, COUT))
    send = pl.pallas_call(
        pack_kernel,
        out_shape=jax.ShapeDtypeStruct((SLABS, 136, 128), BF),
        in_specs=[SMEM, HBM],
        out_specs=VMEM,
        scratch_shapes=[
            pltpu.VMEM((ROWS, CH_DEV, 128), BF),
            pltpu.SMEM((SLABS,), jnp.int32),
            pltpu.VMEM((SLABS, 8, 128), F32),
            pltpu.SemaphoreType.DMA,
        ],
        compiler_params=params(60),
    )(row_target, arrived)
    got = shuffle(send, TM)
    got, moved[2] = lax.optimization_barrier((got, moved[2]))
    far, near = pl.pallas_call(
        place_kernel,
        out_shape=[jax.ShapeDtypeStruct((NY * 6, CH_DEV, 128), BF)] * 2,
        in_specs=[VMEM],
        out_specs=[HBM, HBM],
        scratch_shapes=[
            pltpu.VMEM((97, CH_DEV, 128), BF),
            pltpu.VMEM((8, 128), jnp.int32),
            pltpu.SMEM((8, 128), jnp.int32),
            pltpu.SemaphoreType.DMA((2,)),
        ],
        compiler_params=params(8),
    )(got)
    weights = [moved[0], moved[1], swapped[0], moved[2], swapped[1], moved[3], swapped[2]]
    weights += [moved[4], swapped[3]]
    onward = [(i, i + 1) for i in range(SLABS - 1)]
    far = shuffle(far.reshape(NY, 6, CH_DEV, 128), "y")
    far, far_after = convolve(clip_lengths, far, weights)
    near, far_after = lax.optimization_barrier((near, far_after))
    near = shuffle(near.reshape(NY, 6, CH_DEV, 128), "y")
    far_before = lax.ppermute(far_after, TM, onward)
    near, near_after = convolve(clip_lengths, near, weights)
    near_before = lax.ppermute(near_after, TM, onward)
    far = lax.ppermute(far + far_before, "zh", [(0, 1), (1, 0)])
    near = near + far
    conv, stats = pl.pallas_call(
        stat_kernel,
        out_shape=[jax.ShapeDtypeStruct((128, COUT), F32), jax.ShapeDtypeStruct((16, 8, 128), F32)],
        in_specs=[SMEM, VMEM, VMEM],
        out_specs=[VMEM, VMEM],
        compiler_params=params(16),
    )(clip_lengths, near, near_before)
    stats = shuffle(stats, ("y", "co"))
    stats = pl.pallas_call(
        middle_kernel,
        out_shape=jax.ShapeDtypeStruct((SLABS, 8, 128), F32),
        in_specs=[VMEM],
        out_specs=VMEM,
    )(stats)
    stats = shuffle(stats, ("zl", "zh", "x"))
    out = pl.pallas_call(
        final_kernel,
        out_shape=jax.ShapeDtypeStruct((2, 64, COUT), BF),
        in_specs=[SMEM, VMEM, VMEM, VMEM, VMEM],
        out_specs=VMEM,
        compiler_params=params(16),
    )(clip_lengths, stats, conv, gn_gain.reshape(1, COUT), gn_bias.reshape(1, COUT))
    return out.reshape(1, 2, 64, COUT)


def solution(mesh):
    fine = Mesh(mesh.devices.reshape(4, 4, 2, 2, 8), TM + CH)
    in_specs = (P(TM, CH, None), P(TM), P(), P(None, None, None, CH, None), P(), P())
    out_specs = P(CH, TM, None, None)
    return jax.shard_map(body, mesh=fine, in_specs=in_specs, out_specs=out_specs, check_vma=False)
```
